128 devices in a mesh: tm: 32 (over y, x, core), gz: 4 (over z).
Axes of the slice: x: 4, y: 4, z: 4, core: 2. Of those that a mesh axis runs over, the one named last changes fastest.
Arguments:
- state_rhs: float32 [128, 128, 2048], P('tm', 'gz'), may hold values from -6 to 6
- adjoint_rhs: float32 [128, 128, 2048], P('tm', 'gz'), may hold values from -6 to 6
- diffusivity: float32 [128, 2048], P('gz'), may hold values from 0.02 to 2
- velocity: float32 [3, 128, 2048], P(None, 'gz'), may hold values from -4 to 4
Outputs:
- state_out: float32 [128, 128, 2048], P('tm', 'gz')
- adjoint_out: float32 [128, 128, 2048], P('tm', 'gz')
The draws below stay inside these ranges and needn't reach their ends.
All inputs are finite; a program needn't handle non-finite values.
Results may differ from the reference program's by a relative error of at most 0.0003.
Values sent between devices are 32-bit elements; how exact they have to be, the bound alone decides.
A program may use at most 128 MiB of HBM per device.

```python
import math
import jax
import jax.numpy as jnp
from jax import lax

NY = 64
NXY = 2048
NZ = 128
NT = 128


def block_levels(key, extent, shards, least, high):
    level, own = 1.0, jax.random.fold_in(key, 6)
    for position, blocks in shards:
        heights = jnp.exp(jax.random.uniform(jax.random.fold_in(own, position), (blocks,), jnp.float32, least / len(shards), high / len(shards)))
        level = level * jnp.repeat(heights, extent[position] // blocks).reshape([-1 if axis == position else 1 for axis in range(len(extent))])
    return level


def noise(key, extent, scale, bound, cuts=(), kind=jnp.bfloat16):
    level = block_levels(key, extent, cuts, -0.22, 0.18) if cuts else 1.0
    drawn = jax.random.normal(key, extent, jnp.float32) * scale * level
    return jnp.minimum(jnp.maximum(drawn, -bound), bound).astype(kind)


def setup_inputs(seed: int = 0) -> dict:
    key_of = jax.random.split(jax.random.key(seed), 5)
    return {
        "state_rhs": noise(key_of[0], (NT, NZ, NXY), 1.0, 6.0, ((0, 32), (1, 4)), jnp.float32),
        "adjoint_rhs": noise(key_of[1], (NT, NZ, NXY), 1.0, 6.0, ((0, 32), (1, 4)), jnp.float32),
        "diffusivity": jnp.clip(jnp.exp(math.log(2.0) - 4.6051702 * jax.random.uniform(key_of[2], (NZ, NXY), jnp.float32) ** block_levels(key_of[2], (NZ, NXY), ((0, 4),), -0.2, 0.2)), 0.02, 2.0),
        "velocity": noise(key_of[3], (3, NZ, NXY), 0.8, 4.0, ((1, 4),), jnp.float32),
    }


alpha_wrap = 0.1
beta_couple = 0.5
gamma_couple = 0.5


def ahead_flat(field, stride):
    pad_shape = field.shape[:-1] + (stride,)
    return jnp.concatenate([field[..., stride:], jnp.zeros(pad_shape, field.dtype)], axis=-1)


def behind_flat(field, stride):
    pad_shape = field.shape[:-1] + (stride,)
    return jnp.concatenate([jnp.zeros(pad_shape, field.dtype), field[..., :-stride]], axis=-1)


def neighbour_pairs(field, field_pad, width_y):
    column = jnp.arange(field.shape[-1], dtype=jnp.int32) % width_y
    nothing = jnp.zeros((), field.dtype)
    y_ahead = jnp.where(column == width_y - 1, nothing, ahead_flat(field, 1))
    y_behind = jnp.where(column == 0, nothing, behind_flat(field, 1))
    return [(field_pad[..., 2:, :], field_pad[..., :-2, :]),
            (ahead_flat(field, width_y), behind_flat(field, width_y)),
            (y_ahead, y_behind)]


def face_weights(kappa, kappa_pad, width_y):
    pairs = neighbour_pairs(kappa, kappa_pad, width_y)
    weights = []
    diagonal = jnp.zeros_like(kappa)
    for ahead, behind in pairs:
        face_ahead = jnp.where(ahead > 0.0, 0.5 * (kappa + ahead), kappa)
        face_behind = jnp.where(behind > 0.0, 0.5 * (kappa + behind), kappa)
        weights.append((face_ahead, face_behind))
        diagonal = diagonal + face_ahead + face_behind
    return weights, diagonal


def coupling(field, field_pad, weights, velocity, width_y):
    sign = jnp.array([1.0, -1.0, 1.0, -1.0], field.dtype).reshape((4,) + (1,) * (field.ndim - 1))
    pairs = neighbour_pairs(field, field_pad, width_y)
    speeds = [velocity[2], velocity[0], velocity[1]]
    total = jnp.zeros_like(field)
    for index in range(3):
        ahead, behind = pairs[index]
        face_ahead, face_behind = weights[index]
        total = total + face_ahead * ahead + face_behind * behind - sign * (0.5 * speeds[index]) * (ahead - behind)
    return total


def apply_inverse(stacked, lam_real, lam_imag, diagonal):
    shifted = lam_real + diagonal
    determinant = shifted * shifted + lam_imag * lam_imag + beta_couple * gamma_couple
    state_real, adjoint_real, state_imag, adjoint_imag = stacked[0], stacked[1], stacked[2], stacked[3]
    out_state_real = (shifted * state_real + lam_imag * state_imag + beta_couple * adjoint_real) / determinant
    out_state_imag = (shifted * state_imag - lam_imag * state_real + beta_couple * adjoint_imag) / determinant
    out_adjoint_real = (shifted * adjoint_real - lam_imag * adjoint_imag - gamma_couple * state_real) / determinant
    out_adjoint_imag = (shifted * adjoint_imag + lam_imag * adjoint_real - gamma_couple * state_imag) / determinant
    return jnp.stack([out_state_real, out_adjoint_real, out_state_imag, out_adjoint_imag])


def reference(state_rhs, adjoint_rhs, diffusivity, velocity):
    moments = jnp.arange(NT, dtype=jnp.float32)
    damping = jnp.power(jnp.asarray(alpha_wrap, jnp.float32), moments / NT)
    fields = jnp.stack([state_rhs, adjoint_rhs]) * damping[None, :, None, None]
    spectrum = jnp.fft.fft(fields, axis=1)
    spec_real = jnp.moveaxis(jnp.real(spectrum), 1, 0)
    spec_imag = jnp.moveaxis(jnp.imag(spectrum), 1, 0)
    angle = moments * (2.0 * math.pi / NT)
    ratio = alpha_wrap ** (1.0 / NT)
    lam_real = 1.0 - ratio * jnp.cos(angle)
    lam_imag = ratio * jnp.sin(angle)
    kappa_pad = jnp.pad(diffusivity, ((1, 1), (0, 0)))
    weights, diagonal = face_weights(diffusivity, kappa_pad, NY)

    def solve_one(item):
        part_real, part_imag, one_real, one_imag = item
        stacked = jnp.concatenate([part_real, part_imag])
        first = apply_inverse(stacked, one_real, one_imag, diagonal)
        first_pad = jnp.pad(first, ((0, 0), (1, 1), (0, 0)))
        return apply_inverse(stacked + coupling(first, first_pad, weights, velocity, NY), one_real, one_imag, diagonal)

    solved = lax.map(solve_one, (spec_real, spec_imag, lam_real, lam_imag))
    combined = solved[:, :2] + 1j * solved[:, 2:]
    back = jnp.real(jnp.fft.ifft(combined, axis=0))
    undo = jnp.power(jnp.asarray(alpha_wrap, jnp.float32), -moments / NT)
    result = back * undo[:, None, None, None]
    return result[:, 0], result[:, 1]
```

```python
import functools
import math

import jax
import jax.numpy as jnp
from jax import lax
from jax.experimental import pallas as pl
from jax.experimental.pallas import tpu as pltpu
from jax.sharding import PartitionSpec as P

NY = 64
COL = 128
ALPHA = 0.1
HALF = 0.5


def turn(value, shift, axis):
    return pltpu.roll(value, (-shift) % value.shape[axis], axis)


def kernel(
    chips, slabs, cells, times,
    state_hbm, adjoint_hbm, kappa_hbm, speed_hbm,
    state_out, adjoint_out,
    rhs, first, result, kappa, speed, couple, solve, power,
    carry_out, carry_in, entry_out, entry_in, edge_out, edge_in,
    load_sem, rhs_send, rhs_recv, kappa_send, kappa_recv,
    carry_send, carry_recv, entry_send, entry_recv,
    edge_send, edge_recv, store_sem, give_send, give_recv,
):
    half_times = times // 2
    lanes = chips // 2
    width = cells // lanes
    columns = width // COL
    total = chips * times
    ratio = ALPHA ** (1.0 / total)

    me = lax.axis_index("tm")
    slab = lax.axis_index("gz")
    chip = me // 2
    core = me % 2
    pair = {"tm": chip * 2 + 1 - core, "gz": slab}
    beside = {"tm": chip * 2 + 1 - core, "gz": (slab + slabs + 2 * core - 1) % slabs}

    def peer(other):
        return {"tm": other * 2 + core, "gz": slab}

    rows = pl.ds(pl.multiple_of(core * 16, 16), 16)
    rows_pair = pl.ds(pl.multiple_of(16 - core * 16, 16), 16)
    own_times = pl.ds(core * half_times, half_times)
    pair_times = pl.ds((1 - core) * half_times, half_times)

    def tile8(start):
        return pl.ds(pl.multiple_of(start, 8), 8)

    loads = [
        pltpu.make_async_copy(kappa_hbm.at[rows], kappa.at[pl.ds(8, 16)], load_sem.at[0]),
        pltpu.make_async_copy(
            kappa_hbm.at[tile8(16 - 8 * core)], kappa.at[tile8(24 - 24 * core)], load_sem.at[1]
        ),
        pltpu.make_async_copy(speed_hbm.at[:, rows], speed, load_sem.at[2]),
        pltpu.make_async_copy(state_hbm.at[:, rows], rhs.at[0, own_times], load_sem.at[3]),
        pltpu.make_async_copy(adjoint_hbm.at[:, rows], rhs.at[1, own_times], load_sem.at[4]),
    ]
    for load in loads:
        load.start()

    barrier = pltpu.get_barrier_semaphore()
    pl.semaphore_signal(barrier, inc=1, device_id=pair)
    pl.semaphore_signal(barrier, inc=1, device_id=beside)

    def greet(step, _):
        pl.semaphore_signal(barrier, inc=1, device_id=peer((chip + step) % chips))
        return 0

    lax.fori_loop(1, chips, greet, 0)
    pl.semaphore_wait(barrier, chips + 1)

    kappa_copy = pltpu.make_async_remote_copy(
        src_ref=kappa_hbm.at[tile8(24 * core)],
        dst_ref=kappa.at[tile8(24 - 24 * core)],
        send_sem=kappa_send,
        recv_sem=kappa_recv,
        device_id=beside,
    )
    kappa_copy.start()
    rhs_copies = []
    for field, source in enumerate((state_hbm, adjoint_hbm)):
        rhs_copies.append(
            pltpu.make_async_remote_copy(
                src_ref=source.at[:, rows_pair],
                dst_ref=rhs.at[field, own_times],
                send_sem=rhs_send.at[field],
                recv_sem=rhs_recv.at[field],
                device_id=pair,
            )
        )
        rhs_copies[field].start()

    lane = lax.broadcasted_iota(jnp.int32, (8, COL), 1)
    row = lax.broadcasted_iota(jnp.int32, (8, COL), 0)
    left = lane < 64
    first_row = row == 0
    last_row = row == 7

    zero = jnp.zeros((8, COL), jnp.float32)
    for field in range(2):
        for step in range(times):
            for z in range(2):
                first[field, step, z * 8 : z * 8 + 8, :COL] = zero
                first[field, step, z * 8 : z * 8 + 8, cells + COL :] = zero

    for load in loads[:3]:
        load.wait()
    kappa_copy.wait_recv()

    def coefficients(k, _):
        lane0 = pl.multiple_of(k * COL, COL)
        here = pl.ds(lane0, COL)
        before = pl.ds(pl.multiple_of(((k + cells // COL - 1) % (cells // COL)) * COL, COL), COL)
        after = pl.ds(pl.multiple_of(((k + 1) % (cells // COL)) * COL, COL), COL)
        x_place = k * 2 + lane // NY
        y_place = lane % NY
        for z in range(2):
            z_place = slab * 32 + core * 16 + z * 8 + row
            own = kappa[8 + z * 8 : 16 + z * 8, here]
            turned = turn(own, 64, 1)
            x_ahead = jnp.where(left, turned, turn(kappa[8 + z * 8 : 16 + z * 8, after], 64, 1))
            x_behind = jnp.where(left, turn(kappa[8 + z * 8 : 16 + z * 8, before], 64, 1), turned)
            z_ahead = jnp.where(
                last_row, turn(kappa[16 + z * 8 : 24 + z * 8, here], 1, 0), turn(own, 1, 0)
            )
            z_behind = jnp.where(
                first_row, turn(kappa[z * 8 : z * 8 + 8, here], -1, 0), turn(own, -1, 0)
            )
            diagonal = jnp.zeros((8, COL), jnp.float32)
            there = pl.ds(z * 8, 8)
            for direction, (ahead, behind, place, count, component) in enumerate(
                (
                    (z_ahead, z_behind, z_place, slabs * 32, 2),
                    (x_ahead, x_behind, x_place, cells // NY, 0),
                    (turn(own, 1, 1), turn(own, -1, 1), y_place, NY, 1),
                )
            ):
                has_ahead = place < count - 1
                has_behind = place > 0
                face_ahead = jnp.where(has_ahead, 0.5 * (own + ahead), own)
                face_behind = jnp.where(has_behind, 0.5 * (own + behind), own)
                diagonal = diagonal + face_ahead + face_behind
                drift = 0.5 * speed[component, there, here]
                couple[0, direction, 0, there, here] = jnp.where(has_ahead, face_ahead - drift, 0.0)
                couple[0, direction, 1, there, here] = jnp.where(has_behind, face_behind + drift, 0.0)
                couple[1, direction, 0, there, here] = jnp.where(has_ahead, face_ahead + drift, 0.0)
                couple[1, direction, 1, there, here] = jnp.where(has_behind, face_behind - drift, 0.0)
            large = 1.0 + diagonal
            over = 1.0 / (large * ratio)
            minus = ((large - ratio) * (large - ratio) + HALF * HALF) * over
            plus = minus + 4.0
            root = 2.0 / (minus + 2.0 + jnp.sqrt(minus * plus))
            lead = large - ratio * root
            gain = root * over / (1.0 - root * root)
            solve[0, there, here] = lead
            solve[1, there, here] = root * (1.0 / ratio)
            solve[2, there, here] = root * ratio
            solve[3, there, here] = gain
            solve[4, there, here] = gain * (HALF / lead)
            solve[5, there, here] = over * ratio
            block = z * lanes + k // columns
            inside = pl.ds(pl.multiple_of((k % columns) * COL, COL), COL)
            for index, base in ((0, root * (1.0 / ratio)), (1, root * ratio)):
                square = base * base
                fourth = square * square
                power[block, index, :, inside] = fourth * fourth
        return 0

    lax.fori_loop(0, cells // COL, coefficients, 0)

    for load in loads[3:]:
        load.wait()
    for copy in rhs_copies:
        copy.wait_recv()

    lane_mine = chip % lanes

    def carry_copy(sweep, other):
        return pltpu.make_async_remote_copy(
            src_ref=carry_out.at[sweep, other],
            dst_ref=carry_in.at[sweep, chip],
            send_sem=carry_send.at[sweep, other],
            recv_sem=carry_recv.at[sweep, chip],
            device_id=peer(other),
        )

    def entry_copy(sweep, other):
        return pltpu.make_async_remote_copy(
            src_ref=entry_out.at[sweep, other],
            dst_ref=entry_in.at[sweep, chip],
            send_sem=entry_send.at[sweep, other],
            recv_sem=entry_recv.at[sweep, chip],
            device_id=peer(other),
        )

    def carry_arrival(sweep, other):
        return pltpu.make_async_remote_copy(
            src_ref=carry_out.at[sweep, other],
            dst_ref=carry_in.at[sweep, other],
            send_sem=carry_send.at[sweep, other],
            recv_sem=carry_recv.at[sweep, other],
            device_id=peer(other),
        )

    def entry_arrival(sweep, other):
        return pltpu.make_async_remote_copy(
            src_ref=entry_out.at[sweep, other],
            dst_ref=entry_in.at[sweep, other],
            send_sem=entry_send.at[sweep, other],
            recv_sem=entry_recv.at[sweep, other],
            device_id=peer(other),
        )

    def send_carry(sweep, block):
        @pl.when(block != chip)
        def _():
            carry_copy(sweep, block).start()

        @pl.when(block == chip)
        def _():
            carry_in[sweep, chip] = carry_out[sweep, block]

    def exchange(sweep):
        def arrive(step, _):
            carry_arrival(sweep, (chip + step) % chips).wait_recv()
            return 0

        lax.fori_loop(1, chips, arrive, 0)
        forward = power[chip, 0]
        backward = power[chip, 1]
        forward_all, backward_all = forward, backward
        for _ in range(chips.bit_length() - 1):
            forward_all = forward_all * forward_all
            backward_all = backward_all * backward_all
        run_forward = carry_in[sweep, 0, 0]
        run_backward = carry_in[sweep, chips - 1, 1]
        for step in range(1, chips):
            run_forward = carry_in[sweep, step, 0] + forward * run_forward
            run_backward = carry_in[sweep, chips - 1 - step, 1] + backward * run_backward
        enter_forward = ALPHA * (run_forward / (1.0 - ALPHA * forward_all))
        enter_backward = (1.0 / ALPHA) * (run_backward / (1.0 - (1.0 / ALPHA) * backward_all))
        entry_out[sweep, 0, 0] = enter_forward
        entry_out[sweep, chips - 1, 1] = enter_backward
        for step in range(1, chips):
            enter_forward = carry_in[sweep, step - 1, 0] + forward * enter_forward
            enter_backward = carry_in[sweep, chips - step, 1] + backward * enter_backward
            entry_out[sweep, step, 0] = enter_forward
            entry_out[sweep, chips - 1 - step, 1] = enter_backward
        entry_in[sweep, chip] = entry_out[sweep, chip]

        def give(step, _):
            entry_copy(sweep, (chip + step) % chips).start()
            return 0

        lax.fori_loop(1, chips, give, 0)

    def await_entry(sweep, block):
        @pl.when(block != chip)
        def _():
            entry_arrival(sweep, block).wait_recv()

    def sums(values, forward, backward):
        ahead = values[0]
        behind = values[-1]
        for step in range(1, times):
            ahead = values[step] + forward * ahead
            behind = values[times - 1 - step] + backward * behind
        return ahead, behind

    def first_sums(step, _):
        block_lane = (lane_mine + step) % lanes
        for column in range(columns):
            here = pl.ds(pl.multiple_of(block_lane * width + column * COL, COL), COL)
            inside = slice(column * COL, column * COL + COL)
            for z in range(2):
                there = slice(z * 8, z * 8 + 8)
                lead = solve[0, there, here]
                forward = solve[1, there, here]
                backward = solve[2, there, here]
                sides = [
                    sums([rhs[field, j, there, here] for j in range(times)], forward, backward)
                    for field in range(2)
                ]
                block = z * lanes + block_lane
                carry_out[0, block, 0, :, inside] = lead * sides[0][0] + HALF * sides[1][0]
                carry_out[0, block, 1, :, inside] = lead * sides[1][1] - HALF * sides[0][1]
        for z in range(2):
            send_carry(0, z * lanes + block_lane)
        return 0

    lax.fori_loop(0, lanes, first_sums, 0)
    exchange(0)

    def solved(sweep, block_lane, column, z, emit):
        here = pl.ds(pl.multiple_of(block_lane * width + column * COL, COL), COL)
        inside = slice(column * COL, column * COL + COL)
        there = slice(z * 8, z * 8 + 8)
        block = z * lanes + block_lane
        lead = solve[0, there, here]
        forward = solve[1, there, here]
        backward = solve[2, there, here]
        gain = solve[3, there, here]
        cross = solve[4, there, here]
        plain = solve[5, there, here]
        back = entry_in[sweep, block, 1, :, inside]
        backs = [None] * times
        for j in reversed(range(times)):
            backs[j] = backward * back
            back = (
                lead * rhs[1, j, there, here] - HALF * rhs[0, j, there, here] + backs[j]
            )
        ahead = entry_in[sweep, block, 0, :, inside]
        for j in range(times):
            adjoint = rhs[1, j, there, here]
            ahead = lead * rhs[0, j, there, here] + HALF * adjoint + forward * ahead
            emit(
                j,
                gain * ahead + cross * backs[j],
                gain * backs[j] - cross * ahead + plain * adjoint,
            )

    def edge_copies(block_lane):
        part = pl.ds(pl.multiple_of(block_lane * width, width), width)
        return (
            pltpu.make_async_remote_copy(
                src_ref=edge_out.at[core, :, part],
                dst_ref=edge_in.at[1 - core, :, part],
                send_sem=edge_send.at[0, block_lane],
                recv_sem=edge_recv.at[0, block_lane],
                device_id=beside,
            ),
            pltpu.make_async_remote_copy(
                src_ref=edge_out.at[1 - core, :, part],
                dst_ref=edge_in.at[core, :, part],
                send_sem=edge_send.at[1, block_lane],
                recv_sem=edge_recv.at[1, block_lane],
                device_id=pair,
            ),
        )

    def first_values(step, _):
        block_lane = (lane_mine + step) % lanes
        for z in range(2):
            await_entry(0, z * lanes + block_lane)
            for column in range(columns):
                shifted = pl.ds(pl.multiple_of(block_lane * width + column * COL + COL, COL), COL)
                here = pl.ds(pl.multiple_of(block_lane * width + column * COL, COL), COL)

                def emit(j, state, adjoint):
                    first[0, j, z * 8 : z * 8 + 8, shifted] = state
                    first[1, j, z * 8 : z * 8 + 8, shifted] = adjoint
                    edge = slice(7 * z, 7 * z + 1)
                    edge_out[z, j : j + 1, here] = state[edge]
                    edge_out[z, times + j : times + j + 1, here] = adjoint[edge]

                solved(0, block_lane, column, z, emit)
        for copy in edge_copies(block_lane):
            copy.start()
        return 0

    lax.fori_loop(0, lanes, first_values, 0)

    def second_sums(step, _):
        block_lane = (lane_mine + step) % lanes
        for copy in edge_copies(block_lane):
            copy.wait_recv()
        for column in range(columns):
            lane0 = block_lane * width + column * COL
            here = pl.ds(pl.multiple_of(lane0, COL), COL)
            shifted = pl.ds(pl.multiple_of(lane0 + COL, COL), COL)
            before = here
            after = pl.ds(pl.multiple_of(lane0 + 2 * COL, COL), COL)
            inside = slice(column * COL, column * COL + COL)
            tiles = (slice(0, 8), slice(8, 16))
            forward = [solve[1, there, here] for there in tiles]
            backward = [solve[2, there, here] for there in tiles]
            sides = []
            for field in range(2):
                weights = [
                    [couple[field, d, s, there, here] for there in tiles]
                    for d in range(3)
                    for s in range(2)
                ]
                ahead_sum = [zero, zero]
                behind_sum = [zero, zero]
                scale = [jnp.ones((8, COL), jnp.float32)] * 2
                for j in range(times):
                    line = field * times + j
                    below = jnp.broadcast_to(edge_in[0, line : line + 1, here], (8, COL))
                    above = jnp.broadcast_to(edge_in[1, line : line + 1, here], (8, COL))
                    own = [first[field, j, there, shifted] for there in tiles]
                    up = [turn(value, 1, 0) for value in own]
                    down = [turn(value, -1, 0) for value in own]
                    z_ahead = [jnp.where(last_row, up[1], up[0]), jnp.where(last_row, above, up[1])]
                    z_behind = [
                        jnp.where(first_row, below, down[0]),
                        jnp.where(first_row, down[0], down[1]),
                    ]
                    for z in range(2):
                        there = tiles[z]
                        turned = turn(own[z], 64, 1)
                        x_ahead = jnp.where(left, turned, turn(first[field, j, there, after], 64, 1))
                        x_behind = jnp.where(left, turn(first[field, j, there, before], 64, 1), turned)
                        value = (
                            rhs[field, j, there, here]
                            + weights[0][z] * z_ahead[z]
                            + weights[1][z] * z_behind[z]
                            + weights[2][z] * x_ahead
                            + weights[3][z] * x_behind
                            + weights[4][z] * turn(own[z], 1, 1)
                            + weights[5][z] * turn(own[z], -1, 1)
                        )
                        rhs[field, j, there, here] = value
                        ahead_sum[z] = value + forward[z] * ahead_sum[z]
                        behind_sum[z] = behind_sum[z] + scale[z] * value
                        if j < times - 1:
                            scale[z] = scale[z] * backward[z]
                sides.append((ahead_sum, behind_sum))
            for z in range(2):
                lead = solve[0, tiles[z], here]
                block = z * lanes + block_lane
                carry_out[1, block, 0, :, inside] = lead * sides[0][0][z] + HALF * sides[1][0][z]
                carry_out[1, block, 1, :, inside] = lead * sides[1][1][z] - HALF * sides[0][1][z]
        for z in range(2):
            send_carry(1, z * lanes + block_lane)
        return 0

    lax.fori_loop(0, lanes, second_sums, 0)
    exchange(1)

    def store_copies(block_lane):
        part = pl.ds(pl.multiple_of(block_lane * width, width), width)
        copies = []
        for field, target in enumerate((state_out, adjoint_out)):
            copies.append(
                pltpu.make_async_copy(
                    result.at[field, own_times, :, part],
                    target.at[:, rows, part],
                    store_sem.at[field, block_lane],
                )
            )
        return copies

    def give_copies(block_lane):
        part = pl.ds(pl.multiple_of(block_lane * width, width), width)
        copies = []
        for field, target in enumerate((state_out, adjoint_out)):
            copies.append(
                pltpu.make_async_remote_copy(
                    src_ref=result.at[field, pair_times, :, part],
                    dst_ref=target.at[:, rows, part],
                    send_sem=give_send.at[field, block_lane],
                    recv_sem=give_recv.at[field, block_lane],
                    device_id=pair,
                )
            )
        return copies

    def second_values(step, _):
        block_lane = (lane_mine + step) % lanes
        for z in range(2):
            await_entry(1, z * lanes + block_lane)
            for column in range(columns):
                here = pl.ds(pl.multiple_of(block_lane * width + column * COL, COL), COL)

                def emit(j, state, adjoint):
                    result[0, j, z * 8 : z * 8 + 8, here] = state
                    result[1, j, z * 8 : z * 8 + 8, here] = adjoint

                solved(1, block_lane, column, z, emit)
        for copy in give_copies(block_lane):
            copy.start()
        for copy in store_copies(block_lane):
            copy.start()
        return 0

    lax.fori_loop(0, lanes, second_values, 0)

    kappa_copy.wait_send()
    for copy in rhs_copies:
        copy.wait_send()

    def sent(step, _):
        other = (chip + step) % chips
        for sweep in range(2):
            carry_copy(sweep, other).wait_send()
            entry_copy(sweep, other).wait_send()
        return 0

    lax.fori_loop(1, chips, sent, 0)

    def stored(block_lane, _):
        for copy in edge_copies(block_lane):
            copy.wait_send()
        for copy in give_copies(block_lane):
            copy.wait_send()
            copy.wait_recv()
        for copy in store_copies(block_lane):
            copy.wait()
        return 0

    lax.fori_loop(0, lanes, stored, 0)


def solution(mesh):
    ranks = mesh.shape["tm"]
    slabs = mesh.shape["gz"]
    chips = ranks // 2

    def body(state_rhs, adjoint_rhs, diffusivity, velocity):
        steps, depth, cells = state_rhs.shape
        times = 2 * steps
        lanes = chips // 2
        width = cells // lanes
        f32 = jnp.float32
        dma = pltpu.SemaphoreType.DMA
        anywhere = pl.BlockSpec(memory_space=pl.ANY)
        exchanged = pltpu.VMEM((2, chips, 2, 8, width), f32)
        call = pl.pallas_call(
            functools.partial(kernel, chips, slabs, cells, times),
            out_shape=[jax.ShapeDtypeStruct(state_rhs.shape, f32)] * 2,
            in_specs=[anywhere] * 4,
            out_specs=[anywhere] * 2,
            scratch_shapes=[
                pltpu.VMEM((2, times, 16, cells), f32),
                pltpu.VMEM((2, times, 16, cells + 2 * COL), f32),
                pltpu.VMEM((2, times, 16, cells), f32),
                pltpu.VMEM((32, cells), f32),
                pltpu.VMEM((3, 16, cells), f32),
                pltpu.VMEM((2, 3, 2, 16, cells), f32),
                pltpu.VMEM((6, 16, cells), f32),
                pltpu.VMEM((chips, 2, 8, width), f32),
                exchanged,
                exchanged,
                exchanged,
                exchanged,
                pltpu.VMEM((2, 2 * times, cells), f32),
                pltpu.VMEM((2, 2 * times, cells), f32),
                dma((5,)),
                dma((2,)),
                dma((2,)),
                dma,
                dma,
                dma((2, chips)),
                dma((2, chips)),
                dma((2, chips)),
                dma((2, chips)),
                dma((2, lanes)),
                dma((2, lanes)),
                dma((2, lanes)),
                dma((2, lanes)),
                dma((2, lanes)),
            ],
            compiler_params=pltpu.CompilerParams(
                collective_id=0, has_side_effects=True, vmem_limit_bytes=40 * 1024 * 1024
            ),
            cost_estimate=pl.CostEstimate(
                flops=60 * state_rhs.size, bytes_accessed=20 * state_rhs.size, transcendentals=0
            ),
        )
        return tuple(call(state_rhs, adjoint_rhs, diffusivity, velocity))

    placed = (P("tm", "gz", None), P("tm", "gz", None), P("gz", None), P(None, "gz", None))
    return jax.shard_map(
        body,
        mesh=mesh,
        in_specs=placed,
        out_specs=(P("tm", "gz", None), P("tm", "gz", None)),
        check_vma=False,
    )
```

```python
import functools
import math

import jax
import jax.numpy as jnp
from jax import lax
from jax.experimental import pallas as pl
from jax.experimental.pallas import tpu as pltpu
from jax.sharding import PartitionSpec as P

NY = 64
COL = 128
ALPHA = 0.1
HALF = 0.5


def turn(value, shift, axis):
    return pltpu.roll(value, (-shift) % value.shape[axis], axis)


def kernel(
    chips, slabs, cells, times,
    state_hbm, adjoint_hbm, kappa_hbm, speed_hbm,
    both_out, gain_out,
    rhs, first, twist, result, kappa, edge_row, rim, speed, couple, solve, power, growth,
    carry_out, carry_in, entry_out, entry_in, edge_out, edge_in,
    load_sem, rhs_send, rhs_recv, kappa_send, kappa_recv, gain_sem,
    carry_send, carry_recv, entry_send, entry_recv,
    edge_send, edge_recv, store_sem, give_send, give_recv,
):
    half_times = times // 2
    lanes = chips // 2
    columns = cells // COL
    groups = columns // lanes
    width = lanes * COL
    total = chips * times
    ratio = ALPHA ** (1.0 / total)

    me = lax.axis_index("tm")
    slab = lax.axis_index("gz")
    chip = me // 2
    core = me % 2
    pair = {"tm": chip * 2 + 1 - core, "gz": slab}
    beside = {"tm": chip * 2 + 1 - core, "gz": (slab + slabs + 2 * core - 1) % slabs}

    behind_same = {"tm": me, "gz": (slab + slabs - 1) % slabs}

    def peer(other):
        return {"tm": other * 2 + core, "gz": slab}

    rows = pl.ds(pl.multiple_of(core * 16, 16), 16)
    rows_pair = pl.ds(pl.multiple_of(16 - core * 16, 16), 16)
    own_times = pl.ds(core * half_times, half_times)
    pair_times = pl.ds((1 - core) * half_times, half_times)

    def tile8(start):
        return pl.ds(pl.multiple_of(start, 8), 8)

    loads = [
        pltpu.make_async_copy(kappa_hbm.at[rows], kappa.at[pl.ds(8, 16)], load_sem.at[0]),
        pltpu.make_async_copy(
            kappa_hbm.at[tile8(16 - 8 * core)], kappa.at[tile8(24 - 24 * core)], load_sem.at[0]
        ),
        pltpu.make_async_copy(kappa_hbm.at[pl.ds(0, 8)], edge_row, load_sem.at[0]),
        pltpu.make_async_copy(speed_hbm.at[:, rows], speed, load_sem.at[1]),
        pltpu.make_async_copy(state_hbm.at[:, rows], rhs.at[0, own_times], load_sem.at[2]),
        pltpu.make_async_copy(adjoint_hbm.at[:, rows], rhs.at[1, own_times], load_sem.at[2]),
    ]
    for load in loads:
        load.start()

    barrier = pltpu.get_barrier_semaphore()
    pl.semaphore_signal(barrier, inc=1, device_id=pair)
    pl.semaphore_signal(barrier, inc=1, device_id=beside)

    @pl.when(core == 1)
    def _():
        pl.semaphore_signal(barrier, inc=1, device_id={"tm": me, "gz": (slab + 1) % slabs})


    def greet(step, _):
        pl.semaphore_signal(barrier, inc=1, device_id=peer((chip + step) % chips))
        return 0

    lax.fori_loop(1, chips, greet, 0)
    def kappa_copy(side):
        return pltpu.make_async_remote_copy(
            src_ref=rim.at[side],
            dst_ref=rim.at[2],
            send_sem=kappa_send,
            recv_sem=kappa_recv,
            device_id=beside if side else behind_same,
        )

    def rhs_copies(group):
        part = slice(group * width, group * width + width)
        return [
            pltpu.make_async_remote_copy(
                src_ref=source.at[:, rows_pair, part],
                dst_ref=rhs.at[field, own_times, :, part],
                send_sem=rhs_send,
                recv_sem=rhs_recv.at[group],
                device_id=pair,
            )
            for field, source in enumerate((state_hbm, adjoint_hbm))
        ]

    def lane_of(half, odd):
        if lanes != 8:
            return (chip + 2 * half + odd) % lanes
        outer = half % 3 == 0
        if isinstance(half, int):
            move_x = 2 - 2 * (half // 3) if outer else 1 + 2 * odd
            move_y = odd if outer else half - 1
        else:
            move_x = jnp.where(outer, 2 - 2 * (half // 3), 1 + 2 * odd)
            move_y = jnp.where(outer, odd, half - 1)
        return ((chip // 4 + move_y) % 2) * 4 + (chip % 4 + move_x) % 4

    pairs = lanes // 2
    classes = (pairs + 1) // 2

    lane = lax.broadcasted_iota(jnp.int32, (8, COL), 1)
    row = lax.broadcasted_iota(jnp.int32, (8, COL), 0)
    left = lane < 64
    first_row = row == 0
    last_row = row == 7

    zero = jnp.zeros((8, COL), jnp.float32)
    for field in range(2):
        for step in range(times):
            for z in range(2):
                twist[field, step, z * 8 : z * 8 + 8, :COL] = zero
                twist[field, step, z * 8 : z * 8 + 8, cells + COL :] = zero

    pltpu.make_async_copy(kappa.at[pl.ds(0, 32)], kappa.at[pl.ds(0, 32)], load_sem.at[0]).wait()
    piece_width = cells // 8

    @pl.when(core == 1)
    def _():
        for side, source, line in ((0, edge_row, 0), (1, kappa, 23)):
            for piece in range(8):
                part = slice(piece * piece_width, piece * piece_width + piece_width)
                rim[side, piece : piece + 1, :] = source[line : line + 1, part]

    loads[3].wait()

    def coefficients(k, z):
        there = pl.ds(pl.multiple_of(z * 8, 8), 8)
        centre = pl.ds(pl.multiple_of(8 + z * 8, 8), 8)
        below = pl.ds(pl.multiple_of(z * 8, 8), 8)
        above = pl.ds(pl.multiple_of(16 + z * 8, 8), 8)
        lane0 = pl.multiple_of(k * COL, COL)
        here = pl.ds(lane0, COL)
        before = pl.ds(pl.multiple_of(((k + cells // COL - 1) % (cells // COL)) * COL, COL), COL)
        after = pl.ds(pl.multiple_of(((k + 1) % (cells // COL)) * COL, COL), COL)
        x_place = k * 2 + lane // NY
        y_place = lane % NY
        z_place = slab * 32 + core * 16 + z * 8 + row
        own = kappa[centre, here]
        turned = turn(own, 64, 1)
        x_ahead = jnp.where(left, turned, turn(kappa[centre, after], 64, 1))
        x_behind = jnp.where(left, turn(kappa[centre, before], 64, 1), turned)
        z_ahead = jnp.where(
            last_row, turn(kappa[above, here], 1, 0), turn(own, 1, 0)
        )
        z_behind = jnp.where(
            first_row, turn(kappa[below, here], -1, 0), turn(own, -1, 0)
        )
        diagonal = jnp.zeros((8, COL), jnp.float32)
        for direction, (ahead, behind, place, count, component) in enumerate(
            (
                (z_ahead, z_behind, z_place, slabs * 32, 2),
                (x_ahead, x_behind, x_place, cells // NY, 0),
                (turn(own, 1, 1), turn(own, -1, 1), y_place, NY, 1),
            )
        ):
            has_ahead = place < count - 1
            has_behind = place > 0
            face_ahead = jnp.where(has_ahead, 0.5 * (own + ahead), own)
            face_behind = jnp.where(has_behind, 0.5 * (own + behind), own)
            diagonal = diagonal + face_ahead + face_behind
            drift = 0.5 * speed[component, there, here]
            couple[0, direction, 0, there, here] = jnp.where(has_ahead, face_ahead - drift, 0.0)
            couple[0, direction, 1, there, here] = jnp.where(has_behind, face_behind + drift, 0.0)
            couple[1, direction, 0, there, here] = jnp.where(has_ahead, face_ahead + drift, 0.0)
            couple[1, direction, 1, there, here] = jnp.where(has_behind, face_behind - drift, 0.0)
        large = 1.0 + diagonal
        over = 1.0 / (large * ratio)
        minus = ((large - ratio) * (large - ratio) + HALF * HALF) * over
        plus = minus + 4.0
        root = 2.0 / (minus + 2.0 + jnp.sqrt(minus * plus))
        lead = large - ratio * root
        gain = root * over / (1.0 - root * root)
        solve[0, there, here] = lead
        solve[1, there, here] = root * (1.0 / ratio)
        solve[2, there, here] = root * ratio
        solve[3, there, here] = gain
        solve[4, there, here] = HALF / lead
        solve[5, there, here] = ratio * (1.0 - root * root) / root
        for index, base in ((0, root * (1.0 / ratio)), (1, root * ratio)):
            square = base * base
            fourth = square * square
            power[k // lanes, z * lanes + k % lanes, index] = fourth * fourth

    def inner_coefficients(step, _):
        for k in range(4):
            coefficients(step * 4 + k, 1 - core)
        return 0

    def outer_coefficients(step, _):
        for k in range(4):
            coefficients(step * 4 + k, core)
        return 0

    lax.fori_loop(0, cells // COL // 4, inner_coefficients, 0)
    pl.semaphore_wait(barrier, chips + 1 + core)

    @pl.when(core == 1)
    def _():
        for side in range(2):
            kappa_copy(side).start()

    for group in range(groups):
        for copy in rhs_copies(group):
            copy.start()

    pltpu.make_async_copy(rhs.at[:, own_times], rhs.at[:, own_times], load_sem.at[2]).wait()
    kappa_copy(1).wait_recv()
    for side in range(2):

        @pl.when(core == side)
        def _():
            for piece in range(8):
                part = slice(piece * piece_width, piece * piece_width + piece_width)
                kappa[7 + 17 * side : 8 + 17 * side, part] = rim[2, piece : piece + 1, :]

    lax.fori_loop(0, cells // COL // 4, outer_coefficients, 0)

    def carry_copy(lot, other):
        return pltpu.make_async_remote_copy(
            src_ref=carry_out.at[lot, other],
            dst_ref=carry_in.at[lot, chip],
            send_sem=carry_send,
            recv_sem=carry_recv.at[lot],
            device_id=peer(other),
        )

    def entry_copy(lot, other, kind):
        return pltpu.make_async_remote_copy(
            src_ref=entry_out.at[lot, other],
            dst_ref=entry_in.at[lot, chip],
            send_sem=entry_send,
            recv_sem=entry_recv.at[lot, kind],
            device_id=peer(other),
        )

    def await_entry(lot, kind):
        def take(count):
            blocks = entry_in.at[lot, pl.ds(0, count)]
            pltpu.make_async_copy(blocks, blocks, entry_recv.at[lot, kind]).wait()

        count = 2 * lanes // classes
        if classes == 1:
            take(count - 1)
        else:

            @pl.when(kind == classes - 1)
            def _():
                take(count - 1)

            @pl.when(kind < classes - 1)
            def _():
                take(count)

    def send_carry(lot, block, odd):
        if odd:
            carry_copy(lot, block).start()
        else:

            @pl.when(block != chip)
            def _():
                carry_copy(lot, block).start()

            @pl.when(block == chip)
            def _():
                carry_in[lot, chip] = carry_out[lot, block]

    def powers(group):
        for direction in range(2):
            factor = power[group, chip, direction]
            run = factor
            for step in range(1, chips + 1):
                growth[group, step, direction] = run
                run = run * factor

    def exchange(sweep, group):
        lot = sweep * groups + group

        arrived = carry_in.at[lot, pl.ds(0, chips - 1)]
        pltpu.make_async_copy(arrived, arrived, carry_recv.at[lot]).wait()
        for direction, wrap in ((0, ALPHA), (1, 1.0 / ALPHA)):
            factor = growth[group, 1, direction]
            order = range(chips) if direction == 0 else range(chips - 1, -1, -1)
            run = None
            before = []
            for place in order:
                before.append(run)
                carry = carry_in[lot, place, direction]
                run = carry if run is None else carry + factor * run
            start = wrap * (run / (1.0 - wrap * growth[group, chips, direction]))
            for step, place in enumerate(order):
                value = start
                if step:
                    value = before[step] + start * growth[group, step, direction]
                entry_out[lot, place, direction] = value
        entry_in[lot, chip] = entry_out[lot, chip]

        for half in range(pairs):
            for odd in range(2):
                for z in range(2):
                    other = z * lanes + lane_of(half, odd)
                    if half == pairs - 1 or lanes != 8:

                        @pl.when(other != chip)
                        def _():
                            entry_copy(lot, other, half // 2).start()

                    else:
                        entry_copy(lot, other, half // 2).start()

    def sums(values, forward, backward):
        ahead = values[0]
        behind = values[-1]
        for step in range(1, times):
            ahead = values[step] + forward * ahead
            behind = values[times - 1 - step] + backward * behind
        return ahead, behind

    gain_store = pltpu.make_async_copy(solve.at[3], gain_out.at[rows], load_sem.at[3])
    gain_give = pltpu.make_async_remote_copy(
        src_ref=solve.at[3],
        dst_ref=gain_out.at[rows],
        send_sem=gain_sem.at[0],
        recv_sem=gain_sem.at[1],
        device_id=pair,
    )

    def first_sums(group):
        def pair_sums(half, _):
            for odd in range(2):
                lane = lane_of(half, odd)
                here = pl.ds(pl.multiple_of(group * width + lane * COL, COL), COL)
                for z in range(2):
                    there = slice(z * 8, z * 8 + 8)
                    lead = solve[0, there, here]
                    forward = solve[1, there, here]
                    backward = solve[2, there, here]
                    sides = [
                        sums([rhs[field, j, there, here] for j in range(times)], forward, backward)
                        for field in range(2)
                    ]
                    block = z * lanes + lane
                    carry_out[group, block, 0] = lead * sides[0][0] + HALF * sides[1][0]
                    carry_out[group, block, 1] = lead * sides[1][1] - HALF * sides[0][1]
            for odd in range(2):
                for z in range(2):
                    send_carry(group, z * lanes + lane_of(half, odd), odd)
            return 0

        lax.fori_loop(0, pairs, pair_sums, 0)

    for group in range(groups):
        arrived = rhs.at[:, own_times, :, slice(0, width)]
        pltpu.make_async_copy(arrived, arrived, rhs_recv.at[group]).wait()
        first_sums(group)
    gain_store.start()
    gain_give.start()
    for group in range(groups):
        powers(group)
    for group in range(groups):
        exchange(0, group)

    def solved(sweep, group, lane, z, emit):
        here = pl.ds(pl.multiple_of(group * width + lane * COL, COL), COL)
        there = slice(z * 8, z * 8 + 8)
        lot = sweep * groups + group
        block = z * lanes + lane
        lead = solve[0, there, here]
        forward = solve[1, there, here]
        backward = solve[2, there, here]
        gain = solve[3, there, here]
        cross = solve[4, there, here]
        plain = solve[5, there, here]
        back = entry_in[lot, block, 1]
        backs = [None] * times
        for j in reversed(range(times)):
            backs[j] = backward * back
            back = (
                lead * rhs[1, j, there, here] - HALF * rhs[0, j, there, here] + backs[j]
            )
        ahead = entry_in[lot, block, 0]
        for j in range(times):
            adjoint = rhs[1, j, there, here]
            ahead = lead * rhs[0, j, there, here] + HALF * adjoint + forward * ahead
            state = ahead + cross * backs[j]
            adjoint = backs[j] - cross * ahead + plain * adjoint
            if sweep == 0:
                state, adjoint = gain * state, gain * adjoint
            emit(j, state, adjoint)

    def edge_copies(column, mark):
        part = pl.ds(pl.multiple_of(column * COL, COL), COL)
        return (
            pltpu.make_async_remote_copy(
                src_ref=edge_out.at[core, :, part],
                dst_ref=edge_in.at[1 - core, :, part],
                send_sem=edge_send,
                recv_sem=edge_recv.at[mark],
                device_id=beside,
            ),
            pltpu.make_async_remote_copy(
                src_ref=edge_out.at[1 - core, :, part],
                dst_ref=edge_in.at[core, :, part],
                send_sem=edge_send,
                recv_sem=edge_recv.at[mark],
                device_id=pair,
            ),
        )

    def first_values(group):
        def pair_values(step, _):
            half = pairs - 1 - step

            @pl.when(step % 2 == 0)
            def _():
                await_entry(group, half // 2)

            for odd in (1, 0):
                lane = lane_of(half, odd)
                column = group * lanes + lane
                here = pl.ds(pl.multiple_of(column * COL, COL), COL)
                shifted = pl.ds(pl.multiple_of(column * COL + COL, COL), COL)
                for z in range(2):

                    def emit(j, state, adjoint):
                        first[0, j, z * 8 : z * 8 + 8, here] = state
                        first[1, j, z * 8 : z * 8 + 8, here] = adjoint
                        twist[0, j, z * 8 : z * 8 + 8, shifted] = turn(state, 64, 1)
                        twist[1, j, z * 8 : z * 8 + 8, shifted] = turn(adjoint, 64, 1)
                        edge = slice(7 * z, 7 * z + 1)
                        edge_out[z, j : j + 1, here] = state[edge]
                        edge_out[z, times + j : times + j + 1, here] = adjoint[edge]

                    solved(0, group, lane, z, emit)
            for odd in (1, 0):
                for copy in edge_copies(group * lanes + lane_of(half, odd), group * classes + half // 2):
                    copy.start()
            return 0

        lax.fori_loop(0, pairs, pair_values, 0)

    for group in range(groups):
        first_values(group)

    def second_sums(group):
        def pair_sums(step, _):
            half = pairs - 1 - step

            @pl.when(step % 2 == 0)
            def _():
                arrived = edge_in.at[:, :, pl.ds(0, 2 * pairs // classes * COL)]
                sem = edge_recv.at[group * classes + half // 2]
                pltpu.make_async_copy(arrived, arrived, sem).wait()

            for odd in (1, 0):
                lane = lane_of(half, odd)
                column = group * lanes + lane
                lane0 = column * COL
                here = pl.ds(pl.multiple_of(lane0, COL), COL)
                shifted = pl.ds(pl.multiple_of(lane0 + COL, COL), COL)
                before = here
                after = pl.ds(pl.multiple_of(lane0 + 2 * COL, COL), COL)
                tiles = (slice(0, 8), slice(8, 16))
                forward = [solve[1, there, here] for there in tiles]
                backward = [solve[2, there, here] for there in tiles]
                sides = []
                for field in range(2):
                    weights = [
                        [couple[field, d, s, there, here] for there in tiles]
                        for d in range(3)
                        for s in range(2)
                    ]
                    ahead_sum = [zero, zero]
                    behind_sum = [zero, zero]
                    scale = [jnp.ones((8, COL), jnp.float32)] * 2
                    for j in range(times):
                        line = field * times + j
                        below = jnp.broadcast_to(edge_in[0, line : line + 1, here], (8, COL))
                        above = jnp.broadcast_to(edge_in[1, line : line + 1, here], (8, COL))
                        own = [first[field, j, there, here] for there in tiles]
                        up = [turn(value, 1, 0) for value in own]
                        down = [turn(value, -1, 0) for value in own]
                        z_ahead = [jnp.where(last_row, up[1], up[0]), jnp.where(last_row, above, up[1])]
                        z_behind = [
                            jnp.where(first_row, below, down[0]),
                            jnp.where(first_row, down[0], down[1]),
                        ]
                        for z in range(2):
                            there = tiles[z]
                            turned = twist[field, j, there, shifted]
                            x_ahead = jnp.where(left, turned, twist[field, j, there, after])
                            x_behind = jnp.where(left, twist[field, j, there, before], turned)
                            value = (
                                rhs[field, j, there, here]
                                + weights[0][z] * z_ahead[z]
                                + weights[1][z] * z_behind[z]
                                + weights[2][z] * x_ahead
                                + weights[3][z] * x_behind
                                + weights[4][z] * turn(own[z], 1, 1)
                                + weights[5][z] * turn(own[z], -1, 1)
                            )
                            rhs[field, j, there, here] = value
                            ahead_sum[z] = value + forward[z] * ahead_sum[z]
                            behind_sum[z] = behind_sum[z] + scale[z] * value
                            if j < times - 1:
                                scale[z] = scale[z] * backward[z]
                    sides.append((ahead_sum, behind_sum))
                for z in range(2):
                    lead = solve[0, tiles[z], here]
                    block = z * lanes + lane
                    lot = groups + group
                    carry_out[lot, block, 0] = lead * sides[0][0][z] + HALF * sides[1][0][z]
                    carry_out[lot, block, 1] = lead * sides[1][1][z] - HALF * sides[0][1][z]
            for odd in (1, 0):
                for z in range(2):
                    send_carry(groups + group, z * lanes + lane_of(half, odd), odd)
            return 0

        lax.fori_loop(0, pairs, pair_sums, 0)

    for group in range(groups):
        second_sums(group)
    for group in range(groups):
        exchange(1, group)

    def store_copy(column):
        part = pl.ds(pl.multiple_of(column * COL, COL), COL)
        return pltpu.make_async_copy(
            result.at[:, own_times, :, part], both_out.at[:, :, rows, part], store_sem
        )

    def give_copy(column):
        part = pl.ds(pl.multiple_of(column * COL, COL), COL)
        return pltpu.make_async_remote_copy(
            src_ref=result.at[:, pair_times, :, part],
            dst_ref=both_out.at[:, :, rows, part],
            send_sem=give_send,
            recv_sem=give_recv,
            device_id=pair,
        )

    def second_values(group):
        def pair_values(step, _):
            half = pairs - 1 - step

            @pl.when(step % 2 == 0)
            def _():
                await_entry(groups + group, half // 2)

            for odd in (1, 0):
                lane = lane_of(half, odd)
                here = pl.ds(pl.multiple_of((group * lanes + lane) * COL, COL), COL)
                for z in range(2):

                    def emit(j, state, adjoint):
                        result[0, j, z * 8 : z * 8 + 8, here] = state
                        result[1, j, z * 8 : z * 8 + 8, here] = adjoint

                    solved(1, group, lane, z, emit)
            for odd in (1, 0):
                give_copy(group * lanes + lane_of(half, odd)).start()
                store_copy(group * lanes + lane_of(half, odd)).start()
            return 0

        lax.fori_loop(0, pairs, pair_values, 0)

    for group in range(groups):
        second_values(group)

    def drain(ref, semaphore):
        pltpu.make_async_copy(ref, ref, semaphore).wait()

    gain_store.wait()
    gain_give.wait()

    @pl.when(core == 1)
    def _():
        drain(rim.at[pl.ds(0, 2)], kappa_send)

    drain(rhs.at[:, own_times], rhs_send)
    drain(carry_out.at[:, pl.ds(0, chips - 1)], carry_send)
    drain(entry_out.at[:, pl.ds(0, chips - 1)], entry_send)
    drain(edge_out, edge_send)
    drain(result.at[:, own_times], give_send)
    drain(result.at[:, own_times], store_sem)
    drain(result.at[:, own_times], give_recv)


def solution(mesh):
    ranks = mesh.shape["tm"]
    slabs = mesh.shape["gz"]
    chips = ranks // 2

    def body(state_rhs, adjoint_rhs, diffusivity, velocity):
        steps, depth, cells = state_rhs.shape
        times = 2 * steps
        columns = cells // COL
        groups = 2 * columns // chips
        f32 = jnp.float32
        dma = pltpu.SemaphoreType.DMA
        anywhere = pl.BlockSpec(memory_space=pl.ANY)
        exchanged = pltpu.VMEM((2 * groups, chips, 2, 8, COL), f32)
        call = pl.pallas_call(
            functools.partial(kernel, chips, slabs, cells, times),
            out_shape=[
                pltpu.VMEM((2, steps, depth, cells), f32),
                pltpu.VMEM((depth, cells), f32),
            ],
            in_specs=[anywhere] * 4,
            out_specs=[anywhere] * 2,
            scratch_shapes=[
                pltpu.VMEM((2, times, 16, cells), f32),
                pltpu.VMEM((2, times, 16, cells), f32),
                pltpu.VMEM((2, times, 16, cells + 2 * COL), f32),
                pltpu.VMEM((2, times, 16, cells), f32),
                pltpu.VMEM((32, cells), f32),
                pltpu.VMEM((8, cells), f32),
                pltpu.VMEM((3, 8, cells // 8), f32),
                pltpu.VMEM((3, 16, cells), f32),
                pltpu.VMEM((2, 3, 2, 16, cells), f32),
                pltpu.VMEM((6, 16, cells), f32),
                pltpu.VMEM((groups, chips, 2, 8, COL), f32),
                pltpu.VMEM((groups, chips + 1, 2, 8, COL), f32),
                exchanged,
                exchanged,
                exchanged,
                exchanged,
                pltpu.VMEM((2, 2 * times, cells), f32),
                pltpu.VMEM((2, 2 * times, cells), f32),
                dma((4,)),
                dma,
                dma((groups,)),
                dma,
                dma,
                dma((2,)),
                dma,
                dma((2 * groups,)),
                dma,
                dma((2 * groups, 2)),
                dma,
                dma((2 * groups,)),
                dma,
                dma,
                dma,
            ],
            compiler_params=pltpu.CompilerParams(
                collective_id=0, has_side_effects=True, vmem_limit_bytes=48 * 1024 * 1024
            ),
            cost_estimate=pl.CostEstimate(
                flops=60 * state_rhs.size, bytes_accessed=20 * state_rhs.size, transcendentals=0
            ),
        )
        held = [
            pltpu.with_memory_space_constraint(array, pltpu.HBM)
            for array in (state_rhs, adjoint_rhs, diffusivity, velocity)
        ]
        both, gain = call(*held)
        return both[0] * gain, both[1] * gain

    placed = (P("tm", "gz", None), P("tm", "gz", None), P("gz", None), P(None, "gz", None))
    return jax.shard_map(
        body,
        mesh=mesh,
        in_specs=placed,
        out_specs=(P("tm", "gz", None), P("tm", "gz", None)),
        check_vma=False,
    )
```

```python
import functools
import math

import jax
import jax.numpy as jnp
from jax import lax
from jax.experimental import pallas as pl
from jax.experimental.pallas import tpu as pltpu
from jax.sharding import PartitionSpec as P

NY = 64
COL = 128
ALPHA = 0.1
HALF = 0.5


def turn(value, shift, axis):
    return pltpu.roll(value, (-shift) % value.shape[axis], axis)


def kernel(
    chips, slabs, cells, times,
    state_hbm, adjoint_hbm, kappa_hbm, speed_hbm,
    both_out, gain_out,
    rhs, first, twist, result, kappa, edge_row, rim, speed, couple, solve, power, base, growth,
    carry_out, carry_in, entry_out, entry_in, edge_out, edge_in,
    load_sem, rhs_send, rhs_recv, kappa_send, kappa_recv, gain_sem, base_sem,
    carry_send, carry_recv, entry_send, entry_recv,
    edge_send, edge_recv, store_sem, give_send, give_recv,
):
    half_times = times // 2
    lanes = chips // 2
    columns = cells // COL
    groups = columns // lanes
    width = lanes * COL
    total = chips * times
    ratio = ALPHA ** (1.0 / total)

    me = lax.axis_index("tm")
    slab = lax.axis_index("gz")
    chip = me // 2
    core = me % 2
    pair = {"tm": chip * 2 + 1 - core, "gz": slab}
    beside = {"tm": chip * 2 + 1 - core, "gz": (slab + slabs + 2 * core - 1) % slabs}

    behind_same = {"tm": me, "gz": (slab + slabs - 1) % slabs}

    def peer(other):
        return {"tm": other * 2 + 1 - core, "gz": slab}

    rows = pl.ds(pl.multiple_of(core * 16, 16), 16)
    rows_pair = pl.ds(pl.multiple_of(16 - core * 16, 16), 16)
    own_times = pl.ds(core * half_times, half_times)
    pair_times = pl.ds((1 - core) * half_times, half_times)

    def lane_of(half, odd):
        if lanes != 8:
            return (chip + 2 * half + odd) % lanes
        outer = half % 3 == 0
        if isinstance(half, int):
            move_x = 2 - 2 * (half // 3) if outer else 1 + 2 * odd
            move_y = odd if outer else half - 1
        else:
            move_x = jnp.where(outer, 2 - 2 * (half // 3), 1 + 2 * odd)
            move_y = jnp.where(outer, odd, half - 1)
        return ((chip // 4 + move_y) % 2) * 4 + (chip % 4 + move_x) % 4

    pairs = lanes // 2
    classes = (pairs + 1) // 2

    def tile8(start):
        return pl.ds(pl.multiple_of(start, 8), 8)

    loads = [
        pltpu.make_async_copy(kappa_hbm.at[rows], kappa.at[pl.ds(8, 16)], load_sem.at[0]),
        pltpu.make_async_copy(
            kappa_hbm.at[tile8(16 - 8 * core)], kappa.at[tile8(24 - 24 * core)], load_sem.at[0]
        ),
        pltpu.make_async_copy(kappa_hbm.at[pl.ds(0, 8)], edge_row, load_sem.at[0]),
        pltpu.make_async_copy(speed_hbm.at[:, rows], speed, load_sem.at[1]),
        pltpu.make_async_copy(state_hbm.at[:, rows], rhs.at[0, own_times], load_sem.at[2]),
        pltpu.make_async_copy(adjoint_hbm.at[:, rows], rhs.at[1, own_times], load_sem.at[2]),
    ]
    for load in loads:
        load.start()

    barrier = pltpu.get_barrier_semaphore()
    for half in range(lanes // 2):
        for odd in range(2):
            for z in range(2):
                target = peer(z * lanes + lane_of(half, odd))
                pl.semaphore_signal(barrier, inc=1, device_id=target)
    pl.semaphore_signal(barrier, inc=1, device_id=beside)

    @pl.when(core == 1)
    def _():
        pl.semaphore_signal(barrier, inc=1, device_id={"tm": me, "gz": (slab + 1) % slabs})

    def kappa_copy(side):
        return pltpu.make_async_remote_copy(
            src_ref=rim.at[side],
            dst_ref=rim.at[2],
            send_sem=kappa_send,
            recv_sem=kappa_recv,
            device_id=beside if side else behind_same,
        )

    def rhs_copies(group):
        part = slice(group * width, group * width + width)
        return [
            pltpu.make_async_remote_copy(
                src_ref=source.at[:, rows_pair, part],
                dst_ref=rhs.at[field, own_times, :, part],
                send_sem=rhs_send,
                recv_sem=rhs_recv.at[group],
                device_id=pair,
            )
            for field, source in enumerate((state_hbm, adjoint_hbm))
        ]

    lane = lax.broadcasted_iota(jnp.int32, (8, COL), 1)
    row = lax.broadcasted_iota(jnp.int32, (8, COL), 0)
    left = lane < 64
    first_row = row == 0
    last_row = row == 7

    zero = jnp.zeros((8, COL), jnp.float32)
    for field in range(2):
        for step in range(times):
            for z in range(2):
                twist[field, step, z * 8 : z * 8 + 8, :COL] = zero
                twist[field, step, z * 8 : z * 8 + 8, cells + COL :] = zero

    pltpu.make_async_copy(kappa.at[pl.ds(0, 32)], kappa.at[pl.ds(0, 32)], load_sem.at[0]).wait()
    piece_width = cells // 8

    @pl.when(core == 1)
    def _():
        for side, source, line in ((0, edge_row, 0), (1, kappa, 23)):
            for piece in range(8):
                part = slice(piece * piece_width, piece * piece_width + piece_width)
                rim[side, piece : piece + 1, :] = source[line : line + 1, part]

    loads[3].wait()

    def coefficients(k, z):
        there = pl.ds(pl.multiple_of(z * 8, 8), 8)
        centre = pl.ds(pl.multiple_of(8 + z * 8, 8), 8)
        below = pl.ds(pl.multiple_of(z * 8, 8), 8)
        above = pl.ds(pl.multiple_of(16 + z * 8, 8), 8)
        lane0 = pl.multiple_of(k * COL, COL)
        here = pl.ds(lane0, COL)
        before = pl.ds(pl.multiple_of(((k + cells // COL - 1) % (cells // COL)) * COL, COL), COL)
        after = pl.ds(pl.multiple_of(((k + 1) % (cells // COL)) * COL, COL), COL)
        x_place = k * 2 + lane // NY
        y_place = lane % NY
        z_place = slab * 32 + core * 16 + z * 8 + row
        own = kappa[centre, here]
        turned = turn(own, 64, 1)
        x_ahead = jnp.where(left, turned, turn(kappa[centre, after], 64, 1))
        x_behind = jnp.where(left, turn(kappa[centre, before], 64, 1), turned)
        z_ahead = jnp.where(
            last_row, turn(kappa[above, here], 1, 0), turn(own, 1, 0)
        )
        z_behind = jnp.where(
            first_row, turn(kappa[below, here], -1, 0), turn(own, -1, 0)
        )
        diagonal = jnp.zeros((8, COL), jnp.float32)
        for direction, (ahead, behind, place, count, component) in enumerate(
            (
                (z_ahead, z_behind, z_place, slabs * 32, 2),
                (x_ahead, x_behind, x_place, cells // NY, 0),
                (turn(own, 1, 1), turn(own, -1, 1), y_place, NY, 1),
            )
        ):
            has_ahead = place < count - 1
            has_behind = place > 0
            face_ahead = jnp.where(has_ahead, 0.5 * (own + ahead), own)
            face_behind = jnp.where(has_behind, 0.5 * (own + behind), own)
            diagonal = diagonal + face_ahead + face_behind
            drift = 0.5 * speed[component, there, here]
            couple[0, direction, 0, there, here] = jnp.where(has_ahead, face_ahead - drift, 0.0)
            couple[0, direction, 1, there, here] = jnp.where(has_behind, face_behind + drift, 0.0)
            couple[1, direction, 0, there, here] = jnp.where(has_ahead, face_ahead + drift, 0.0)
            couple[1, direction, 1, there, here] = jnp.where(has_behind, face_behind - drift, 0.0)
        large = 1.0 + diagonal
        over = 1.0 / (large * ratio)
        minus = ((large - ratio) * (large - ratio) + HALF * HALF) * over
        plus = minus + 4.0
        root = 2.0 / (minus + 2.0 + jnp.sqrt(minus * plus))
        lead = large - ratio * root
        gain = root * over / (1.0 - root * root)
        solve[0, there, here] = lead
        solve[1, there, here] = root * (1.0 / ratio)
        solve[2, there, here] = root * ratio
        solve[3, there, here] = gain
        solve[4, there, here] = HALF / lead
        solve[5, there, here] = ratio * (1.0 - root * root) / root
        for index, base in ((0, root * (1.0 / ratio)), (1, root * ratio)):
            square = base * base
            fourth = square * square
            power[k // lanes, z * lanes + k % lanes, index] = fourth * fourth

    def inner_coefficients(step, _):
        for k in range(4):
            coefficients(step * 4 + k, 1 - core)
        return 0

    def outer_coefficients(step, _):
        for k in range(4):
            coefficients(step * 4 + k, core)
        return 0

    lax.fori_loop(0, cells // COL // 4, inner_coefficients, 0)
    pl.semaphore_wait(barrier, chips + 1 + core)

    @pl.when(core == 1)
    def _():
        for side in range(2):
            kappa_copy(side).start()

    for group in range(groups):
        for copy in rhs_copies(group):
            copy.start()

    pltpu.make_async_copy(rhs.at[:, own_times], rhs.at[:, own_times], load_sem.at[2]).wait()
    kappa_copy(1).wait_recv()
    for side in range(2):

        @pl.when(core == side)
        def _():
            for piece in range(8):
                part = slice(piece * piece_width, piece * piece_width + piece_width)
                kappa[7 + 17 * side : 8 + 17 * side, part] = rim[2, piece : piece + 1, :]

    lax.fori_loop(0, cells // COL // 4, outer_coefficients, 0)

    def carry_copy(lot, other):
        return pltpu.make_async_remote_copy(
            src_ref=carry_out.at[lot, other],
            dst_ref=carry_in.at[lot, chip],
            send_sem=carry_send,
            recv_sem=carry_recv.at[lot],
            device_id=peer(other),
        )

    def entry_copy(lot, other, kind):
        return pltpu.make_async_remote_copy(
            src_ref=entry_out.at[lot, other],
            dst_ref=entry_in.at[lot, chip],
            send_sem=entry_send,
            recv_sem=entry_recv.at[lot, kind],
            device_id=peer(other),
        )

    def await_entry(lot, kind):
        blocks = entry_in.at[lot, pl.ds(0, chips // classes)]
        pltpu.make_async_copy(blocks, blocks, entry_recv.at[lot, kind]).wait()

    def powers(group):
        for direction in range(2):
            factor = base[group, direction]
            run = factor
            for step in range(1, chips + 1):
                growth[group, step, direction] = run
                run = run * factor

    def exchange(sweep, group):
        lot = sweep * groups + group

        arrived = carry_in.at[lot]
        pltpu.make_async_copy(arrived, arrived, carry_recv.at[lot]).wait()
        for direction, wrap in ((0, ALPHA), (1, 1.0 / ALPHA)):
            factor = growth[group, 1, direction]
            order = range(chips) if direction == 0 else range(chips - 1, -1, -1)
            run = None
            before = []
            for place in order:
                before.append(run)
                carry = carry_in[lot, place, direction]
                run = carry if run is None else carry + factor * run
            start = wrap * (run / (1.0 - wrap * growth[group, chips, direction]))
            for step, place in enumerate(order):
                value = start
                if step:
                    value = before[step] + start * growth[group, step, direction]
                entry_out[lot, place, direction] = value
        for half in range(pairs):
            for odd in range(2):
                for z in range(2):
                    other = z * lanes + lane_of(half, odd)
                    entry_copy(lot, other, half // 2).start()

    def sums(values, forward, backward):
        ahead = values[0]
        behind = values[-1]
        for step in range(1, times):
            ahead = values[step] + forward * ahead
            behind = values[times - 1 - step] + backward * behind
        return ahead, behind

    base_copy = pltpu.make_async_remote_copy(
        src_ref=power.at[:, chip],
        dst_ref=base,
        send_sem=base_sem.at[0],
        recv_sem=base_sem.at[1],
        device_id=pair,
    )
    base_copy.start()
    gain_store = pltpu.make_async_copy(solve.at[3], gain_out.at[rows], load_sem.at[3])
    gain_give = pltpu.make_async_remote_copy(
        src_ref=solve.at[3],
        dst_ref=gain_out.at[rows],
        send_sem=gain_sem.at[0],
        recv_sem=gain_sem.at[1],
        device_id=pair,
    )

    def first_sums(group):
        def pair_sums(half, _):
            for odd in range(2):
                lane = lane_of(half, odd)
                here = pl.ds(pl.multiple_of(group * width + lane * COL, COL), COL)
                for z in range(2):
                    there = slice(z * 8, z * 8 + 8)
                    lead = solve[0, there, here]
                    forward = solve[1, there, here]
                    backward = solve[2, there, here]
                    sides = [
                        sums([rhs[field, j, there, here] for j in range(times)], forward, backward)
                        for field in range(2)
                    ]
                    block = z * lanes + lane
                    carry_out[group, block, 0] = lead * sides[0][0] + HALF * sides[1][0]
                    carry_out[group, block, 1] = lead * sides[1][1] - HALF * sides[0][1]
            for odd in range(2):
                for z in range(2):
                    carry_copy(group, z * lanes + lane_of(half, odd)).start()
            return 0

        lax.fori_loop(0, pairs, pair_sums, 0)

    for group in range(groups):
        arrived = rhs.at[:, own_times, :, slice(0, width)]
        pltpu.make_async_copy(arrived, arrived, rhs_recv.at[group]).wait()
        first_sums(group)
    gain_store.start()
    gain_give.start()
    base_copy.wait_recv()
    for group in range(groups):
        powers(group)
    for group in range(groups):
        exchange(0, group)

    def solved(sweep, group, lane, z, emit):
        here = pl.ds(pl.multiple_of(group * width + lane * COL, COL), COL)
        there = slice(z * 8, z * 8 + 8)
        lot = sweep * groups + group
        block = z * lanes + lane
        lead = solve[0, there, here]
        forward = solve[1, there, here]
        backward = solve[2, there, here]
        gain = solve[3, there, here]
        cross = solve[4, there, here]
        plain = solve[5, there, here]
        back = entry_in[lot, block, 1]
        backs = [None] * times
        for j in reversed(range(times)):
            backs[j] = backward * back
            back = (
                lead * rhs[1, j, there, here] - HALF * rhs[0, j, there, here] + backs[j]
            )
        ahead = entry_in[lot, block, 0]
        for j in range(times):
            adjoint = rhs[1, j, there, here]
            ahead = lead * rhs[0, j, there, here] + HALF * adjoint + forward * ahead
            state = ahead + cross * backs[j]
            adjoint = backs[j] - cross * ahead + plain * adjoint
            if sweep == 0:
                state, adjoint = gain * state, gain * adjoint
            emit(j, state, adjoint)

    def edge_copies(column, mark):
        part = pl.ds(pl.multiple_of(column * COL, COL), COL)
        return (
            pltpu.make_async_remote_copy(
                src_ref=edge_out.at[core, :, part],
                dst_ref=edge_in.at[1 - core, :, part],
                send_sem=edge_send,
                recv_sem=edge_recv.at[mark],
                device_id=beside,
            ),
            pltpu.make_async_remote_copy(
                src_ref=edge_out.at[1 - core, :, part],
                dst_ref=edge_in.at[core, :, part],
                send_sem=edge_send,
                recv_sem=edge_recv.at[mark],
                device_id=pair,
            ),
        )

    def first_values(group):
        def pair_values(step, _):
            half = pairs - 1 - step

            @pl.when(step % 2 == 0)
            def _():
                await_entry(group, half // 2)

            for odd in (1, 0):
                lane = lane_of(half, odd)
                column = group * lanes + lane
                here = pl.ds(pl.multiple_of(column * COL, COL), COL)
                shifted = pl.ds(pl.multiple_of(column * COL + COL, COL), COL)
                for z in range(2):

                    def emit(j, state, adjoint):
                        first[0, j, z * 8 : z * 8 + 8, here] = state
                        first[1, j, z * 8 : z * 8 + 8, here] = adjoint
                        twist[0, j, z * 8 : z * 8 + 8, shifted] = turn(state, 64, 1)
                        twist[1, j, z * 8 : z * 8 + 8, shifted] = turn(adjoint, 64, 1)
                        edge = slice(7 * z, 7 * z + 1)
                        edge_out[z, j : j + 1, here] = state[edge]
                        edge_out[z, times + j : times + j + 1, here] = adjoint[edge]

                    solved(0, group, lane, z, emit)
            for odd in (1, 0):
                for copy in edge_copies(group * lanes + lane_of(half, odd), group * classes + half // 2):
                    copy.start()
            return 0

        lax.fori_loop(0, pairs, pair_values, 0)

    for group in range(groups):
        first_values(group)

    def second_sums(group):
        def pair_sums(step, _):
            half = pairs - 1 - step

            @pl.when(step % 2 == 0)
            def _():
                arrived = edge_in.at[:, :, pl.ds(0, 2 * pairs // classes * COL)]
                sem = edge_recv.at[group * classes + half // 2]
                pltpu.make_async_copy(arrived, arrived, sem).wait()

            for odd in (1, 0):
                lane = lane_of(half, odd)
                column = group * lanes + lane
                lane0 = column * COL
                here = pl.ds(pl.multiple_of(lane0, COL), COL)
                shifted = pl.ds(pl.multiple_of(lane0 + COL, COL), COL)
                before = here
                after = pl.ds(pl.multiple_of(lane0 + 2 * COL, COL), COL)
                tiles = (slice(0, 8), slice(8, 16))
                forward = [solve[1, there, here] for there in tiles]
                backward = [solve[2, there, here] for there in tiles]
                sides = []
                for field in range(2):
                    weights = [
                        [couple[field, d, s, there, here] for there in tiles]
                        for d in range(3)
                        for s in range(2)
                    ]
                    ahead_sum = [zero, zero]
                    behind_sum = [zero, zero]
                    scale = [jnp.ones((8, COL), jnp.float32)] * 2
                    for j in range(times):
                        line = field * times + j
                        below = jnp.broadcast_to(edge_in[0, line : line + 1, here], (8, COL))
                        above = jnp.broadcast_to(edge_in[1, line : line + 1, here], (8, COL))
                        own = [first[field, j, there, here] for there in tiles]
                        up = [turn(value, 1, 0) for value in own]
                        down = [turn(value, -1, 0) for value in own]
                        z_ahead = [jnp.where(last_row, up[1], up[0]), jnp.where(last_row, above, up[1])]
                        z_behind = [
                            jnp.where(first_row, below, down[0]),
                            jnp.where(first_row, down[0], down[1]),
                        ]
                        for z in range(2):
                            there = tiles[z]
                            turned = twist[field, j, there, shifted]
                            x_ahead = jnp.where(left, turned, twist[field, j, there, after])
                            x_behind = jnp.where(left, twist[field, j, there, before], turned)
                            value = (
                                rhs[field, j, there, here]
                                + weights[0][z] * z_ahead[z]
                                + weights[1][z] * z_behind[z]
                                + weights[2][z] * x_ahead
                                + weights[3][z] * x_behind
                                + weights[4][z] * turn(own[z], 1, 1)
                                + weights[5][z] * turn(own[z], -1, 1)
                            )
                            rhs[field, j, there, here] = value
                            ahead_sum[z] = value + forward[z] * ahead_sum[z]
                            behind_sum[z] = behind_sum[z] + scale[z] * value
                            if j < times - 1:
                                scale[z] = scale[z] * backward[z]
                    sides.append((ahead_sum, behind_sum))
                for z in range(2):
                    lead = solve[0, tiles[z], here]
                    block = z * lanes + lane
                    lot = groups + group
                    carry_out[lot, block, 0] = lead * sides[0][0][z] + HALF * sides[1][0][z]
                    carry_out[lot, block, 1] = lead * sides[1][1][z] - HALF * sides[0][1][z]
            for odd in (1, 0):
                for z in range(2):
                    carry_copy(groups + group, z * lanes + lane_of(half, odd)).start()
            return 0

        lax.fori_loop(0, pairs, pair_sums, 0)

    for group in range(groups):
        second_sums(group)
    for group in range(groups):
        exchange(1, group)

    def store_copy(column):
        part = pl.ds(pl.multiple_of(column * COL, COL), COL)
        return pltpu.make_async_copy(
            result.at[:, own_times, :, part], both_out.at[:, :, rows, part], store_sem
        )

    def give_copy(column):
        part = pl.ds(pl.multiple_of(column * COL, COL), COL)
        return pltpu.make_async_remote_copy(
            src_ref=result.at[:, pair_times, :, part],
            dst_ref=both_out.at[:, :, rows, part],
            send_sem=give_send,
            recv_sem=give_recv,
            device_id=pair,
        )

    def second_values(group):
        def pair_values(step, _):
            half = pairs - 1 - step

            @pl.when(step % 2 == 0)
            def _():
                await_entry(groups + group, half // 2)

            for odd in (1, 0):
                lane = lane_of(half, odd)
                here = pl.ds(pl.multiple_of((group * lanes + lane) * COL, COL), COL)
                for z in range(2):

                    def emit(j, state, adjoint):
                        result[0, j, z * 8 : z * 8 + 8, here] = state
                        result[1, j, z * 8 : z * 8 + 8, here] = adjoint

                    solved(1, group, lane, z, emit)
            for odd in (1, 0):
                give_copy(group * lanes + lane_of(half, odd)).start()
                store_copy(group * lanes + lane_of(half, odd)).start()
            return 0

        lax.fori_loop(0, pairs, pair_values, 0)

    for group in range(groups):
        second_values(group)

    def drain(ref, semaphore):
        pltpu.make_async_copy(ref, ref, semaphore).wait()

    gain_store.wait()
    gain_give.wait()
    base_copy.wait_send()

    @pl.when(core == 1)
    def _():
        drain(rim.at[pl.ds(0, 2)], kappa_send)

    drain(rhs.at[:, own_times], rhs_send)
    drain(carry_out, carry_send)
    drain(entry_out, entry_send)
    drain(edge_out, edge_send)
    drain(result.at[:, own_times], give_send)
    drain(result.at[:, own_times], store_sem)
    drain(result.at[:, own_times], give_recv)


def solution(mesh):
    ranks = mesh.shape["tm"]
    slabs = mesh.shape["gz"]
    chips = ranks // 2

    def body(state_rhs, adjoint_rhs, diffusivity, velocity):
        steps, depth, cells = state_rhs.shape
        times = 2 * steps
        columns = cells // COL
        groups = 2 * columns // chips
        f32 = jnp.float32
        dma = pltpu.SemaphoreType.DMA
        anywhere = pl.BlockSpec(memory_space=pl.ANY)
        exchanged = pltpu.VMEM((2 * groups, chips, 2, 8, COL), f32)
        call = pl.pallas_call(
            functools.partial(kernel, chips, slabs, cells, times),
            out_shape=[
                pltpu.VMEM((2, steps, depth, cells), f32),
                pltpu.VMEM((depth, cells), f32),
            ],
            in_specs=[anywhere] * 4,
            out_specs=[anywhere] * 2,
            scratch_shapes=[
                pltpu.VMEM((2, times, 16, cells), f32),
                pltpu.VMEM((2, times, 16, cells), f32),
                pltpu.VMEM((2, times, 16, cells + 2 * COL), f32),
                pltpu.VMEM((2, times, 16, cells), f32),
                pltpu.VMEM((32, cells), f32),
                pltpu.VMEM((8, cells), f32),
                pltpu.VMEM((3, 8, cells // 8), f32),
                pltpu.VMEM((3, 16, cells), f32),
                pltpu.VMEM((2, 3, 2, 16, cells), f32),
                pltpu.VMEM((6, 16, cells), f32),
                pltpu.VMEM((groups, chips, 2, 8, COL), f32),
                pltpu.VMEM((groups, 2, 8, COL), f32),
                pltpu.VMEM((groups, chips + 1, 2, 8, COL), f32),
                exchanged,
                exchanged,
                exchanged,
                exchanged,
                pltpu.VMEM((2, 2 * times, cells), f32),
                pltpu.VMEM((2, 2 * times, cells), f32),
                dma((4,)),
                dma,
                dma((groups,)),
                dma,
                dma,
                dma((2,)),
                dma((2,)),
                dma,
                dma((2 * groups,)),
                dma,
                dma((2 * groups, 2)),
                dma,
                dma((2 * groups,)),
                dma,
                dma,
                dma,
            ],
            compiler_params=pltpu.CompilerParams(
                collective_id=0, has_side_effects=True, vmem_limit_bytes=48 * 1024 * 1024
            ),
            cost_estimate=pl.CostEstimate(
                flops=60 * state_rhs.size, bytes_accessed=20 * state_rhs.size, transcendentals=0
            ),
        )
        held = [
            pltpu.with_memory_space_constraint(array, pltpu.HBM)
            for array in (state_rhs, adjoint_rhs, diffusivity, velocity)
        ]
        both, gain = call(*held)
        return both[0] * gain, both[1] * gain

    placed = (P("tm", "gz", None), P("tm", "gz", None), P("gz", None), P(None, "gz", None))
    return jax.shard_map(
        body,
        mesh=mesh,
        in_specs=placed,
        out_specs=(P("tm", "gz", None), P("tm", "gz", None)),
        check_vma=False,
    )
```

```python
import functools
import math

import jax
import jax.numpy as jnp
from jax import lax
from jax.experimental import pallas as pl
from jax.experimental.pallas import tpu as pltpu
from jax.sharding import PartitionSpec as P

NY = 64
COL = 128
ALPHA = 0.1
HALF = 0.5


def turn(value, shift, axis):
    return pltpu.roll(value, (-shift) % value.shape[axis], axis)


def kernel(
    chips, slabs, cells, times,
    state_hbm, adjoint_hbm, kappa_hbm, speed_hbm,
    both_out, gain_out,
    rhs, first, twist, result, kappa, edge_row, rim, speed, couple, solve, power, base, growth,
    carry_out, carry_in, entry_out, entry_in, edge_out, edge_in,
    response, entered, pack_out, pack_in, twin, given, twin_entry,
    load_sem, rhs_send, rhs_recv, kappa_send, kappa_recv, gain_sem, base_sem,
    carry_send, carry_recv, entry_send, entry_recv,
    edge_send, edge_recv, pack_send, pack_recv, twin_send, twin_recv, twin_entry_send, twin_entry_recv, give_send, give_recv,
):
    half_times = times // 2
    lanes = chips // 2
    columns = cells // COL
    groups = columns // lanes
    width = lanes * COL
    total = chips * times
    ratio = ALPHA ** (1.0 / total)

    me = lax.axis_index("tm")
    slab = lax.axis_index("gz")
    chip = me // 2
    core = me % 2
    pair = {"tm": chip * 2 + 1 - core, "gz": slab}
    beside = {"tm": chip * 2 + 1 - core, "gz": (slab + slabs + 2 * core - 1) % slabs}

    behind_same = {"tm": me, "gz": (slab + slabs - 1) % slabs}

    def peer(other):
        return {"tm": other * 2 + 1 - core, "gz": slab}

    rows = pl.ds(pl.multiple_of(core * 16, 16), 16)
    rows_pair = pl.ds(pl.multiple_of(16 - core * 16, 16), 16)
    own_times = pl.ds(core * half_times, half_times)
    pair_times = pl.ds((1 - core) * half_times, half_times)

    def lane_of(half, odd):
        if lanes != 8:
            return (chip + 2 * half + odd) % lanes
        outer = half % 3 == 0
        if isinstance(half, int):
            move_x = 2 - 2 * (half // 3) if outer else 1 + 2 * odd
            move_y = odd if outer else half - 1
        else:
            move_x = jnp.where(outer, 2 - 2 * (half // 3), 1 + 2 * odd)
            move_y = jnp.where(outer, odd, half - 1)
        return ((chip // 4 + move_y) % 2) * 4 + (chip % 4 + move_x) % 4

    pairs = lanes // 2
    classes = (pairs + 1) // 2

    def tile8(start):
        return pl.ds(pl.multiple_of(start, 8), 8)

    loads = [
        pltpu.make_async_copy(kappa_hbm.at[rows], kappa.at[pl.ds(8, 16)], load_sem.at[0]),
        pltpu.make_async_copy(
            kappa_hbm.at[tile8(16 - 8 * core)], kappa.at[tile8(24 - 24 * core)], load_sem.at[0]
        ),
        pltpu.make_async_copy(kappa_hbm.at[pl.ds(0, 8)], edge_row, load_sem.at[0]),
        pltpu.make_async_copy(speed_hbm.at[:, rows], speed, load_sem.at[1]),
        pltpu.make_async_copy(state_hbm.at[:, rows], rhs.at[0, own_times], load_sem.at[2]),
        pltpu.make_async_copy(adjoint_hbm.at[:, rows], rhs.at[1, own_times], load_sem.at[2]),
    ]
    for load in loads:
        load.start()

    barrier = pltpu.get_barrier_semaphore()
    for half in range(lanes // 2):
        for odd in range(2):
            for z in range(2):
                target = peer(z * lanes + lane_of(half, odd))
                pl.semaphore_signal(barrier, inc=1, device_id=target)
    pl.semaphore_signal(barrier, inc=1, device_id=beside)

    @pl.when(core == 1)
    def _():
        pl.semaphore_signal(barrier, inc=1, device_id={"tm": me, "gz": (slab + 1) % slabs})

    def kappa_copy(side):
        return pltpu.make_async_remote_copy(
            src_ref=rim.at[side],
            dst_ref=rim.at[2],
            send_sem=kappa_send,
            recv_sem=kappa_recv,
            device_id=beside if side else behind_same,
        )

    def rhs_copies(group):
        part = slice(group * width, group * width + width)
        return [
            pltpu.make_async_remote_copy(
                src_ref=source.at[:, rows_pair, part],
                dst_ref=rhs.at[field, own_times, :, part],
                send_sem=rhs_send,
                recv_sem=rhs_recv.at[group],
                device_id=pair,
            )
            for field, source in enumerate((state_hbm, adjoint_hbm))
        ]

    lane = lax.broadcasted_iota(jnp.int32, (8, COL), 1)
    row = lax.broadcasted_iota(jnp.int32, (8, COL), 0)
    left = lane < 64
    first_row = row == 0
    last_row = row == 7

    zero = jnp.zeros((8, COL), jnp.float32)
    for field in range(2):
        for step in range(times):
            for z in range(2):
                twist[field, step, z * 8 : z * 8 + 8, :COL] = zero
                twist[field, step, z * 8 : z * 8 + 8, cells + COL :] = zero

    pltpu.make_async_copy(kappa.at[pl.ds(0, 32)], kappa.at[pl.ds(0, 32)], load_sem.at[0]).wait()
    piece_width = cells // 8

    @pl.when(core == 1)
    def _():
        for side, source, line in ((0, edge_row, 0), (1, kappa, 23)):
            for piece in range(8):
                part = slice(piece * piece_width, piece * piece_width + piece_width)
                rim[side, piece : piece + 1, :] = source[line : line + 1, part]

    loads[3].wait()

    def coefficients(k, z):
        there = pl.ds(pl.multiple_of(z * 8, 8), 8)
        centre = pl.ds(pl.multiple_of(8 + z * 8, 8), 8)
        below = pl.ds(pl.multiple_of(z * 8, 8), 8)
        above = pl.ds(pl.multiple_of(16 + z * 8, 8), 8)
        lane0 = pl.multiple_of(k * COL, COL)
        here = pl.ds(lane0, COL)
        before = pl.ds(pl.multiple_of(((k + cells // COL - 1) % (cells // COL)) * COL, COL), COL)
        after = pl.ds(pl.multiple_of(((k + 1) % (cells // COL)) * COL, COL), COL)
        x_place = k * 2 + lane // NY
        y_place = lane % NY
        z_place = slab * 32 + core * 16 + z * 8 + row
        own = kappa[centre, here]
        turned = turn(own, 64, 1)
        x_ahead = jnp.where(left, turned, turn(kappa[centre, after], 64, 1))
        x_behind = jnp.where(left, turn(kappa[centre, before], 64, 1), turned)
        z_ahead = jnp.where(
            last_row, turn(kappa[above, here], 1, 0), turn(own, 1, 0)
        )
        z_behind = jnp.where(
            first_row, turn(kappa[below, here], -1, 0), turn(own, -1, 0)
        )
        diagonal = jnp.zeros((8, COL), jnp.float32)
        for direction, (ahead, behind, place, count, component) in enumerate(
            (
                (z_ahead, z_behind, z_place, slabs * 32, 2),
                (x_ahead, x_behind, x_place, cells // NY, 0),
                (turn(own, 1, 1), turn(own, -1, 1), y_place, NY, 1),
            )
        ):
            has_ahead = place < count - 1
            has_behind = place > 0
            face_ahead = jnp.where(has_ahead, 0.5 * (own + ahead), own)
            face_behind = jnp.where(has_behind, 0.5 * (own + behind), own)
            diagonal = diagonal + face_ahead + face_behind
            drift = 0.5 * speed[component, there, here]
            couple[0, direction, 0, there, here] = jnp.where(has_ahead, face_ahead - drift, 0.0)
            couple[0, direction, 1, there, here] = jnp.where(has_behind, face_behind + drift, 0.0)
            couple[1, direction, 0, there, here] = jnp.where(has_ahead, face_ahead + drift, 0.0)
            couple[1, direction, 1, there, here] = jnp.where(has_behind, face_behind - drift, 0.0)
        large = 1.0 + diagonal
        over = 1.0 / (large * ratio)
        minus = ((large - ratio) * (large - ratio) + HALF * HALF) * over
        plus = minus + 4.0
        root = 2.0 / (minus + 2.0 + jnp.sqrt(minus * plus))
        lead = large - ratio * root
        gain = root * over / (1.0 - root * root)
        solve[0, there, here] = lead
        solve[1, there, here] = root * (1.0 / ratio)
        solve[2, there, here] = root * ratio
        solve[3, there, here] = gain
        solve[4, there, here] = HALF / lead
        solve[5, there, here] = ratio * (1.0 - root * root) / root
        for index, base in ((0, root * (1.0 / ratio)), (1, root * ratio)):
            square = base * base
            fourth = square * square
            power[k // lanes, z * lanes + k % lanes, index] = fourth * fourth

    def inner_coefficients(step, _):
        for k in range(4):
            coefficients(step * 4 + k, 1 - core)
        return 0

    def outer_coefficients(step, _):
        for k in range(4):
            coefficients(step * 4 + k, core)
        return 0

    lax.fori_loop(0, cells // COL // 4, inner_coefficients, 0)
    pl.semaphore_wait(barrier, chips + 1 + core)

    @pl.when(core == 1)
    def _():
        for side in range(2):
            kappa_copy(side).start()

    for group in range(groups):
        for copy in rhs_copies(group):
            copy.start()

    pltpu.make_async_copy(rhs.at[:, own_times], rhs.at[:, own_times], load_sem.at[2]).wait()
    kappa_copy(1).wait_recv()
    for side in range(2):

        @pl.when(core == side)
        def _():
            for piece in range(8):
                part = slice(piece * piece_width, piece * piece_width + piece_width)
                kappa[7 + 17 * side : 8 + 17 * side, part] = rim[2, piece : piece + 1, :]

    lax.fori_loop(0, cells // COL // 4, outer_coefficients, 0)

    def carry_copy(lot, other):
        return pltpu.make_async_remote_copy(
            src_ref=carry_out.at[lot, other],
            dst_ref=carry_in.at[lot, chip],
            send_sem=carry_send,
            recv_sem=carry_recv.at[lot],
            device_id=peer(other),
        )

    def entry_copy(lot, other, kind):
        return pltpu.make_async_remote_copy(
            src_ref=entry_out.at[lot, other],
            dst_ref=entry_in.at[lot, chip],
            send_sem=entry_send,
            recv_sem=entry_recv.at[lot, kind],
            device_id=peer(other),
        )

    def await_entry(lot, kind):
        blocks = entry_in.at[lot, pl.ds(0, chips // classes)]
        pltpu.make_async_copy(blocks, blocks, entry_recv.at[lot, kind]).wait()

    def powers(group):
        for direction in range(2):
            factor = base[group, direction]
            run = factor
            for step in range(1, chips + 1):
                growth[group, step, direction] = run
                run = run * factor

    def exchange(sweep, group):
        lot = sweep * groups + group

        arrived = carry_in.at[lot]
        pltpu.make_async_copy(arrived, arrived, carry_recv.at[lot]).wait()
        for direction, wrap in ((0, ALPHA), (1, 1.0 / ALPHA)):
            factor = growth[group, 1, direction]
            order = range(chips) if direction == 0 else range(chips - 1, -1, -1)
            run = None
            before = []
            for place in order:
                before.append(run)
                carry = carry_in[lot, place, direction]
                run = carry if run is None else carry + factor * run
            start = wrap * (run / (1.0 - wrap * growth[group, chips, direction]))
            for step, place in enumerate(order):
                value = start
                if step:
                    value = before[step] + start * growth[group, step, direction]
                entry_out[lot, place, direction] = value
        for half in range(pairs):
            for odd in range(2):
                for z in range(2):
                    other = z * lanes + lane_of(half, odd)
                    entry_copy(lot, other, half // 2).start()

    def sums(values, forward, backward):
        ahead = values[0]
        behind = values[-1]
        for step in range(1, times):
            ahead = values[step] + forward * ahead
            behind = values[times - 1 - step] + backward * behind
        return ahead, behind

    base_copy = pltpu.make_async_remote_copy(
        src_ref=power.at[:, chip],
        dst_ref=base,
        send_sem=base_sem.at[0],
        recv_sem=base_sem.at[1],
        device_id=pair,
    )
    base_copy.start()
    gain_store = pltpu.make_async_copy(solve.at[3], gain_out.at[rows], load_sem.at[3])
    gain_give = pltpu.make_async_remote_copy(
        src_ref=solve.at[3],
        dst_ref=gain_out.at[rows],
        send_sem=gain_sem.at[0],
        recv_sem=gain_sem.at[1],
        device_id=pair,
    )

    twin_copies = [
        pltpu.make_async_remote_copy(
            src_ref=solve.at[source],
            dst_ref=twin.at[target],
            send_sem=twin_send,
            recv_sem=twin_recv,
            device_id=pair,
        )
        for target, source in enumerate((1, 4))
    ]

    def first_sums(group):
        def pair_sums(half, _):
            for odd in range(2):
                lane = lane_of(half, odd)
                here = pl.ds(pl.multiple_of(group * width + lane * COL, COL), COL)
                for z in range(2):
                    there = slice(z * 8, z * 8 + 8)
                    lead = solve[0, there, here]
                    forward = solve[1, there, here]
                    backward = solve[2, there, here]
                    sides = [
                        sums([rhs[field, j, there, here] for j in range(times)], forward, backward)
                        for field in range(2)
                    ]
                    block = z * lanes + lane
                    carry_out[group, block, 0] = lead * sides[0][0] + HALF * sides[1][0]
                    carry_out[group, block, 1] = lead * sides[1][1] - HALF * sides[0][1]
            for odd in range(2):
                for z in range(2):
                    carry_copy(group, z * lanes + lane_of(half, odd)).start()
            return 0

        lax.fori_loop(0, pairs, pair_sums, 0)

    for group in range(groups):
        arrived = rhs.at[:, own_times, :, slice(0, width)]
        pltpu.make_async_copy(arrived, arrived, rhs_recv.at[group]).wait()
        first_sums(group)
    gain_store.start()
    gain_give.start()
    for copy in twin_copies:
        copy.start()
    base_copy.wait_recv()
    for group in range(groups):
        powers(group)
    def solved(group, lane, z, scaled, ahead, back, emit):
        here = pl.ds(pl.multiple_of(group * width + lane * COL, COL), COL)
        there = slice(z * 8, z * 8 + 8)
        lead = solve[0, there, here]
        forward = solve[1, there, here]
        backward = solve[2, there, here]
        gain = solve[3, there, here]
        cross = solve[4, there, here]
        plain = solve[5, there, here]
        backs = [None] * times
        for j in reversed(range(times)):
            backs[j] = backward * back
            back = (
                lead * rhs[1, j, there, here] - HALF * rhs[0, j, there, here] + backs[j]
            )
        for j in range(times):
            adjoint = rhs[1, j, there, here]
            ahead = lead * rhs[0, j, there, here] + HALF * adjoint + forward * ahead
            state = ahead + cross * backs[j]
            adjoint = backs[j] - cross * ahead + plain * adjoint
            if scaled:
                state, adjoint = gain * state, gain * adjoint
            emit(j, state, adjoint)

    def edge_copies(column, mark):
        part = pl.ds(pl.multiple_of(column * COL, COL), COL)
        return (
            pltpu.make_async_remote_copy(
                src_ref=edge_out.at[core, :, part],
                dst_ref=edge_in.at[1 - core, :, part],
                send_sem=edge_send,
                recv_sem=edge_recv.at[mark],
                device_id=beside,
            ),
            pltpu.make_async_remote_copy(
                src_ref=edge_out.at[1 - core, :, part],
                dst_ref=edge_in.at[core, :, part],
                send_sem=edge_send,
                recv_sem=edge_recv.at[mark],
                device_id=pair,
            ),
        )

    def first_values(group):
        def pair_values(step, _):
            half = pairs - 1 - step
            for odd in (1, 0):
                lane = lane_of(half, odd)
                column = group * lanes + lane
                here = pl.ds(pl.multiple_of(column * COL, COL), COL)
                shifted = pl.ds(pl.multiple_of(column * COL + COL, COL), COL)
                for z in range(2):

                    def emit(j, state, adjoint):
                        first[0, j, z * 8 : z * 8 + 8, here] = state
                        first[1, j, z * 8 : z * 8 + 8, here] = adjoint
                        twist[0, j, z * 8 : z * 8 + 8, shifted] = turn(state, 64, 1)
                        twist[1, j, z * 8 : z * 8 + 8, shifted] = turn(adjoint, 64, 1)
                        edge = slice(7 * z, 7 * z + 1)
                        edge_out[z, j : j + 1, here] = state[edge]
                        edge_out[z, times + j : times + j + 1, here] = adjoint[edge]

                    solved(group, lane, z, True, zero, zero, emit)
                    line = z * 15
                    edge_out[z, 2 * times : 2 * times + 1, here] = solve[1, line : line + 1, here]
                    edge_out[z, 2 * times + 1 : 2 * times + 2, here] = solve[4, line : line + 1, here]
            for odd in (1, 0):
                for copy in edge_copies(group * lanes + lane_of(half, odd), group * classes + half // 2):
                    copy.start()
            return 0

        lax.fori_loop(0, pairs, pair_values, 0)

    for group in range(groups):
        first_values(group)

    for group in range(groups):
        exchange(0, group)

    tiles = (slice(0, 8), slice(8, 16))

    def column_of(column):
        return pl.ds(pl.multiple_of((column % columns) * COL, COL), COL)

    def in_z(own, below, above):
        up = [turn(value, 1, 0) for value in own]
        down = [turn(value, -1, 0) for value in own]
        return (
            [jnp.where(last_row, up[1], up[0]), jnp.where(last_row, above, up[1])],
            [jnp.where(first_row, below, down[0]), jnp.where(first_row, down[0], down[1])],
        )

    def in_plane(own, before, after):
        turned = turn(own, 64, 1)
        return (
            jnp.where(left, turned, turn(after, 64, 1)),
            jnp.where(left, turn(before, 64, 1), turned),
            turn(own, 1, 1),
            turn(own, -1, 1),
        )

    def edge_rows(line, here):
        return [jnp.broadcast_to(edge_in[side, line : line + 1, here], (8, COL)) for side in range(2)]

    def make_responses(column):
        here, before, after = column_of(column), column_of(column + columns - 1), column_of(column + 1)
        sides = []
        for index, line in ((1, 2 * times), (4, 2 * times + 1)):
            own = [solve[index, there, here] for there in tiles]
            z_ahead, z_behind = in_z(own, *edge_rows(line, here))
            sides.append(
                [
                    (z_ahead[z], z_behind[z])
                    + in_plane(own[z], solve[index, tiles[z], before], solve[index, tiles[z], after])
                    for z in range(2)
                ]
            )
        square_ratio = ratio * ratio
        for z in range(2):
            there = tiles[z]
            lead = solve[0, there, here]
            base_own = solve[1, there, here]
            square_own = base_own * base_own
            fourth_own = square_own * square_own
            for place in range(6):
                base_near, cross_near = sides[0][z][place], sides[1][z][place]
                square_near = base_near * base_near
                mixed = (base_own + base_near) * (square_own + square_near)
                mixed = mixed * (fourth_own + square_near * square_near)
                product = square_ratio * (base_own * base_near)
                square = product * product
                series = (1.0 + product) * (1.0 + square) * (1.0 + square * square)
                to_state = couple[0, place // 2, place % 2, there, here]
                to_adjoint = couple[1, place // 2, place % 2, there, here]
                state_lead, state_half = lead * to_state, HALF * to_state
                adjoint_lead, adjoint_half = lead * to_adjoint, HALF * to_adjoint
                response[place, 0, there, here] = mixed * (state_lead - cross_near * adjoint_half)
                response[place, 1, there, here] = series * (cross_near * state_lead + adjoint_half)
                response[place, 2, there, here] = -series * (state_half + cross_near * adjoint_lead)
                response[place, 3, there, here] = (square_ratio**7 * mixed) * (
                    adjoint_lead - cross_near * state_half
                )

    def couplings(group, summed):
        def pair_couplings(step, _):
            half = pairs - 1 - step
            if summed:

                @pl.when(step % 2 == 0)
                def _():
                    arrived = edge_in.at[:, :, pl.ds(0, 2 * pairs // classes * COL)]
                    sem = edge_recv.at[group * classes + half // 2]
                    pltpu.make_async_copy(arrived, arrived, sem).wait()

            for odd in (1, 0):
                lane = lane_of(half, odd)
                column = group * lanes + lane
                lane0 = column * COL
                here = pl.ds(pl.multiple_of(lane0, COL), COL)
                shifted = pl.ds(pl.multiple_of(lane0 + COL, COL), COL)
                after = pl.ds(pl.multiple_of(lane0 + 2 * COL, COL), COL)
                forward = [solve[1, there, here] for there in tiles]
                backward = [solve[2, there, here] for there in tiles]
                sides = []
                for field in range(2):
                    weights = [
                        [couple[field, d, s, there, here] for there in tiles]
                        for d in range(3)
                        for s in range(2)
                    ]
                    ahead_sum = [zero, zero]
                    behind_sum = [zero, zero]
                    scale = [jnp.ones((8, COL), jnp.float32)] * 2
                    for j in range(times):
                        own = [first[field, j, there, here] for there in tiles]
                        z_ahead, z_behind = in_z(own, *edge_rows(field * times + j, here))
                        for z in range(2):
                            there = tiles[z]
                            turned = twist[field, j, there, shifted]
                            x_ahead = jnp.where(left, turned, twist[field, j, there, after])
                            x_behind = jnp.where(left, twist[field, j, there, here], turned)
                            value = (
                                rhs[field, j, there, here]
                                + weights[0][z] * z_ahead[z]
                                + weights[1][z] * z_behind[z]
                                + weights[2][z] * x_ahead
                                + weights[3][z] * x_behind
                                + weights[4][z] * turn(own[z], 1, 1)
                                + weights[5][z] * turn(own[z], -1, 1)
                            )
                            rhs[field, j, there, here] = value
                            if summed:
                                ahead_sum[z] = value + forward[z] * ahead_sum[z]
                                behind_sum[z] = behind_sum[z] + scale[z] * value
                                if j < times - 1:
                                    scale[z] = scale[z] * backward[z]
                    sides.append((ahead_sum, behind_sum))
                if summed:
                    make_responses(column)
                    for z in range(2):
                        lead = solve[0, tiles[z], here]
                        block = z * lanes + lane
                        lot = groups + group
                        carry_out[lot, block, 0] = lead * sides[0][0][z] + HALF * sides[1][0][z]
                        carry_out[lot, block, 1] = lead * sides[1][1][z] - HALF * sides[0][1][z]
            return 0

        lax.fori_loop(0, pairs, pair_couplings, 0)

    for group in range(groups):
        couplings(group, True)

    def entries(group):
        def pair_entries(step, _):
            half = pairs - 1 - step

            @pl.when(step % 2 == 0)
            def _():
                await_entry(group, half // 2)

            for odd in (1, 0):
                lane = lane_of(half, odd)
                here = pl.ds(pl.multiple_of((group * lanes + lane) * COL, COL), COL)
                for z in range(2):
                    gain = solve[3, tiles[z], here]
                    for index in range(2):
                        entered[index, 8 + z * 8 : 16 + z * 8, here] = (
                            gain * solve[1 + index, tiles[z], here] * entry_in[group, z * lanes + lane, index]
                        )
            return 0

        lax.fori_loop(0, pairs, pair_entries, 0)

    for group in range(groups):
        entries(group)
    for side in range(2):
        for index in range(2):
            for column in range(columns):
                part = slice(column * COL, column * COL + COL)
                line = 8 + 15 * side
                pack_out[side, index, column : column + 1, :] = entered[index, line : line + 1, part]
    pack_copies = [
        pltpu.make_async_remote_copy(
            src_ref=pack_out.at[1 - core],
            dst_ref=pack_in.at[core],
            send_sem=pack_send,
            recv_sem=pack_recv.at[0],
            device_id=pair,
        ),
        pltpu.make_async_remote_copy(
            src_ref=pack_out.at[core],
            dst_ref=pack_in.at[1 - core],
            send_sem=pack_send,
            recv_sem=pack_recv.at[1],
            device_id=beside,
        ),
    ]
    for copy in pack_copies:
        copy.start()

    def unpack(side):
        for index in range(2):
            for column in range(columns):
                part = slice(column * COL, column * COL + COL)
                line = 7 + 17 * side
                entered[index, line : line + 1, part] = pack_in[side, index, column : column + 1, :]

    def second_sums(step, _):
        for k in range(4):
            column = step * 4 + k
            here, before, after = column_of(column), column_of(column + columns - 1), column_of(column + 1)
            lot = groups + column // lanes
            sides = [[], []]
            for index in range(2):
                own = [entered[index, 8 + z * 8 : 16 + z * 8, here] for z in range(2)]
                z_ahead, z_behind = in_z(own, zero, zero)
                for z in range(2):
                    centre = slice(8 + z * 8, 16 + z * 8)
                    sides[z].append(
                        (z_ahead[z], z_behind[z])
                        + in_plane(own[z], entered[index, centre, before], entered[index, centre, after])
                    )
            for z in range(2):
                block = z * lanes + column % lanes
                for direction in range(2):
                    total_sum = carry_out[lot, block, direction]
                    for place in range(6):
                        for index in range(2):
                            factor = response[place, 2 * direction + index, tiles[z], here]
                            total_sum = total_sum + factor * sides[z][index][place]
                    carry_out[lot, block, direction] = total_sum
        return 0

    lax.fori_loop(0, columns // 4, second_sums, 0)

    def add_rows(side):
        z, place, edge = side, 1 - side, (last_row if side else first_row)
        for column in range(columns):
            here = slice(column * COL, column * COL + COL)
            lot, block = groups + column // lanes, z * lanes + column % lanes
            enter = [
                jnp.broadcast_to(pack_in[side, index, column : column + 1, :], (8, COL)) for index in range(2)
            ]
            for direction in range(2):
                more = (
                    response[place, 2 * direction, tiles[z], here] * enter[0]
                    + response[place, 2 * direction + 1, tiles[z], here] * enter[1]
                )
                carry_out[lot, block, direction] = carry_out[lot, block, direction] + jnp.where(edge, more, 0.0)
        for group in range(groups):
            for half in range(pairs):
                for odd in range(2):
                    carry_copy(groups + group, z * lanes + lane_of(half, odd)).start()

    for outer in range(2):
        pack_copies[outer].wait_recv()
        for side in range(2):

            @pl.when(core == (side if outer else 1 - side))
            def _():
                add_rows(side)

    for side in range(2):
        unpack(side)

    def entered_values(step, _):
        for k in range(2):
            column_values(step * 2 + k)
        return 0

    def column_values(column):
        here = pl.ds(pl.multiple_of(column * COL, COL), COL)
        shifted = pl.ds(pl.multiple_of(column * COL + COL, COL), COL)

        def emit_all(ahead, behind, forward, backward, cross, emit):
            behinds = [behind]
            for _ in range(times - 1):
                behinds.append(behinds[-1] * backward)
            for j in range(times):
                emit(j, ahead + cross * behinds[times - 1 - j], behinds[times - 1 - j] - cross * ahead)
                if j < times - 1:
                    ahead = ahead * forward

        for z in range(2):

            def emit(j, state, adjoint):
                first[0, j, tiles[z], here] = state
                first[1, j, tiles[z], here] = adjoint
                twist[0, j, tiles[z], shifted] = turn(state, 64, 1)
                twist[1, j, tiles[z], shifted] = turn(adjoint, 64, 1)

            own = slice(8 + z * 8, 16 + z * 8)
            emit_all(
                entered[0, own, here],
                entered[1, own, here],
                solve[1, tiles[z], here],
                solve[2, tiles[z], here],
                solve[4, tiles[z], here],
                emit,
            )
        for side in range(2):

            def emit(j, state, adjoint):
                edge_in[side, j : j + 1, here] = state
                edge_in[side, times + j : times + j + 1, here] = adjoint

            line = slice(7 + 17 * side, 8 + 17 * side)
            forward = edge_in[side, 2 * times : 2 * times + 1, here]
            cross = edge_in[side, 2 * times + 1 : 2 * times + 2, here]
            emit_all(
                entered[0, line, here],
                entered[1, line, here],
                forward,
                forward * (ratio * ratio),
                cross,
                emit,
            )

    lax.fori_loop(0, columns // 2, entered_values, 0)
    def give_copy(column):
        part = pl.ds(pl.multiple_of(column * COL, COL), COL)
        return pltpu.make_async_remote_copy(
            src_ref=result.at[:, pair_times, :, part],
            dst_ref=given.at[:, :, :, part],
            send_sem=give_send,
            recv_sem=give_recv,
            device_id=pair,
        )

    def second_values(step, _):
        for k in range(2):
            column = step * 2 + k
            here = pl.ds(pl.multiple_of(column * COL, COL), COL)
            for z in range(2):

                def emit(j, state, adjoint):
                    result[0, j, tiles[z], here] = state
                    result[1, j, tiles[z], here] = adjoint

                solved(0, column, z, False, zero, zero, emit)
        for k in range(2):
            give_copy(step * 2 + k).start()
        return 0

    for group in range(groups):
        couplings(group, False)
        lax.fori_loop(group * lanes // 2, (group + 1) * lanes // 2, second_values, 0)
        if group == groups // 2 - 1:
            for other_group in range(groups):
                exchange(1, other_group)

    def twin_entry_copy(group):
        return pltpu.make_async_remote_copy(
            src_ref=entry_in.at[groups + group],
            dst_ref=twin_entry.at[group],
            send_sem=twin_entry_send,
            recv_sem=twin_entry_recv,
            device_id=pair,
        )

    for group in range(groups):
        for kind in range(classes):
            await_entry(groups + group, kind)
        twin_entry_copy(group).start()

    def finish(first_line, entered_at, base_at, cross_at, value_at):
        def finish_columns(step, _):
            for k in range(2):
                column = step * 2 + k
                here = pl.ds(pl.multiple_of(column * COL, COL), COL)
                group, lane = column // lanes, column % lanes
                for z in range(2):
                    there = pl.ds(pl.multiple_of(first_line + z * 8, 8), 8)
                    forward = base_at(tiles[z], here)
                    backward = forward * (ratio * ratio)
                    cross = cross_at(tiles[z], here)
                    forward_half, backward_half = forward, backward
                    for _ in range(half_times.bit_length() - 1):
                        forward_half = forward_half * forward_half
                        backward_half = backward_half * backward_half
                    ahead = entered_at(group, z * lanes + lane, 0)
                    ahead = jnp.where(core == 1, forward_half * ahead, ahead)
                    behind = entered_at(group, z * lanes + lane, 1)
                    behind = jnp.where(core == 1, behind, backward_half * behind)
                    behinds = []
                    for _ in range(half_times):
                        behind = backward * behind
                        behinds.append(behind)
                    for j in range(half_times):
                        ahead = forward * ahead
                        behind = behinds[half_times - 1 - j]
                        both_out[0, j, there, here] = value_at(0, j, tiles[z], here) + (ahead + cross * behind)
                        both_out[1, j, there, here] = value_at(1, j, tiles[z], here) + (behind - cross * ahead)
            return 0

        lax.fori_loop(0, columns // 2, finish_columns, 0)

    def drain(ref, semaphore):
        pltpu.make_async_copy(ref, ref, semaphore).wait()

    finish(
        core * 16,
        lambda group, block, index: entry_in[groups + group, block, index],
        lambda there, here: solve[1, there, here],
        lambda there, here: solve[4, there, here],
        lambda field, j, there, here: result[field, core * half_times + j, there, here],
    )
    drain(twin, twin_recv)
    drain(given, give_recv)
    drain(twin_entry, twin_entry_recv)
    finish(
        16 - core * 16,
        lambda group, block, index: twin_entry[group, block, index],
        lambda there, here: twin[0, there, here],
        lambda there, here: twin[1, there, here],
        lambda field, j, there, here: given[field, j, there, here],
    )

    gain_store.wait()
    gain_give.wait()
    base_copy.wait_send()

    @pl.when(core == 1)
    def _():
        drain(rim.at[pl.ds(0, 2)], kappa_send)

    drain(rhs.at[:, own_times], rhs_send)
    drain(carry_out, carry_send)
    drain(entry_out, entry_send)
    drain(edge_out, edge_send)
    drain(pack_out, pack_send)
    drain(result.at[:, own_times], give_send)
    drain(twin, twin_send)
    drain(twin_entry, twin_entry_send)


def solution(mesh):
    ranks = mesh.shape["tm"]
    slabs = mesh.shape["gz"]
    chips = ranks // 2

    def body(state_rhs, adjoint_rhs, diffusivity, velocity):
        steps, depth, cells = state_rhs.shape
        times = 2 * steps
        columns = cells // COL
        groups = 2 * columns // chips
        f32 = jnp.float32
        dma = pltpu.SemaphoreType.DMA
        anywhere = pl.BlockSpec(memory_space=pl.ANY)
        exchanged = pltpu.VMEM((2 * groups, chips, 2, 8, COL), f32)
        call = pl.pallas_call(
            functools.partial(kernel, chips, slabs, cells, times),
            out_shape=[
                pltpu.VMEM((2, steps, depth, cells), f32),
                pltpu.VMEM((depth, cells), f32),
            ],
            in_specs=[anywhere] * 4,
            out_specs=[pl.BlockSpec(memory_space=pltpu.VMEM), anywhere],
            scratch_shapes=[
                pltpu.VMEM((2, times, 16, cells), f32),
                pltpu.VMEM((2, times, 16, cells), f32),
                pltpu.VMEM((2, times, 16, cells + 2 * COL), f32),
                pltpu.VMEM((2, times, 16, cells), f32),
                pltpu.VMEM((32, cells), f32),
                pltpu.VMEM((8, cells), f32),
                pltpu.VMEM((3, 8, cells // 8), f32),
                pltpu.VMEM((3, 16, cells), f32),
                pltpu.VMEM((2, 3, 2, 16, cells), f32),
                pltpu.VMEM((6, 16, cells), f32),
                pltpu.VMEM((groups, chips, 2, 8, COL), f32),
                pltpu.VMEM((groups, 2, 8, COL), f32),
                pltpu.VMEM((groups, chips + 1, 2, 8, COL), f32),
                exchanged,
                exchanged,
                exchanged,
                exchanged,
                pltpu.VMEM((2, 3 * times, cells), f32),
                pltpu.VMEM((2, 3 * times, cells), f32),
                pltpu.VMEM((6, 4, 16, cells), f32),
                pltpu.VMEM((2, 32, cells), f32),
                pltpu.VMEM((2, 2, columns, COL), f32),
                pltpu.VMEM((2, 2, columns, COL), f32),
                pltpu.VMEM((2, 16, cells), f32),
                pltpu.VMEM((2, steps, 16, cells), f32),
                pltpu.VMEM((groups, chips, 2, 8, COL), f32),
                dma((4,)),
                dma,
                dma((groups,)),
                dma,
                dma,
                dma((2,)),
                dma((2,)),
                dma,
                dma((2 * groups,)),
                dma,
                dma((2 * groups, 2)),
                dma,
                dma((2 * groups,)),
                dma,
                dma((2,)),
                dma,
                dma,
                dma,
                dma,
                dma,
                dma,
            ],
            compiler_params=pltpu.CompilerParams(
                collective_id=0, has_side_effects=True, vmem_limit_bytes=48 * 1024 * 1024
            ),
            cost_estimate=pl.CostEstimate(
                flops=60 * state_rhs.size, bytes_accessed=20 * state_rhs.size, transcendentals=0
            ),
        )
        held = [
            pltpu.with_memory_space_constraint(array, pltpu.HBM)
            for array in (state_rhs, adjoint_rhs, diffusivity, velocity)
        ]
        both, gain = call(*held)
        return both[0] * gain, both[1] * gain

    placed = (P("tm", "gz", None), P("tm", "gz", None), P("gz", None), P(None, "gz", None))
    return jax.shard_map(
        body,
        mesh=mesh,
        in_specs=placed,
        out_specs=(P("tm", "gz", None), P("tm", "gz", None)),
        check_vma=False,
    )
```

```python
import functools
import math

import jax
import jax.numpy as jnp
from jax import lax
from jax.experimental import pallas as pl
from jax.experimental.pallas import tpu as pltpu
from jax.sharding import PartitionSpec as P

NY = 64
COL = 128
ALPHA = 0.1
HALF = 0.5


def turn(value, shift, axis):
    return pltpu.roll(value, (-shift) % value.shape[axis], axis)


def kernel(
    chips, slabs, cells, times,
    state_hbm, adjoint_hbm, kappa_hbm, speed_hbm,
    both_out, gain_out,
    rhs, first, twist, result, kappa, edge_row, rim, speed, couple, solve, power, base, growth,
    carry_out, carry_in, entry_out, entry_in, edge_out, edge_in,
    response, entered, pack_out, pack_in, twin, given, twin_entry,
    load_sem, rhs_send, rhs_recv, kappa_send, kappa_recv, gain_sem, base_sem,
    carry_send, carry_recv, entry_send, entry_recv,
    edge_send, edge_recv, pack_send, pack_recv, twin_send, twin_recv, twin_entry_send, twin_entry_recv, give_send, give_recv,
):
    half_times = times // 2
    lanes = chips // 2
    columns = cells // COL
    groups = columns // lanes
    width = lanes * COL
    total = chips * times
    ratio = ALPHA ** (1.0 / total)

    me = lax.axis_index("tm")
    slab = lax.axis_index("gz")
    chip = me // 2
    core = me % 2
    pair = {"tm": chip * 2 + 1 - core, "gz": slab}
    beside = {"tm": chip * 2 + 1 - core, "gz": (slab + slabs + 2 * core - 1) % slabs}

    behind_same = {"tm": me, "gz": (slab + slabs - 1) % slabs}

    def peer(other):
        return {"tm": other * 2 + 1 - core, "gz": slab}

    rows = pl.ds(pl.multiple_of(core * 16, 16), 16)
    rows_pair = pl.ds(pl.multiple_of(16 - core * 16, 16), 16)
    own_times = pl.ds(core * half_times, half_times)
    pair_times = pl.ds((1 - core) * half_times, half_times)

    def lane_of(half, odd):
        if lanes != 8:
            return (chip + 2 * half + odd) % lanes
        outer = half % 3 == 0
        if isinstance(half, int):
            move_x = 2 - 2 * (half // 3) if outer else 1 + 2 * odd
            move_y = odd if outer else half - 1
        else:
            move_x = jnp.where(outer, 2 - 2 * (half // 3), 1 + 2 * odd)
            move_y = jnp.where(outer, odd, half - 1)
        return ((chip // 4 + move_y) % 2) * 4 + (chip % 4 + move_x) % 4

    pairs = lanes // 2
    classes = (pairs + 1) // 2

    def tile8(start):
        return pl.ds(pl.multiple_of(start, 8), 8)

    barrier = pltpu.get_barrier_semaphore()
    for half in range(lanes // 2):
        for odd in range(2):
            for z in range(2):
                target = peer(z * lanes + lane_of(half, odd))
                pl.semaphore_signal(barrier, inc=1, device_id=target)
    pl.semaphore_signal(barrier, inc=1, device_id=beside)

    @pl.when(core == 1)
    def _():
        pl.semaphore_signal(barrier, inc=1, device_id={"tm": me, "gz": (slab + 1) % slabs})

    loads = [
        pltpu.make_async_copy(kappa_hbm.at[rows], kappa.at[pl.ds(8, 16)], load_sem.at[0]),
        pltpu.make_async_copy(
            kappa_hbm.at[tile8(16 - 8 * core)], kappa.at[tile8(24 - 24 * core)], load_sem.at[0]
        ),
        pltpu.make_async_copy(kappa_hbm.at[pl.ds(0, 8)], edge_row, load_sem.at[0]),
        pltpu.make_async_copy(speed_hbm.at[:, rows], speed, load_sem.at[1]),
        pltpu.make_async_copy(state_hbm.at[:, rows], rhs.at[0, own_times], load_sem.at[2]),
        pltpu.make_async_copy(adjoint_hbm.at[:, rows], rhs.at[1, own_times], load_sem.at[2]),
    ]
    for load in loads:
        load.start()

    def kappa_copy(side):
        return pltpu.make_async_remote_copy(
            src_ref=rim.at[side],
            dst_ref=rim.at[2],
            send_sem=kappa_send,
            recv_sem=kappa_recv,
            device_id=beside if side else behind_same,
        )

    def rhs_copies(group):
        part = slice(group * width, group * width + width)
        return [
            pltpu.make_async_remote_copy(
                src_ref=source.at[:, rows_pair, part],
                dst_ref=rhs.at[field, own_times, :, part],
                send_sem=rhs_send,
                recv_sem=rhs_recv.at[group],
                device_id=pair,
            )
            for field, source in enumerate((state_hbm, adjoint_hbm))
        ]

    lane = lax.broadcasted_iota(jnp.int32, (8, COL), 1)
    row = lax.broadcasted_iota(jnp.int32, (8, COL), 0)
    left = lane < 64
    first_row = row == 0
    last_row = row == 7

    zero = jnp.zeros((8, COL), jnp.float32)
    for field in range(2):
        for step in range(times):
            for z in range(2):
                twist[field, step, z * 8 : z * 8 + 8, :COL] = zero
                twist[field, step, z * 8 : z * 8 + 8, cells + COL :] = zero

    pltpu.make_async_copy(kappa.at[pl.ds(0, 32)], kappa.at[pl.ds(0, 32)], load_sem.at[0]).wait()
    piece_width = cells // 8

    @pl.when(core == 1)
    def _():
        for side, source, line in ((0, edge_row, 0), (1, kappa, 23)):
            for piece in range(8):
                part = slice(piece * piece_width, piece * piece_width + piece_width)
                rim[side, piece : piece + 1, :] = source[line : line + 1, part]

    loads[3].wait()

    def coefficients(k, z):
        there = pl.ds(pl.multiple_of(z * 8, 8), 8)
        centre = pl.ds(pl.multiple_of(8 + z * 8, 8), 8)
        below = pl.ds(pl.multiple_of(z * 8, 8), 8)
        above = pl.ds(pl.multiple_of(16 + z * 8, 8), 8)
        lane0 = pl.multiple_of(k * COL, COL)
        here = pl.ds(lane0, COL)
        before = pl.ds(pl.multiple_of(((k + cells // COL - 1) % (cells // COL)) * COL, COL), COL)
        after = pl.ds(pl.multiple_of(((k + 1) % (cells // COL)) * COL, COL), COL)
        x_place = k * 2 + lane // NY
        y_place = lane % NY
        z_place = slab * 32 + core * 16 + z * 8 + row
        own = kappa[centre, here]
        turned = turn(own, 64, 1)
        x_ahead = jnp.where(left, turned, turn(kappa[centre, after], 64, 1))
        x_behind = jnp.where(left, turn(kappa[centre, before], 64, 1), turned)
        z_ahead = jnp.where(
            last_row, turn(kappa[above, here], 1, 0), turn(own, 1, 0)
        )
        z_behind = jnp.where(
            first_row, turn(kappa[below, here], -1, 0), turn(own, -1, 0)
        )
        diagonal = jnp.zeros((8, COL), jnp.float32)
        for direction, (ahead, behind, place, count, component) in enumerate(
            (
                (z_ahead, z_behind, z_place, slabs * 32, 2),
                (x_ahead, x_behind, x_place, cells // NY, 0),
                (turn(own, 1, 1), turn(own, -1, 1), y_place, NY, 1),
            )
        ):
            has_ahead = place < count - 1
            has_behind = place > 0
            face_ahead = jnp.where(has_ahead, 0.5 * (own + ahead), own)
            face_behind = jnp.where(has_behind, 0.5 * (own + behind), own)
            diagonal = diagonal + face_ahead + face_behind
            drift = 0.5 * speed[component, there, here]
            couple[0, direction, 0, there, here] = jnp.where(has_ahead, face_ahead - drift, 0.0)
            couple[0, direction, 1, there, here] = jnp.where(has_behind, face_behind + drift, 0.0)
            couple[1, direction, 0, there, here] = jnp.where(has_ahead, face_ahead + drift, 0.0)
            couple[1, direction, 1, there, here] = jnp.where(has_behind, face_behind - drift, 0.0)
        large = 1.0 + diagonal
        over = 1.0 / (large * ratio)
        minus = ((large - ratio) * (large - ratio) + HALF * HALF) * over
        plus = minus + 4.0
        root = 2.0 / (minus + 2.0 + jnp.sqrt(minus * plus))
        lead = large - ratio * root
        gain = root * over / (1.0 - root * root)
        solve[0, there, here] = lead
        solve[1, there, here] = root * (1.0 / ratio)
        solve[2, there, here] = root * ratio
        solve[3, there, here] = gain
        solve[4, there, here] = HALF / lead
        solve[5, there, here] = ratio * (1.0 - root * root) / root
        for index, base in ((0, root * (1.0 / ratio)), (1, root * ratio)):
            square = base * base
            fourth = square * square
            power[k // lanes, z * lanes + k % lanes, index] = fourth * fourth

    def inner_coefficients(step, _):
        for k in range(4):
            coefficients(step * 4 + k, 1 - core)
        return 0

    def outer_coefficients(step, _):
        for k in range(4):
            coefficients(step * 4 + k, core)
        return 0

    pl.semaphore_wait(barrier, chips + 1 + core)

    @pl.when(core == 1)
    def _():
        for side in range(2):
            kappa_copy(side).start()

    for group in range(groups):
        for copy in rhs_copies(group):
            copy.start()

    lax.fori_loop(0, cells // COL // 4, inner_coefficients, 0)
    pltpu.make_async_copy(rhs.at[:, own_times], rhs.at[:, own_times], load_sem.at[2]).wait()
    kappa_copy(1).wait_recv()
    for side in range(2):

        @pl.when(core == side)
        def _():
            for piece in range(8):
                part = slice(piece * piece_width, piece * piece_width + piece_width)
                kappa[7 + 17 * side : 8 + 17 * side, part] = rim[2, piece : piece + 1, :]

    lax.fori_loop(0, cells // COL // 4, outer_coefficients, 0)

    def carry_copy(lot, other):
        return pltpu.make_async_remote_copy(
            src_ref=carry_out.at[lot, other],
            dst_ref=carry_in.at[lot, chip],
            send_sem=carry_send,
            recv_sem=carry_recv.at[lot],
            device_id=peer(other),
        )

    def entry_copy(lot, other, kind):
        return pltpu.make_async_remote_copy(
            src_ref=entry_out.at[lot, other],
            dst_ref=entry_in.at[lot, chip],
            send_sem=entry_send,
            recv_sem=entry_recv.at[lot, kind],
            device_id=peer(other),
        )

    def await_entry(lot, kind):
        blocks = entry_in.at[lot, pl.ds(0, chips // classes)]
        pltpu.make_async_copy(blocks, blocks, entry_recv.at[lot, kind]).wait()

    def powers(group):
        for direction in range(2):
            factor = base[group, direction]
            run = factor
            for step in range(1, chips + 1):
                growth[group, step, direction] = run
                run = run * factor

    def exchange(sweep, group):
        lot = sweep * groups + group

        arrived = carry_in.at[lot]
        pltpu.make_async_copy(arrived, arrived, carry_recv.at[lot]).wait()
        for direction, wrap in ((0, ALPHA), (1, 1.0 / ALPHA)):
            factor = growth[group, 1, direction]
            order = range(chips) if direction == 0 else range(chips - 1, -1, -1)
            run = None
            before = []
            for place in order:
                before.append(run)
                carry = carry_in[lot, place, direction]
                run = carry if run is None else carry + factor * run
            start = wrap * (run / (1.0 - wrap * growth[group, chips, direction]))
            for step, place in enumerate(order):
                value = start
                if step:
                    value = before[step] + start * growth[group, step, direction]
                entry_out[lot, place, direction] = value
        for half in range(pairs):
            for odd in range(2):
                for z in range(2):
                    other = z * lanes + lane_of(half, odd)
                    entry_copy(lot, other, half // 2).start()

    def sums(values, forward, backward):
        ahead = values[0]
        behind = values[-1]
        for step in range(1, times):
            ahead = values[step] + forward * ahead
            behind = values[times - 1 - step] + backward * behind
        return ahead, behind

    base_copy = pltpu.make_async_remote_copy(
        src_ref=power.at[:, chip],
        dst_ref=base,
        send_sem=base_sem.at[0],
        recv_sem=base_sem.at[1],
        device_id=pair,
    )
    base_copy.start()
    gain_store = pltpu.make_async_copy(solve.at[3], gain_out.at[rows], load_sem.at[3])
    gain_give = pltpu.make_async_remote_copy(
        src_ref=solve.at[3],
        dst_ref=gain_out.at[rows],
        send_sem=gain_sem.at[0],
        recv_sem=gain_sem.at[1],
        device_id=pair,
    )

    twin_copies = [
        pltpu.make_async_remote_copy(
            src_ref=solve.at[source],
            dst_ref=twin.at[target],
            send_sem=twin_send,
            recv_sem=twin_recv,
            device_id=pair,
        )
        for target, source in enumerate((1, 4))
    ]

    def first_sums(group):
        def pair_sums(half, _):
            for odd in range(2):
                lane = lane_of(half, odd)
                here = pl.ds(pl.multiple_of(group * width + lane * COL, COL), COL)
                for z in range(2):
                    there = slice(z * 8, z * 8 + 8)
                    lead = solve[0, there, here]
                    forward = solve[1, there, here]
                    backward = solve[2, there, here]
                    sides = [
                        sums([rhs[field, j, there, here] for j in range(times)], forward, backward)
                        for field in range(2)
                    ]
                    block = z * lanes + lane
                    carry_out[group, block, 0] = lead * sides[0][0] + HALF * sides[1][0]
                    carry_out[group, block, 1] = lead * sides[1][1] - HALF * sides[0][1]
            for odd in range(2):
                for z in range(2):
                    carry_copy(group, z * lanes + lane_of(half, odd)).start()
            return 0

        lax.fori_loop(0, pairs, pair_sums, 0)

    for group in range(groups):
        arrived = rhs.at[:, own_times, :, slice(0, width)]
        pltpu.make_async_copy(arrived, arrived, rhs_recv.at[group]).wait()
        first_sums(group)
    gain_store.start()
    gain_give.start()
    for copy in twin_copies:
        copy.start()
    base_copy.wait_recv()
    for group in range(groups):
        powers(group)
    def solved(group, lane, z, scaled, ahead, back, emit):
        here = pl.ds(pl.multiple_of(group * width + lane * COL, COL), COL)
        there = slice(z * 8, z * 8 + 8)
        lead = solve[0, there, here]
        forward = solve[1, there, here]
        backward = solve[2, there, here]
        gain = solve[3, there, here]
        cross = solve[4, there, here]
        plain = solve[5, there, here]
        backs = [None] * times
        for j in reversed(range(times)):
            backs[j] = backward * back
            back = (
                lead * rhs[1, j, there, here] - HALF * rhs[0, j, there, here] + backs[j]
            )
        for j in range(times):
            adjoint = rhs[1, j, there, here]
            ahead = lead * rhs[0, j, there, here] + HALF * adjoint + forward * ahead
            state = ahead + cross * backs[j]
            adjoint = backs[j] - cross * ahead + plain * adjoint
            if scaled:
                state, adjoint = gain * state, gain * adjoint
            emit(j, state, adjoint)

    def edge_copies(column, mark):
        part = pl.ds(pl.multiple_of(column * COL, COL), COL)
        return (
            pltpu.make_async_remote_copy(
                src_ref=edge_out.at[core, :, part],
                dst_ref=edge_in.at[1 - core, :, part],
                send_sem=edge_send,
                recv_sem=edge_recv.at[mark],
                device_id=beside,
            ),
            pltpu.make_async_remote_copy(
                src_ref=edge_out.at[1 - core, :, part],
                dst_ref=edge_in.at[core, :, part],
                send_sem=edge_send,
                recv_sem=edge_recv.at[mark],
                device_id=pair,
            ),
        )

    def first_values(group):
        def pair_values(step, _):
            half = pairs - 1 - step
            for odd in (1, 0):
                lane = lane_of(half, odd)
                column = group * lanes + lane
                here = pl.ds(pl.multiple_of(column * COL, COL), COL)
                shifted = pl.ds(pl.multiple_of(column * COL + COL, COL), COL)
                for z in range(2):

                    def emit(j, state, adjoint):
                        first[0, j, z * 8 : z * 8 + 8, here] = state
                        first[1, j, z * 8 : z * 8 + 8, here] = adjoint
                        twist[0, j, z * 8 : z * 8 + 8, shifted] = turn(state, 64, 1)
                        twist[1, j, z * 8 : z * 8 + 8, shifted] = turn(adjoint, 64, 1)
                        edge = slice(7 * z, 7 * z + 1)
                        edge_out[z, j : j + 1, here] = state[edge]
                        edge_out[z, times + j : times + j + 1, here] = adjoint[edge]

                    solved(group, lane, z, True, zero, zero, emit)
                    line = z * 15
                    edge_out[z, 2 * times : 2 * times + 1, here] = solve[1, line : line + 1, here]
                    edge_out[z, 2 * times + 1 : 2 * times + 2, here] = solve[4, line : line + 1, here]
            for odd in (1, 0):
                for copy in edge_copies(group * lanes + lane_of(half, odd), group * classes + half // 2):
                    copy.start()
            return 0

        lax.fori_loop(0, pairs, pair_values, 0)

    for group in range(groups):
        first_values(group)

    for group in range(groups):
        exchange(0, group)

    tiles = (slice(0, 8), slice(8, 16))

    def column_of(column):
        return pl.ds(pl.multiple_of((column % columns) * COL, COL), COL)

    def in_z(own, below, above):
        up = [turn(value, 1, 0) for value in own]
        down = [turn(value, -1, 0) for value in own]
        return (
            [jnp.where(last_row, up[1], up[0]), jnp.where(last_row, above, up[1])],
            [jnp.where(first_row, below, down[0]), jnp.where(first_row, down[0], down[1])],
        )

    def in_plane(own, before, after):
        turned = turn(own, 64, 1)
        return (
            jnp.where(left, turned, turn(after, 64, 1)),
            jnp.where(left, turn(before, 64, 1), turned),
            turn(own, 1, 1),
            turn(own, -1, 1),
        )

    def edge_rows(line, here):
        return [jnp.broadcast_to(edge_in[side, line : line + 1, here], (8, COL)) for side in range(2)]

    def make_responses(column):
        here, before, after = column_of(column), column_of(column + columns - 1), column_of(column + 1)
        sides = []
        for index, line in ((1, 2 * times), (4, 2 * times + 1)):
            own = [solve[index, there, here] for there in tiles]
            z_ahead, z_behind = in_z(own, *edge_rows(line, here))
            sides.append(
                [
                    (z_ahead[z], z_behind[z])
                    + in_plane(own[z], solve[index, tiles[z], before], solve[index, tiles[z], after])
                    for z in range(2)
                ]
            )
        square_ratio = ratio * ratio
        for z in range(2):
            there = tiles[z]
            lead = solve[0, there, here]
            base_own = solve[1, there, here]
            square_own = base_own * base_own
            fourth_own = square_own * square_own
            for place in range(6):
                base_near, cross_near = sides[0][z][place], sides[1][z][place]
                square_near = base_near * base_near
                mixed = (base_own + base_near) * (square_own + square_near)
                mixed = mixed * (fourth_own + square_near * square_near)
                product = square_ratio * (base_own * base_near)
                square = product * product
                series = (1.0 + product) * (1.0 + square) * (1.0 + square * square)
                to_state = couple[0, place // 2, place % 2, there, here]
                to_adjoint = couple[1, place // 2, place % 2, there, here]
                state_lead, state_half = lead * to_state, HALF * to_state
                adjoint_lead, adjoint_half = lead * to_adjoint, HALF * to_adjoint
                response[place, 0, there, here] = mixed * (state_lead - cross_near * adjoint_half)
                response[place, 1, there, here] = series * (cross_near * state_lead + adjoint_half)
                response[place, 2, there, here] = -series * (state_half + cross_near * adjoint_lead)
                response[place, 3, there, here] = (square_ratio**7 * mixed) * (
                    adjoint_lead - cross_near * state_half
                )

    def couplings(group, summed):
        def pair_couplings(step, _):
            half = pairs - 1 - step
            if summed:

                @pl.when(step % 2 == 0)
                def _():
                    arrived = edge_in.at[:, :, pl.ds(0, 2 * pairs // classes * COL)]
                    sem = edge_recv.at[group * classes + half // 2]
                    pltpu.make_async_copy(arrived, arrived, sem).wait()

            for odd in (1, 0):
                lane = lane_of(half, odd)
                column = group * lanes + lane
                lane0 = column * COL
                here = pl.ds(pl.multiple_of(lane0, COL), COL)
                shifted = pl.ds(pl.multiple_of(lane0 + COL, COL), COL)
                after = pl.ds(pl.multiple_of(lane0 + 2 * COL, COL), COL)
                forward = [solve[1, there, here] for there in tiles]
                backward = [solve[2, there, here] for there in tiles]
                sides = []
                for field in range(2):
                    weights = [
                        [couple[field, d, s, there, here] for there in tiles]
                        for d in range(3)
                        for s in range(2)
                    ]
                    ahead_sum = [zero, zero]
                    behind_sum = [zero, zero]
                    scale = [jnp.ones((8, COL), jnp.float32)] * 2
                    for j in range(times):
                        own = [first[field, j, there, here] for there in tiles]
                        z_ahead, z_behind = in_z(own, *edge_rows(field * times + j, here))
                        for z in range(2):
                            there = tiles[z]
                            turned = twist[field, j, there, shifted]
                            x_ahead = jnp.where(left, turned, twist[field, j, there, after])
                            x_behind = jnp.where(left, twist[field, j, there, here], turned)
                            value = (
                                rhs[field, j, there, here]
                                + weights[0][z] * z_ahead[z]
                                + weights[1][z] * z_behind[z]
                                + weights[2][z] * x_ahead
                                + weights[3][z] * x_behind
                                + weights[4][z] * turn(own[z], 1, 1)
                                + weights[5][z] * turn(own[z], -1, 1)
                            )
                            rhs[field, j, there, here] = value
                            if summed:
                                ahead_sum[z] = value + forward[z] * ahead_sum[z]
                                behind_sum[z] = behind_sum[z] + scale[z] * value
                                if j < times - 1:
                                    scale[z] = scale[z] * backward[z]
                    sides.append((ahead_sum, behind_sum))
                if summed:
                    make_responses(column)
                    for z in range(2):
                        lead = solve[0, tiles[z], here]
                        block = z * lanes + lane
                        lot = groups + group
                        carry_out[lot, block, 0] = lead * sides[0][0][z] + HALF * sides[1][0][z]
                        carry_out[lot, block, 1] = lead * sides[1][1][z] - HALF * sides[0][1][z]
            return 0

        lax.fori_loop(0, pairs, pair_couplings, 0)

    for group in range(groups):
        couplings(group, True)

    def entries(group):
        def pair_entries(step, _):
            half = pairs - 1 - step

            for odd in (1, 0):
                lane = lane_of(half, odd)
                here = pl.ds(pl.multiple_of((group * lanes + lane) * COL, COL), COL)
                for z in range(2):
                    gain = solve[3, tiles[z], here]
                    for index in range(2):
                        entered[index, 8 + z * 8 : 16 + z * 8, here] = (
                            gain * solve[1 + index, tiles[z], here] * entry_in[group, z * lanes + lane, index]
                        )
            return 0

        lax.fori_loop(0, pairs, pair_entries, 0)

    for group in range(groups):
        for kind in range(classes):
            await_entry(group, kind)
        for lane in range(lanes):
            column = group * lanes + lane
            here = slice(column * COL, column * COL + COL)
            for side in range(2):
                line, edge, block = slice(15 * side, 15 * side + 1), slice(7 * side, 7 * side + 1), side * lanes + lane
                gain = solve[3, line, here]
                for index in range(2):
                    pack_out[side, index, column : column + 1, :] = (
                        gain * solve[1 + index, line, here] * entry_in[group, block, index, edge]
                    )
    pack_copies = [
        pltpu.make_async_remote_copy(
            src_ref=pack_out.at[1 - core],
            dst_ref=pack_in.at[core],
            send_sem=pack_send,
            recv_sem=pack_recv.at[0],
            device_id=pair,
        ),
        pltpu.make_async_remote_copy(
            src_ref=pack_out.at[core],
            dst_ref=pack_in.at[1 - core],
            send_sem=pack_send,
            recv_sem=pack_recv.at[1],
            device_id=beside,
        ),
    ]
    for copy in pack_copies:
        copy.start()
    for group in range(groups):
        entries(group)

    def unpack(side):
        for index in range(2):
            for column in range(columns):
                part = slice(column * COL, column * COL + COL)
                line = 7 + 17 * side
                entered[index, line : line + 1, part] = pack_in[side, index, column : column + 1, :]

    def second_sums(step, _):
        for k in range(4):
            column = step * 4 + k
            here, before, after = column_of(column), column_of(column + columns - 1), column_of(column + 1)
            lot = groups + column // lanes
            sides = [[], []]
            for index in range(2):
                own = [entered[index, 8 + z * 8 : 16 + z * 8, here] for z in range(2)]
                z_ahead, z_behind = in_z(own, zero, zero)
                for z in range(2):
                    centre = slice(8 + z * 8, 16 + z * 8)
                    sides[z].append(
                        (z_ahead[z], z_behind[z])
                        + in_plane(own[z], entered[index, centre, before], entered[index, centre, after])
                    )
            for z in range(2):
                block = z * lanes + column % lanes
                for direction in range(2):
                    total_sum = carry_out[lot, block, direction]
                    for place in range(6):
                        for index in range(2):
                            factor = response[place, 2 * direction + index, tiles[z], here]
                            total_sum = total_sum + factor * sides[z][index][place]
                    carry_out[lot, block, direction] = total_sum
        return 0

    lax.fori_loop(0, columns // 4, second_sums, 0)

    def add_rows(side):
        z, place, edge = side, 1 - side, (last_row if side else first_row)
        for column in range(columns):
            here = slice(column * COL, column * COL + COL)
            lot, block = groups + column // lanes, z * lanes + column % lanes
            enter = [
                jnp.broadcast_to(pack_in[side, index, column : column + 1, :], (8, COL)) for index in range(2)
            ]
            for direction in range(2):
                more = (
                    response[place, 2 * direction, tiles[z], here] * enter[0]
                    + response[place, 2 * direction + 1, tiles[z], here] * enter[1]
                )
                carry_out[lot, block, direction] = carry_out[lot, block, direction] + jnp.where(edge, more, 0.0)
        for group in range(groups):
            for half in range(pairs):
                for odd in range(2):
                    carry_copy(groups + group, z * lanes + lane_of(half, odd)).start()

    for outer in range(2):
        pack_copies[outer].wait_recv()
        for side in range(2):

            @pl.when(core == (side if outer else 1 - side))
            def _():
                add_rows(side)

    for side in range(2):
        unpack(side)

    def entered_values(step, _):
        for k in range(2):
            column_values(step * 2 + k)
        return 0

    def column_values(column):
        here = pl.ds(pl.multiple_of(column * COL, COL), COL)
        shifted = pl.ds(pl.multiple_of(column * COL + COL, COL), COL)

        def emit_all(ahead, behind, forward, backward, cross, emit):
            behinds = [behind]
            for _ in range(times - 1):
                behinds.append(behinds[-1] * backward)
            for j in range(times):
                emit(j, ahead + cross * behinds[times - 1 - j], behinds[times - 1 - j] - cross * ahead)
                if j < times - 1:
                    ahead = ahead * forward

        for z in range(2):

            def emit(j, state, adjoint):
                first[0, j, tiles[z], here] = state
                first[1, j, tiles[z], here] = adjoint
                twist[0, j, tiles[z], shifted] = turn(state, 64, 1)
                twist[1, j, tiles[z], shifted] = turn(adjoint, 64, 1)

            own = slice(8 + z * 8, 16 + z * 8)
            emit_all(
                entered[0, own, here],
                entered[1, own, here],
                solve[1, tiles[z], here],
                solve[2, tiles[z], here],
                solve[4, tiles[z], here],
                emit,
            )
        for side in range(2):

            def emit(j, state, adjoint):
                edge_in[side, j : j + 1, here] = state
                edge_in[side, times + j : times + j + 1, here] = adjoint

            line = slice(7 + 17 * side, 8 + 17 * side)
            forward = edge_in[side, 2 * times : 2 * times + 1, here]
            cross = edge_in[side, 2 * times + 1 : 2 * times + 2, here]
            emit_all(
                entered[0, line, here],
                entered[1, line, here],
                forward,
                forward * (ratio * ratio),
                cross,
                emit,
            )

    lax.fori_loop(0, columns // 2, entered_values, 0)
    def give_copy(column):
        part = pl.ds(pl.multiple_of(column * COL, COL), COL)
        return pltpu.make_async_remote_copy(
            src_ref=result.at[:, pair_times, :, part],
            dst_ref=given.at[:, :, :, part],
            send_sem=give_send,
            recv_sem=give_recv,
            device_id=pair,
        )

    def second_values(step, _):
        for k in range(2):
            column = step * 2 + k
            here = pl.ds(pl.multiple_of(column * COL, COL), COL)
            for z in range(2):

                def emit(j, state, adjoint):
                    result[0, j, tiles[z], here] = state
                    result[1, j, tiles[z], here] = adjoint

                solved(0, column, z, False, zero, zero, emit)
        for k in range(2):
            give_copy(step * 2 + k).start()
        return 0

    for group in range(groups):
        couplings(group, False)
        lax.fori_loop(group * lanes // 2, (group + 1) * lanes // 2, second_values, 0)
        if group == groups // 2 - 1:
            for other_group in range(groups):
                exchange(1, other_group)

    def twin_entry_copy(group):
        return pltpu.make_async_remote_copy(
            src_ref=entry_in.at[groups + group],
            dst_ref=twin_entry.at[group],
            send_sem=twin_entry_send,
            recv_sem=twin_entry_recv.at[group],
            device_id=pair,
        )

    def finish(group, first_line, entered_at, base_at, cross_at, value_at):
        def finish_columns(step, _):
            for k in range(2):
                lane = step * 2 + k
                here = pl.ds(pl.multiple_of((group * lanes + lane) * COL, COL), COL)
                for z in range(2):
                    there = pl.ds(pl.multiple_of(first_line + z * 8, 8), 8)
                    forward = base_at(tiles[z], here)
                    backward = forward * (ratio * ratio)
                    cross = cross_at(tiles[z], here)
                    forward_half, backward_half = forward, backward
                    for _ in range(half_times.bit_length() - 1):
                        forward_half = forward_half * forward_half
                        backward_half = backward_half * backward_half
                    ahead = entered_at(z * lanes + lane, 0)
                    ahead = jnp.where(core == 1, forward_half * ahead, ahead)
                    behind = entered_at(z * lanes + lane, 1)
                    behind = jnp.where(core == 1, behind, backward_half * behind)
                    behinds = []
                    for _ in range(half_times):
                        behind = backward * behind
                        behinds.append(behind)
                    for j in range(half_times):
                        ahead = forward * ahead
                        behind = behinds[half_times - 1 - j]
                        both_out[0, j, there, here] = value_at(0, j, tiles[z], here) + (ahead + cross * behind)
                        both_out[1, j, there, here] = value_at(1, j, tiles[z], here) + (behind - cross * ahead)
            return 0

        lax.fori_loop(0, lanes // 2, finish_columns, 0)

    def drain(ref, semaphore):
        pltpu.make_async_copy(ref, ref, semaphore).wait()

    for group in range(groups):
        for kind in range(classes):
            await_entry(groups + group, kind)
        twin_entry_copy(group).start()
        finish(
            group,
            core * 16,
            lambda block, index: entry_in[groups + group, block, index],
            lambda there, here: solve[1, there, here],
            lambda there, here: solve[4, there, here],
            lambda field, j, there, here: result[field, core * half_times + j, there, here],
        )
    drain(twin, twin_recv)
    drain(given, give_recv)
    for group in range(groups):
        drain(twin_entry.at[group], twin_entry_recv.at[group])
        finish(
            group,
            16 - core * 16,
            lambda block, index: twin_entry[group, block, index],
            lambda there, here: twin[0, there, here],
            lambda there, here: twin[1, there, here],
            lambda field, j, there, here: given[field, j, there, here],
        )

    gain_store.wait()
    gain_give.wait()
    base_copy.wait_send()

    @pl.when(core == 1)
    def _():
        drain(rim.at[pl.ds(0, 2)], kappa_send)

    drain(rhs.at[:, own_times], rhs_send)
    drain(carry_out, carry_send)
    drain(entry_out, entry_send)
    drain(edge_out, edge_send)
    drain(pack_out, pack_send)
    drain(result.at[:, own_times], give_send)
    drain(twin, twin_send)
    drain(twin_entry, twin_entry_send)


def write_kernel(both, gain, state_out, adjoint_out, stage, semaphore):
    for field, target in enumerate((state_out, adjoint_out)):
        for step in range(both.shape[1]):
            stage[field, step] = both[field, step] * gain[...]
            pltpu.make_async_copy(stage.at[field, step], target.at[step], semaphore.at[field]).start()
    for field, target in enumerate((state_out, adjoint_out)):
        pltpu.make_async_copy(stage.at[field], target, semaphore.at[field]).wait()


def solution(mesh):
    ranks = mesh.shape["tm"]
    slabs = mesh.shape["gz"]
    chips = ranks // 2

    def body(state_rhs, adjoint_rhs, diffusivity, velocity):
        steps, depth, cells = state_rhs.shape
        times = 2 * steps
        columns = cells // COL
        groups = 2 * columns // chips
        f32 = jnp.float32
        dma = pltpu.SemaphoreType.DMA
        anywhere = pl.BlockSpec(memory_space=pl.ANY)
        exchanged = pltpu.VMEM((2 * groups, chips, 2, 8, COL), f32)
        call = pl.pallas_call(
            functools.partial(kernel, chips, slabs, cells, times),
            out_shape=[
                pltpu.VMEM((2, steps, depth, cells), f32),
                pltpu.VMEM((depth, cells), f32),
            ],
            in_specs=[anywhere] * 4,
            out_specs=[pl.BlockSpec(memory_space=pltpu.VMEM), anywhere],
            scratch_shapes=[
                pltpu.VMEM((2, times, 16, cells), f32),
                pltpu.VMEM((2, times, 16, cells), f32),
                pltpu.VMEM((2, times, 16, cells + 2 * COL), f32),
                pltpu.VMEM((2, times, 16, cells), f32),
                pltpu.VMEM((32, cells), f32),
                pltpu.VMEM((8, cells), f32),
                pltpu.VMEM((3, 8, cells // 8), f32),
                pltpu.VMEM((3, 16, cells), f32),
                pltpu.VMEM((2, 3, 2, 16, cells), f32),
                pltpu.VMEM((6, 16, cells), f32),
                pltpu.VMEM((groups, chips, 2, 8, COL), f32),
                pltpu.VMEM((groups, 2, 8, COL), f32),
                pltpu.VMEM((groups, chips + 1, 2, 8, COL), f32),
                exchanged,
                exchanged,
                exchanged,
                exchanged,
                pltpu.VMEM((2, 3 * times, cells), f32),
                pltpu.VMEM((2, 3 * times, cells), f32),
                pltpu.VMEM((6, 4, 16, cells), f32),
                pltpu.VMEM((2, 32, cells), f32),
                pltpu.VMEM((2, 2, columns, COL), f32),
                pltpu.VMEM((2, 2, columns, COL), f32),
                pltpu.VMEM((2, 16, cells), f32),
                pltpu.VMEM((2, steps, 16, cells), f32),
                pltpu.VMEM((groups, chips, 2, 8, COL), f32),
                dma((4,)),
                dma,
                dma((groups,)),
                dma,
                dma,
                dma((2,)),
                dma((2,)),
                dma,
                dma((2 * groups,)),
                dma,
                dma((2 * groups, 2)),
                dma,
                dma((2 * groups,)),
                dma,
                dma((2,)),
                dma,
                dma,
                dma,
                dma((groups,)),
                dma,
                dma,
            ],
            compiler_params=pltpu.CompilerParams(
                collective_id=0, has_side_effects=True, vmem_limit_bytes=48 * 1024 * 1024
            ),
            cost_estimate=pl.CostEstimate(
                flops=60 * state_rhs.size, bytes_accessed=20 * state_rhs.size, transcendentals=0
            ),
        )
        held = [
            pltpu.with_memory_space_constraint(array, pltpu.HBM)
            for array in (state_rhs, adjoint_rhs, diffusivity, velocity)
        ]
        both, gain = call(*held)
        write = pl.pallas_call(
            write_kernel,
            out_shape=[jax.ShapeDtypeStruct(state_rhs.shape, f32)] * 2,
            in_specs=[pl.BlockSpec(memory_space=pltpu.VMEM)] * 2,
            out_specs=[anywhere] * 2,
            scratch_shapes=[pltpu.VMEM((2, steps, depth, cells), f32), dma((2,))],
            compiler_params=pltpu.CompilerParams(vmem_limit_bytes=48 * 1024 * 1024),
        )
        placed_inputs = [pltpu.with_memory_space_constraint(array, pltpu.VMEM) for array in (both, gain)]
        return tuple(write(*placed_inputs))

    placed = (P("tm", "gz", None), P("tm", "gz", None), P("gz", None), P(None, "gz", None))
    return jax.shard_map(
        body,
        mesh=mesh,
        in_specs=placed,
        out_specs=(P("tm", "gz", None), P("tm", "gz", None)),
        check_vma=False,
    )
```

```python
import functools
import math

import jax
import jax.numpy as jnp
from jax import lax
from jax.experimental import pallas as pl
from jax.experimental.pallas import tpu as pltpu
from jax.sharding import PartitionSpec as P

NY = 64
COL = 128
ALPHA = 0.1
HALF = 0.5


def turn(value, shift, axis):
    return pltpu.roll(value, (-shift) % value.shape[axis], axis)


def kernel(
    chips, slabs, cells, times,
    state_hbm, adjoint_hbm, kappa_hbm, speed_hbm,
    both_out, gain_out,
    rhs, first, twist, result, kappa, edge_row, rim, speed, couple, solve, power, base, growth,
    carry_out, carry_in, entry_out, entry_in, edge_out, edge_in,
    response, entered, pack_out, pack_in, twin, given, twin_entry,
    load_sem, rhs_send, rhs_recv, kappa_send, kappa_recv, gain_sem, base_sem,
    carry_send, carry_recv, entry_send, entry_recv,
    edge_send, edge_recv, pack_send, pack_recv, twin_send, twin_recv, twin_entry_send, twin_entry_recv, give_send, give_recv,
):
    half_times = times // 2
    lanes = chips // 2
    columns = cells // COL
    groups = columns // lanes
    width = lanes * COL
    total = chips * times
    ratio = ALPHA ** (1.0 / total)

    me = lax.axis_index("tm")
    slab = lax.axis_index("gz")
    chip = me // 2
    core = me % 2
    pair = {"tm": chip * 2 + 1 - core, "gz": slab}
    beside = {"tm": chip * 2 + 1 - core, "gz": (slab + slabs + 2 * core - 1) % slabs}

    behind_same = {"tm": me, "gz": (slab + slabs - 1) % slabs}

    def peer(other):
        return {"tm": other * 2 + 1 - core, "gz": slab}

    rows = pl.ds(pl.multiple_of(core * 16, 16), 16)
    rows_pair = pl.ds(pl.multiple_of(16 - core * 16, 16), 16)
    own_times = pl.ds(core * half_times, half_times)
    pair_times = pl.ds((1 - core) * half_times, half_times)

    def lane_of(half, odd):
        if lanes != 8:
            return (chip + 2 * half + odd) % lanes
        outer = half % 3 == 0
        if isinstance(half, int):
            move_x = 2 - 2 * (half // 3) if outer else 1 + 2 * odd
            move_y = odd if outer else half - 1
        else:
            move_x = jnp.where(outer, 2 - 2 * (half // 3), 1 + 2 * odd)
            move_y = jnp.where(outer, odd, half - 1)
        return ((chip // 4 + move_y) % 2) * 4 + (chip % 4 + move_x) % 4

    pairs = lanes // 2
    classes = (pairs + 1) // 2

    def tile8(start):
        return pl.ds(pl.multiple_of(start, 8), 8)

    barrier = pltpu.get_barrier_semaphore()
    for half in range(lanes // 2):
        for odd in range(2):
            for z in range(2):
                target = peer(z * lanes + lane_of(half, odd))
                pl.semaphore_signal(barrier, inc=1, device_id=target)
    pl.semaphore_signal(barrier, inc=1, device_id=beside)

    @pl.when(core == 1)
    def _():
        pl.semaphore_signal(barrier, inc=1, device_id={"tm": me, "gz": (slab + 1) % slabs})

    loads = [
        pltpu.make_async_copy(kappa_hbm.at[rows], kappa.at[pl.ds(8, 16)], load_sem.at[0]),
        pltpu.make_async_copy(
            kappa_hbm.at[tile8(16 - 8 * core)], kappa.at[tile8(24 - 24 * core)], load_sem.at[0]
        ),
        pltpu.make_async_copy(kappa_hbm.at[pl.ds(0, 8)], edge_row, load_sem.at[0]),
        pltpu.make_async_copy(speed_hbm.at[:, rows], speed, load_sem.at[1]),
        pltpu.make_async_copy(state_hbm.at[:, rows], rhs.at[0, own_times], load_sem.at[2]),
        pltpu.make_async_copy(adjoint_hbm.at[:, rows], rhs.at[1, own_times], load_sem.at[2]),
    ]
    for load in loads:
        load.start()

    def kappa_copy(side):
        return pltpu.make_async_remote_copy(
            src_ref=rim.at[side],
            dst_ref=rim.at[2],
            send_sem=kappa_send,
            recv_sem=kappa_recv,
            device_id=beside if side else behind_same,
        )

    def rhs_copies(group):
        part = slice(group * width, group * width + width)
        return [
            pltpu.make_async_remote_copy(
                src_ref=source.at[:, rows_pair, part],
                dst_ref=rhs.at[field, own_times, :, part],
                send_sem=rhs_send,
                recv_sem=rhs_recv.at[group],
                device_id=pair,
            )
            for field, source in enumerate((state_hbm, adjoint_hbm))
        ]

    lane = lax.broadcasted_iota(jnp.int32, (8, COL), 1)
    row = lax.broadcasted_iota(jnp.int32, (8, COL), 0)
    left = lane < 64
    first_row = row == 0
    last_row = row == 7

    zero = jnp.zeros((8, COL), jnp.float32)
    for field in range(2):
        for step in range(times):
            for z in range(2):
                twist[field, step, z * 8 : z * 8 + 8, :COL] = zero
                twist[field, step, z * 8 : z * 8 + 8, cells + COL :] = zero

    pltpu.make_async_copy(kappa.at[pl.ds(0, 32)], kappa.at[pl.ds(0, 32)], load_sem.at[0]).wait()
    piece_width = cells // 8

    @pl.when(core == 1)
    def _():
        for side, source, line in ((0, edge_row, 0), (1, kappa, 23)):
            for piece in range(8):
                part = slice(piece * piece_width, piece * piece_width + piece_width)
                rim[side, piece : piece + 1, :] = source[line : line + 1, part]

    loads[3].wait()

    def coefficients(k, z):
        there = pl.ds(pl.multiple_of(z * 8, 8), 8)
        centre = pl.ds(pl.multiple_of(8 + z * 8, 8), 8)
        below = pl.ds(pl.multiple_of(z * 8, 8), 8)
        above = pl.ds(pl.multiple_of(16 + z * 8, 8), 8)
        lane0 = pl.multiple_of(k * COL, COL)
        here = pl.ds(lane0, COL)
        before = pl.ds(pl.multiple_of(((k + cells // COL - 1) % (cells // COL)) * COL, COL), COL)
        after = pl.ds(pl.multiple_of(((k + 1) % (cells // COL)) * COL, COL), COL)
        x_place = k * 2 + lane // NY
        y_place = lane % NY
        z_place = slab * 32 + core * 16 + z * 8 + row
        own = kappa[centre, here]
        turned = turn(own, 64, 1)
        x_ahead = jnp.where(left, turned, turn(kappa[centre, after], 64, 1))
        x_behind = jnp.where(left, turn(kappa[centre, before], 64, 1), turned)
        z_ahead = jnp.where(
            last_row, turn(kappa[above, here], 1, 0), turn(own, 1, 0)
        )
        z_behind = jnp.where(
            first_row, turn(kappa[below, here], -1, 0), turn(own, -1, 0)
        )
        diagonal = jnp.zeros((8, COL), jnp.float32)
        for direction, (ahead, behind, place, count, component) in enumerate(
            (
                (z_ahead, z_behind, z_place, slabs * 32, 2),
                (x_ahead, x_behind, x_place, cells // NY, 0),
                (turn(own, 1, 1), turn(own, -1, 1), y_place, NY, 1),
            )
        ):
            has_ahead = place < count - 1
            has_behind = place > 0
            face_ahead = jnp.where(has_ahead, 0.5 * (own + ahead), own)
            face_behind = jnp.where(has_behind, 0.5 * (own + behind), own)
            diagonal = diagonal + face_ahead + face_behind
            drift = 0.5 * speed[component, there, here]
            couple[0, direction, 0, there, here] = jnp.where(has_ahead, face_ahead - drift, 0.0)
            couple[0, direction, 1, there, here] = jnp.where(has_behind, face_behind + drift, 0.0)
            couple[1, direction, 0, there, here] = jnp.where(has_ahead, face_ahead + drift, 0.0)
            couple[1, direction, 1, there, here] = jnp.where(has_behind, face_behind - drift, 0.0)
        large = 1.0 + diagonal
        over = 1.0 / (large * ratio)
        minus = ((large - ratio) * (large - ratio) + HALF * HALF) * over
        plus = minus + 4.0
        root = 2.0 / (minus + 2.0 + jnp.sqrt(minus * plus))
        lead = large - ratio * root
        gain = root * over / (1.0 - root * root)
        solve[0, there, here] = lead
        solve[1, there, here] = root * (1.0 / ratio)
        solve[2, there, here] = root * ratio
        solve[3, there, here] = gain
        solve[4, there, here] = HALF / lead
        solve[5, there, here] = ratio * (1.0 - root * root) / root
        for index, base in ((0, root * (1.0 / ratio)), (1, root * ratio)):
            square = base * base
            fourth = square * square
            power[k // lanes, z * lanes + k % lanes, index] = fourth * fourth

    def inner_coefficients(step, _):
        for k in range(4):
            coefficients(step * 4 + k, 1 - core)
        return 0

    def outer_coefficients(step, _):
        for k in range(8):
            coefficients(step * 8 + k, core)
        return 0

    pl.semaphore_wait(barrier, chips + 1 + core)

    @pl.when(core == 1)
    def _():
        for side in range(2):
            kappa_copy(side).start()

    for group in range(groups):
        for copy in rhs_copies(group):
            copy.start()

    lax.fori_loop(0, cells // COL // 4, inner_coefficients, 0)
    pltpu.make_async_copy(rhs.at[:, own_times], rhs.at[:, own_times], load_sem.at[2]).wait()
    kappa_copy(1).wait_recv()
    for side in range(2):

        @pl.when(core == side)
        def _():
            for piece in range(8):
                part = slice(piece * piece_width, piece * piece_width + piece_width)
                kappa[7 + 17 * side : 8 + 17 * side, part] = rim[2, piece : piece + 1, :]

    lax.fori_loop(0, cells // COL // 8, outer_coefficients, 0)

    def carry_copy(lot, other):
        return pltpu.make_async_remote_copy(
            src_ref=carry_out.at[lot, other],
            dst_ref=carry_in.at[lot, chip],
            send_sem=carry_send,
            recv_sem=carry_recv.at[lot],
            device_id=peer(other),
        )

    def entry_copy(lot, other, kind):
        return pltpu.make_async_remote_copy(
            src_ref=entry_out.at[lot, other],
            dst_ref=entry_in.at[lot, chip],
            send_sem=entry_send,
            recv_sem=entry_recv.at[lot, kind],
            device_id=peer(other),
        )

    def await_entry(lot, kind):
        blocks = entry_in.at[lot, pl.ds(0, chips // classes)]
        pltpu.make_async_copy(blocks, blocks, entry_recv.at[lot, kind]).wait()

    def powers(group):
        for direction in range(2):
            factor = base[group, direction]
            run = factor
            for step in range(1, chips + 1):
                growth[group, step, direction] = run
                run = run * factor

    def exchange(sweep, group):
        lot = sweep * groups + group

        arrived = carry_in.at[lot]
        pltpu.make_async_copy(arrived, arrived, carry_recv.at[lot]).wait()
        for direction, wrap in ((0, ALPHA), (1, 1.0 / ALPHA)):
            factor = growth[group, 1, direction]
            order = range(chips) if direction == 0 else range(chips - 1, -1, -1)
            run = None
            before = []
            for place in order:
                before.append(run)
                carry = carry_in[lot, place, direction]
                run = carry if run is None else carry + factor * run
            start = wrap * (run / (1.0 - wrap * growth[group, chips, direction]))
            for step, place in enumerate(order):
                value = start
                if step:
                    value = before[step] + start * growth[group, step, direction]
                entry_out[lot, place, direction] = value
        for half in range(pairs):
            for odd in range(2):
                for z in range(2):
                    other = z * lanes + lane_of(half, odd)
                    entry_copy(lot, other, half // 2).start()

    def sums(values, forward, backward):
        ahead = values[0]
        behind = values[-1]
        for step in range(1, times):
            ahead = values[step] + forward * ahead
            behind = values[times - 1 - step] + backward * behind
        return ahead, behind

    base_copy = pltpu.make_async_remote_copy(
        src_ref=power.at[:, chip],
        dst_ref=base,
        send_sem=base_sem.at[0],
        recv_sem=base_sem.at[1],
        device_id=pair,
    )
    base_copy.start()
    gain_store = pltpu.make_async_copy(solve.at[3], gain_out.at[rows], load_sem.at[3])
    gain_give = pltpu.make_async_remote_copy(
        src_ref=solve.at[3],
        dst_ref=gain_out.at[rows],
        send_sem=gain_sem.at[0],
        recv_sem=gain_sem.at[1],
        device_id=pair,
    )

    twin_copies = [
        pltpu.make_async_remote_copy(
            src_ref=solve.at[source],
            dst_ref=twin.at[target],
            send_sem=twin_send,
            recv_sem=twin_recv,
            device_id=pair,
        )
        for target, source in enumerate((1, 4))
    ]

    def first_sums(group):
        def quad_sums(step, _):
            places = [(2 * step + more, odd) for more in range(2) for odd in range(2)]
            for half, odd in places:
                lane = lane_of(half, odd)
                here = pl.ds(pl.multiple_of(group * width + lane * COL, COL), COL)
                for z in range(2):
                    there = slice(z * 8, z * 8 + 8)
                    lead = solve[0, there, here]
                    forward = solve[1, there, here]
                    backward = solve[2, there, here]
                    sides = [
                        sums([rhs[field, j, there, here] for j in range(times)], forward, backward)
                        for field in range(2)
                    ]
                    block = z * lanes + lane
                    carry_out[group, block, 0] = lead * sides[0][0] + HALF * sides[1][0]
                    carry_out[group, block, 1] = lead * sides[1][1] - HALF * sides[0][1]
            for half, odd in places:
                for z in range(2):
                    carry_copy(group, z * lanes + lane_of(half, odd)).start()
            return 0

        lax.fori_loop(0, pairs // 2, quad_sums, 0)

    for group in range(groups):
        arrived = rhs.at[:, own_times, :, slice(0, width)]
        pltpu.make_async_copy(arrived, arrived, rhs_recv.at[group]).wait()
        first_sums(group)
    gain_store.start()
    gain_give.start()
    for copy in twin_copies:
        copy.start()
    base_copy.wait_recv()
    for group in range(groups):
        powers(group)
    def solved(group, lane, z, scaled, ahead, back, emit):
        here = pl.ds(pl.multiple_of(group * width + lane * COL, COL), COL)
        there = slice(z * 8, z * 8 + 8)
        lead = solve[0, there, here]
        forward = solve[1, there, here]
        backward = solve[2, there, here]
        gain = solve[3, there, here]
        cross = solve[4, there, here]
        plain = solve[5, there, here]
        backs = [None] * times
        for j in reversed(range(times)):
            backs[j] = backward * back
            back = (
                lead * rhs[1, j, there, here] - HALF * rhs[0, j, there, here] + backs[j]
            )
        for j in range(times):
            adjoint = rhs[1, j, there, here]
            ahead = lead * rhs[0, j, there, here] + HALF * adjoint + forward * ahead
            state = ahead + cross * backs[j]
            adjoint = backs[j] - cross * ahead + plain * adjoint
            if scaled:
                state, adjoint = gain * state, gain * adjoint
            emit(j, state, adjoint)

    def edge_copies(column, mark):
        part = pl.ds(pl.multiple_of(column * COL, COL), COL)
        return (
            pltpu.make_async_remote_copy(
                src_ref=edge_out.at[core, :, part],
                dst_ref=edge_in.at[1 - core, :, part],
                send_sem=edge_send,
                recv_sem=edge_recv.at[mark],
                device_id=beside,
            ),
            pltpu.make_async_remote_copy(
                src_ref=edge_out.at[1 - core, :, part],
                dst_ref=edge_in.at[core, :, part],
                send_sem=edge_send,
                recv_sem=edge_recv.at[mark],
                device_id=pair,
            ),
        )

    def first_values(group):
        def pair_values(step, _):
            half = pairs - 1 - step
            for odd in (1, 0):
                lane = lane_of(half, odd)
                column = group * lanes + lane
                here = pl.ds(pl.multiple_of(column * COL, COL), COL)
                shifted = pl.ds(pl.multiple_of(column * COL + COL, COL), COL)
                for z in range(2):

                    def emit(j, state, adjoint):
                        first[0, j, z * 8 : z * 8 + 8, here] = state
                        first[1, j, z * 8 : z * 8 + 8, here] = adjoint
                        twist[0, j, z * 8 : z * 8 + 8, shifted] = turn(state, 64, 1)
                        twist[1, j, z * 8 : z * 8 + 8, shifted] = turn(adjoint, 64, 1)
                        edge = slice(7 * z, 7 * z + 1)
                        edge_out[z, j : j + 1, here] = state[edge]
                        edge_out[z, times + j : times + j + 1, here] = adjoint[edge]

                    solved(group, lane, z, True, zero, zero, emit)
                    line = z * 15
                    edge_out[z, 2 * times : 2 * times + 1, here] = solve[1, line : line + 1, here]
                    edge_out[z, 2 * times + 1 : 2 * times + 2, here] = solve[4, line : line + 1, here]
            for odd in (1, 0):
                for copy in edge_copies(group * lanes + lane_of(half, odd), group * classes + half // 2):
                    copy.start()
            return 0

        lax.fori_loop(0, pairs, pair_values, 0)

    for group in range(groups):
        first_values(group)

    for group in range(groups):
        exchange(0, group)

    tiles = (slice(0, 8), slice(8, 16))

    def column_of(column):
        return pl.ds(pl.multiple_of((column % columns) * COL, COL), COL)

    def in_z(own, below, above):
        up = [turn(value, 1, 0) for value in own]
        down = [turn(value, -1, 0) for value in own]
        return (
            [jnp.where(last_row, up[1], up[0]), jnp.where(last_row, above, up[1])],
            [jnp.where(first_row, below, down[0]), jnp.where(first_row, down[0], down[1])],
        )

    def in_plane(own, before, after):
        turned = turn(own, 64, 1)
        return (
            jnp.where(left, turned, turn(after, 64, 1)),
            jnp.where(left, turn(before, 64, 1), turned),
            turn(own, 1, 1),
            turn(own, -1, 1),
        )

    def edge_rows(line, here):
        return [jnp.broadcast_to(edge_in[side, line : line + 1, here], (8, COL)) for side in range(2)]

    def make_responses(column):
        here, before, after = column_of(column), column_of(column + columns - 1), column_of(column + 1)
        sides = []
        for index, line in ((1, 2 * times), (4, 2 * times + 1)):
            own = [solve[index, there, here] for there in tiles]
            z_ahead, z_behind = in_z(own, *edge_rows(line, here))
            sides.append(
                [
                    (z_ahead[z], z_behind[z])
                    + in_plane(own[z], solve[index, tiles[z], before], solve[index, tiles[z], after])
                    for z in range(2)
                ]
            )
        square_ratio = ratio * ratio
        for z in range(2):
            there = tiles[z]
            lead = solve[0, there, here]
            base_own = solve[1, there, here]
            square_own = base_own * base_own
            fourth_own = square_own * square_own
            for place in range(6):
                base_near, cross_near = sides[0][z][place], sides[1][z][place]
                square_near = base_near * base_near
                mixed = (base_own + base_near) * (square_own + square_near)
                mixed = mixed * (fourth_own + square_near * square_near)
                product = square_ratio * (base_own * base_near)
                square = product * product
                series = (1.0 + product) * (1.0 + square) * (1.0 + square * square)
                to_state = couple[0, place // 2, place % 2, there, here]
                to_adjoint = couple[1, place // 2, place % 2, there, here]
                state_lead, state_half = lead * to_state, HALF * to_state
                adjoint_lead, adjoint_half = lead * to_adjoint, HALF * to_adjoint
                response[place, 0, there, here] = mixed * (state_lead - cross_near * adjoint_half)
                response[place, 1, there, here] = series * (cross_near * state_lead + adjoint_half)
                response[place, 2, there, here] = -series * (state_half + cross_near * adjoint_lead)
                response[place, 3, there, here] = (square_ratio**7 * mixed) * (
                    adjoint_lead - cross_near * state_half
                )

    def couplings(group, summed):
        def pair_couplings(step, _):
            half = pairs - 1 - step
            if summed:

                @pl.when(step % 2 == 0)
                def _():
                    arrived = edge_in.at[:, :, pl.ds(0, 2 * pairs // classes * COL)]
                    sem = edge_recv.at[group * classes + half // 2]
                    pltpu.make_async_copy(arrived, arrived, sem).wait()

            for odd in (1, 0):
                lane = lane_of(half, odd)
                column = group * lanes + lane
                lane0 = column * COL
                here = pl.ds(pl.multiple_of(lane0, COL), COL)
                shifted = pl.ds(pl.multiple_of(lane0 + COL, COL), COL)
                after = pl.ds(pl.multiple_of(lane0 + 2 * COL, COL), COL)
                forward = [solve[1, there, here] for there in tiles]
                backward = [solve[2, there, here] for there in tiles]
                sides = []
                for field in range(2):
                    weights = [
                        [couple[field, d, s, there, here] for there in tiles]
                        for d in range(3)
                        for s in range(2)
                    ]
                    ahead_sum = [zero, zero]
                    behind_sum = [zero, zero]
                    scale = [jnp.ones((8, COL), jnp.float32)] * 2
                    for j in range(times):
                        own = [first[field, j, there, here] for there in tiles]
                        z_ahead, z_behind = in_z(own, *edge_rows(field * times + j, here))
                        for z in range(2):
                            there = tiles[z]
                            turned = twist[field, j, there, shifted]
                            x_ahead = jnp.where(left, turned, twist[field, j, there, after])
                            x_behind = jnp.where(left, twist[field, j, there, here], turned)
                            value = (
                                rhs[field, j, there, here]
                                + weights[0][z] * z_ahead[z]
                                + weights[1][z] * z_behind[z]
                                + weights[2][z] * x_ahead
                                + weights[3][z] * x_behind
                                + weights[4][z] * turn(own[z], 1, 1)
                                + weights[5][z] * turn(own[z], -1, 1)
                            )
                            rhs[field, j, there, here] = value
                            if summed:
                                ahead_sum[z] = value + forward[z] * ahead_sum[z]
                                behind_sum[z] = behind_sum[z] + scale[z] * value
                                if j < times - 1:
                                    scale[z] = scale[z] * backward[z]
                    sides.append((ahead_sum, behind_sum))
                if summed:
                    make_responses(column)
                    for z in range(2):
                        lead = solve[0, tiles[z], here]
                        block = z * lanes + lane
                        lot = groups + group
                        carry_out[lot, block, 0] = lead * sides[0][0][z] + HALF * sides[1][0][z]
                        carry_out[lot, block, 1] = lead * sides[1][1][z] - HALF * sides[0][1][z]
            return 0

        lax.fori_loop(0, pairs, pair_couplings, 0)

    for group in range(groups):
        couplings(group, True)

    def entries(group):
        def pair_entries(step, _):
            half = pairs - 1 - step

            for odd in (1, 0):
                lane = lane_of(half, odd)
                here = pl.ds(pl.multiple_of((group * lanes + lane) * COL, COL), COL)
                for z in range(2):
                    gain = solve[3, tiles[z], here]
                    for index in range(2):
                        entered[index, 8 + z * 8 : 16 + z * 8, here] = (
                            gain * solve[1 + index, tiles[z], here] * entry_in[group, z * lanes + lane, index]
                        )
            return 0

        lax.fori_loop(0, pairs, pair_entries, 0)

    for group in range(groups):
        for kind in range(classes):
            await_entry(group, kind)
        for lane in range(lanes):
            column = group * lanes + lane
            here = slice(column * COL, column * COL + COL)
            for side in range(2):
                line, edge, block = slice(15 * side, 15 * side + 1), slice(7 * side, 7 * side + 1), side * lanes + lane
                gain = solve[3, line, here]
                for index in range(2):
                    pack_out[side, index, column : column + 1, :] = (
                        gain * solve[1 + index, line, here] * entry_in[group, block, index, edge]
                    )
    pack_copies = [
        pltpu.make_async_remote_copy(
            src_ref=pack_out.at[1 - core],
            dst_ref=pack_in.at[core],
            send_sem=pack_send,
            recv_sem=pack_recv.at[0],
            device_id=pair,
        ),
        pltpu.make_async_remote_copy(
            src_ref=pack_out.at[core],
            dst_ref=pack_in.at[1 - core],
            send_sem=pack_send,
            recv_sem=pack_recv.at[1],
            device_id=beside,
        ),
    ]
    for copy in pack_copies:
        copy.start()
    for group in range(groups):
        entries(group)

    def unpack(side):
        for index in range(2):
            for column in range(columns):
                part = slice(column * COL, column * COL + COL)
                line = 7 + 17 * side
                entered[index, line : line + 1, part] = pack_in[side, index, column : column + 1, :]

    def second_sums(step, _):
        for k in range(4):
            column = step * 4 + k
            here, before, after = column_of(column), column_of(column + columns - 1), column_of(column + 1)
            lot = groups + column // lanes
            sides = [[], []]
            for index in range(2):
                own = [entered[index, 8 + z * 8 : 16 + z * 8, here] for z in range(2)]
                z_ahead, z_behind = in_z(own, zero, zero)
                for z in range(2):
                    centre = slice(8 + z * 8, 16 + z * 8)
                    sides[z].append(
                        (z_ahead[z], z_behind[z])
                        + in_plane(own[z], entered[index, centre, before], entered[index, centre, after])
                    )
            for z in range(2):
                block = z * lanes + column % lanes
                for direction in range(2):
                    total_sum = carry_out[lot, block, direction]
                    for place in range(6):
                        for index in range(2):
                            factor = response[place, 2 * direction + index, tiles[z], here]
                            total_sum = total_sum + factor * sides[z][index][place]
                    carry_out[lot, block, direction] = total_sum
        return 0

    lax.fori_loop(0, columns // 4, second_sums, 0)

    def add_rows(side):
        z, place, edge = side, 1 - side, (last_row if side else first_row)
        for column in range(columns):
            here = slice(column * COL, column * COL + COL)
            lot, block = groups + column // lanes, z * lanes + column % lanes
            enter = [
                jnp.broadcast_to(pack_in[side, index, column : column + 1, :], (8, COL)) for index in range(2)
            ]
            for direction in range(2):
                more = (
                    response[place, 2 * direction, tiles[z], here] * enter[0]
                    + response[place, 2 * direction + 1, tiles[z], here] * enter[1]
                )
                carry_out[lot, block, direction] = carry_out[lot, block, direction] + jnp.where(edge, more, 0.0)
        for group in range(groups):
            for half in range(pairs):
                for odd in range(2):
                    carry_copy(groups + group, z * lanes + lane_of(half, odd)).start()

    for outer in range(2):
        pack_copies[outer].wait_recv()
        for side in range(2):

            @pl.when(core == (side if outer else 1 - side))
            def _():
                add_rows(side)

    for side in range(2):
        unpack(side)

    def entered_values(step, _):
        for k in range(2):
            column_values(step * 2 + k)
        return 0

    def column_values(column):
        here = pl.ds(pl.multiple_of(column * COL, COL), COL)
        shifted = pl.ds(pl.multiple_of(column * COL + COL, COL), COL)

        def emit_all(ahead, behind, forward, backward, cross, emit):
            behinds = [behind]
            for _ in range(times - 1):
                behinds.append(behinds[-1] * backward)
            for j in range(times):
                emit(j, ahead + cross * behinds[times - 1 - j], behinds[times - 1 - j] - cross * ahead)
                if j < times - 1:
                    ahead = ahead * forward

        for z in range(2):

            def emit(j, state, adjoint):
                first[0, j, tiles[z], here] = state
                first[1, j, tiles[z], here] = adjoint
                twist[0, j, tiles[z], shifted] = turn(state, 64, 1)
                twist[1, j, tiles[z], shifted] = turn(adjoint, 64, 1)

            own = slice(8 + z * 8, 16 + z * 8)
            emit_all(
                entered[0, own, here],
                entered[1, own, here],
                solve[1, tiles[z], here],
                solve[2, tiles[z], here],
                solve[4, tiles[z], here],
                emit,
            )
        for side in range(2):

            def emit(j, state, adjoint):
                edge_in[side, j : j + 1, here] = state
                edge_in[side, times + j : times + j + 1, here] = adjoint

            line = slice(7 + 17 * side, 8 + 17 * side)
            forward = edge_in[side, 2 * times : 2 * times + 1, here]
            cross = edge_in[side, 2 * times + 1 : 2 * times + 2, here]
            emit_all(
                entered[0, line, here],
                entered[1, line, here],
                forward,
                forward * (ratio * ratio),
                cross,
                emit,
            )

    lax.fori_loop(0, columns // 2, entered_values, 0)
    def give_copy(column):
        part = pl.ds(pl.multiple_of(column * COL, COL), COL)
        return pltpu.make_async_remote_copy(
            src_ref=result.at[:, pair_times, :, part],
            dst_ref=given.at[:, :, :, part],
            send_sem=give_send,
            recv_sem=give_recv,
            device_id=pair,
        )

    def second_values(step, _):
        for k in range(2):
            column = step * 2 + k
            here = pl.ds(pl.multiple_of(column * COL, COL), COL)
            for z in range(2):

                def emit(j, state, adjoint):
                    result[0, j, tiles[z], here] = state
                    result[1, j, tiles[z], here] = adjoint

                solved(0, column, z, False, zero, zero, emit)
        for k in range(2):
            give_copy(step * 2 + k).start()
        return 0

    for group in range(groups):
        couplings(group, False)
        lax.fori_loop(group * lanes // 2, (group + 1) * lanes // 2, second_values, 0)
        if group == groups // 2 - 1:
            for other_group in range(groups):
                exchange(1, other_group)

    def twin_entry_copy(group):
        return pltpu.make_async_remote_copy(
            src_ref=entry_in.at[groups + group],
            dst_ref=twin_entry.at[group],
            send_sem=twin_entry_send,
            recv_sem=twin_entry_recv.at[group],
            device_id=pair,
        )

    def finish(group, first_line, entered_at, base_at, cross_at, value_at):
        def finish_columns(step, _):
            for k in range(4):
                lane = step * 4 + k
                here = pl.ds(pl.multiple_of((group * lanes + lane) * COL, COL), COL)
                for z in range(2):
                    there = pl.ds(pl.multiple_of(first_line + z * 8, 8), 8)
                    forward = base_at(tiles[z], here)
                    backward = forward * (ratio * ratio)
                    cross = cross_at(tiles[z], here)
                    forward_half, backward_half = forward, backward
                    for _ in range(half_times.bit_length() - 1):
                        forward_half = forward_half * forward_half
                        backward_half = backward_half * backward_half
                    ahead = entered_at(z * lanes + lane, 0)
                    ahead = jnp.where(core == 1, forward_half * ahead, ahead)
                    behind = entered_at(z * lanes + lane, 1)
                    behind = jnp.where(core == 1, behind, backward_half * behind)
                    behinds = []
                    for _ in range(half_times):
                        behind = backward * behind
                        behinds.append(behind)
                    for j in range(half_times):
                        ahead = forward * ahead
                        behind = behinds[half_times - 1 - j]
                        both_out[0, j, there, here] = value_at(0, j, tiles[z], here) + (ahead + cross * behind)
                        both_out[1, j, there, here] = value_at(1, j, tiles[z], here) + (behind - cross * ahead)
            return 0

        lax.fori_loop(0, lanes // 4, finish_columns, 0)

    def drain(ref, semaphore):
        pltpu.make_async_copy(ref, ref, semaphore).wait()

    for group in range(groups):
        for kind in range(classes):
            await_entry(groups + group, kind)
        twin_entry_copy(group).start()
        finish(
            group,
            core * 16,
            lambda block, index: entry_in[groups + group, block, index],
            lambda there, here: solve[1, there, here],
            lambda there, here: solve[4, there, here],
            lambda field, j, there, here: result[field, core * half_times + j, there, here],
        )
    drain(twin, twin_recv)
    drain(given, give_recv)
    for group in range(groups):
        drain(twin_entry.at[group], twin_entry_recv.at[group])
        finish(
            group,
            16 - core * 16,
            lambda block, index: twin_entry[group, block, index],
            lambda there, here: twin[0, there, here],
            lambda there, here: twin[1, there, here],
            lambda field, j, there, here: given[field, j, there, here],
        )

    gain_store.wait()
    gain_give.wait()
    base_copy.wait_send()

    @pl.when(core == 1)
    def _():
        drain(rim.at[pl.ds(0, 2)], kappa_send)

    drain(rhs.at[:, own_times], rhs_send)
    drain(carry_out, carry_send)
    drain(entry_out, entry_send)
    drain(edge_out, edge_send)
    drain(pack_out, pack_send)
    drain(result.at[:, own_times], give_send)
    drain(twin, twin_send)
    drain(twin_entry, twin_entry_send)


def write_kernel(both, gain, state_out, adjoint_out, stage, semaphore):
    for field, target in enumerate((state_out, adjoint_out)):
        for step in range(both.shape[1]):
            stage[field, step] = both[field, step] * gain[...]
            pltpu.make_async_copy(stage.at[field, step], target.at[step], semaphore.at[field]).start()
    for field, target in enumerate((state_out, adjoint_out)):
        pltpu.make_async_copy(stage.at[field], target, semaphore.at[field]).wait()


def solution(mesh):
    ranks = mesh.shape["tm"]
    slabs = mesh.shape["gz"]
    chips = ranks // 2

    def body(state_rhs, adjoint_rhs, diffusivity, velocity):
        steps, depth, cells = state_rhs.shape
        times = 2 * steps
        columns = cells // COL
        groups = 2 * columns // chips
        f32 = jnp.float32
        dma = pltpu.SemaphoreType.DMA
        anywhere = pl.BlockSpec(memory_space=pl.ANY)
        exchanged = pltpu.VMEM((2 * groups, chips, 2, 8, COL), f32)
        call = pl.pallas_call(
            functools.partial(kernel, chips, slabs, cells, times),
            out_shape=[
                pltpu.VMEM((2, steps, depth, cells), f32),
                pltpu.VMEM((depth, cells), f32),
            ],
            in_specs=[anywhere] * 4,
            out_specs=[pl.BlockSpec(memory_space=pltpu.VMEM), anywhere],
            scratch_shapes=[
                pltpu.VMEM((2, times, 16, cells), f32),
                pltpu.VMEM((2, times, 16, cells), f32),
                pltpu.VMEM((2, times, 16, cells + 2 * COL), f32),
                pltpu.VMEM((2, times, 16, cells), f32),
                pltpu.VMEM((32, cells), f32),
                pltpu.VMEM((8, cells), f32),
                pltpu.VMEM((3, 8, cells // 8), f32),
                pltpu.VMEM((3, 16, cells), f32),
                pltpu.VMEM((2, 3, 2, 16, cells), f32),
                pltpu.VMEM((6, 16, cells), f32),
                pltpu.VMEM((groups, chips, 2, 8, COL), f32),
                pltpu.VMEM((groups, 2, 8, COL), f32),
                pltpu.VMEM((groups, chips + 1, 2, 8, COL), f32),
                exchanged,
                exchanged,
                exchanged,
                exchanged,
                pltpu.VMEM((2, 3 * times, cells), f32),
                pltpu.VMEM((2, 3 * times, cells), f32),
                pltpu.VMEM((6, 4, 16, cells), f32),
                pltpu.VMEM((2, 32, cells), f32),
                pltpu.VMEM((2, 2, columns, COL), f32),
                pltpu.VMEM((2, 2, columns, COL), f32),
                pltpu.VMEM((2, 16, cells), f32),
                pltpu.VMEM((2, steps, 16, cells), f32),
                pltpu.VMEM((groups, chips, 2, 8, COL), f32),
                dma((4,)),
                dma,
                dma((groups,)),
                dma,
                dma,
                dma((2,)),
                dma((2,)),
                dma,
                dma((2 * groups,)),
                dma,
                dma((2 * groups, 2)),
                dma,
                dma((2 * groups,)),
                dma,
                dma((2,)),
                dma,
                dma,
                dma,
                dma((groups,)),
                dma,
                dma,
            ],
            compiler_params=pltpu.CompilerParams(
                collective_id=0, has_side_effects=True, vmem_limit_bytes=48 * 1024 * 1024
            ),
            cost_estimate=pl.CostEstimate(
                flops=60 * state_rhs.size, bytes_accessed=20 * state_rhs.size, transcendentals=0
            ),
        )
        held = [
            pltpu.with_memory_space_constraint(array, pltpu.HBM)
            for array in (state_rhs, adjoint_rhs, diffusivity, velocity)
        ]
        both, gain = call(*held)
        write = pl.pallas_call(
            write_kernel,
            out_shape=[jax.ShapeDtypeStruct(state_rhs.shape, f32)] * 2,
            in_specs=[pl.BlockSpec(memory_space=pltpu.VMEM)] * 2,
            out_specs=[anywhere] * 2,
            scratch_shapes=[pltpu.VMEM((2, steps, depth, cells), f32), dma((2,))],
            compiler_params=pltpu.CompilerParams(vmem_limit_bytes=48 * 1024 * 1024),
        )
        placed_inputs = [pltpu.with_memory_space_constraint(array, pltpu.VMEM) for array in (both, gain)]
        return tuple(write(*placed_inputs))

    placed = (P("tm", "gz", None), P("tm", "gz", None), P("gz", None), P(None, "gz", None))
    return jax.shard_map(
        body,
        mesh=mesh,
        in_specs=placed,
        out_specs=(P("tm", "gz", None), P("tm", "gz", None)),
        check_vma=False,
    )
```

```python
import functools
import math

import jax
import jax.numpy as jnp
from jax import lax
from jax.experimental import pallas as pl
from jax.experimental.pallas import tpu as pltpu
from jax.sharding import PartitionSpec as P

NY = 64
COL = 128
ALPHA = 0.1
HALF = 0.5


def turn(value, shift, axis):
    return pltpu.roll(value, (-shift) % value.shape[axis], axis)


def kernel(
    chips, slabs, cells, times,
    state_hbm, adjoint_hbm, kappa_hbm, speed_hbm,
    both_out,
    rhs, first, twist, result, kappa, edge_row, rim, speed, couple, solve, power, base, growth,
    carry_out, carry_in, entry_out, entry_in, edge_out, edge_in,
    response, entered, pack_out, pack_in, twin, given, twin_entry,
    load_sem, rhs_send, rhs_recv, kappa_send, kappa_recv, base_sem,
    carry_send, carry_recv, entry_send, entry_recv,
    edge_send, edge_recv, pack_send, pack_recv, twin_send, twin_recv, twin_entry_send, twin_entry_recv, give_send, give_recv,
):
    half_times = times // 2
    lanes = chips // 2
    columns = cells // COL
    groups = columns // lanes
    width = lanes * COL
    total = chips * times
    ratio = ALPHA ** (1.0 / total)

    me = lax.axis_index("tm")
    slab = lax.axis_index("gz")
    chip = me // 2
    core = me % 2
    pair = {"tm": chip * 2 + 1 - core, "gz": slab}
    beside = {"tm": chip * 2 + 1 - core, "gz": (slab + slabs + 2 * core - 1) % slabs}

    behind_same = {"tm": me, "gz": (slab + slabs - 1) % slabs}

    def peer(other):
        return {"tm": other * 2 + 1 - core, "gz": slab}

    rows = pl.ds(pl.multiple_of(core * 16, 16), 16)
    rows_pair = pl.ds(pl.multiple_of(16 - core * 16, 16), 16)
    own_times = pl.ds(core * half_times, half_times)
    pair_times = pl.ds((1 - core) * half_times, half_times)

    def lane_of(half, odd):
        if lanes != 8:
            return (chip + 2 * half + odd) % lanes
        outer = half % 3 == 0
        if isinstance(half, int):
            move_x = 2 - 2 * (half // 3) if outer else 1 + 2 * odd
            move_y = odd if outer else half - 1
        else:
            move_x = jnp.where(outer, 2 - 2 * (half // 3), 1 + 2 * odd)
            move_y = jnp.where(outer, odd, half - 1)
        return ((chip // 4 + move_y) % 2) * 4 + (chip % 4 + move_x) % 4

    pairs = lanes // 2
    classes = (pairs + 1) // 2

    def tile8(start):
        return pl.ds(pl.multiple_of(start, 8), 8)

    barrier = pltpu.get_barrier_semaphore()
    for half in range(lanes // 2):
        for odd in range(2):
            for z in range(2):
                target = peer(z * lanes + lane_of(half, odd))
                pl.semaphore_signal(barrier, inc=1, device_id=target)
    pl.semaphore_signal(barrier, inc=1, device_id=beside)

    @pl.when(core == 1)
    def _():
        pl.semaphore_signal(barrier, inc=1, device_id={"tm": me, "gz": (slab + 1) % slabs})

    loads = [
        pltpu.make_async_copy(kappa_hbm.at[rows], kappa.at[pl.ds(8, 16)], load_sem.at[0]),
        pltpu.make_async_copy(
            kappa_hbm.at[tile8(16 - 8 * core)], kappa.at[tile8(24 - 24 * core)], load_sem.at[0]
        ),
        pltpu.make_async_copy(kappa_hbm.at[pl.ds(0, 8)], edge_row, load_sem.at[0]),
        pltpu.make_async_copy(speed_hbm.at[:, rows], speed, load_sem.at[1]),
        pltpu.make_async_copy(state_hbm.at[:, rows], rhs.at[0, own_times], load_sem.at[2]),
        pltpu.make_async_copy(adjoint_hbm.at[:, rows], rhs.at[1, own_times], load_sem.at[2]),
    ]
    for load in loads:
        load.start()

    def kappa_copy(side):
        return pltpu.make_async_remote_copy(
            src_ref=rim.at[side],
            dst_ref=rim.at[2],
            send_sem=kappa_send,
            recv_sem=kappa_recv,
            device_id=beside if side else behind_same,
        )

    def rhs_copies(group):
        part = slice(group * width, group * width + width)
        return [
            pltpu.make_async_remote_copy(
                src_ref=source.at[:, rows_pair, part],
                dst_ref=rhs.at[field, own_times, :, part],
                send_sem=rhs_send,
                recv_sem=rhs_recv.at[group],
                device_id=pair,
            )
            for field, source in enumerate((state_hbm, adjoint_hbm))
        ]

    lane = lax.broadcasted_iota(jnp.int32, (8, COL), 1)
    row = lax.broadcasted_iota(jnp.int32, (8, COL), 0)
    left = lane < 64
    first_row = row == 0
    last_row = row == 7

    zero = jnp.zeros((8, COL), jnp.float32)
    for field in range(2):
        for step in range(times):
            for z in range(2):
                twist[field, step, z * 8 : z * 8 + 8, :COL] = zero
                twist[field, step, z * 8 : z * 8 + 8, cells + COL :] = zero

    pltpu.make_async_copy(kappa.at[pl.ds(0, 32)], kappa.at[pl.ds(0, 32)], load_sem.at[0]).wait()
    piece_width = cells // 8

    @pl.when(core == 1)
    def _():
        for side, source, line in ((0, edge_row, 0), (1, kappa, 23)):
            for piece in range(8):
                part = slice(piece * piece_width, piece * piece_width + piece_width)
                rim[side, piece : piece + 1, :] = source[line : line + 1, part]

    loads[3].wait()

    def coefficients(k, z):
        there = pl.ds(pl.multiple_of(z * 8, 8), 8)
        centre = pl.ds(pl.multiple_of(8 + z * 8, 8), 8)
        below = pl.ds(pl.multiple_of(z * 8, 8), 8)
        above = pl.ds(pl.multiple_of(16 + z * 8, 8), 8)
        lane0 = pl.multiple_of(k * COL, COL)
        here = pl.ds(lane0, COL)
        before = pl.ds(pl.multiple_of(((k + cells // COL - 1) % (cells // COL)) * COL, COL), COL)
        after = pl.ds(pl.multiple_of(((k + 1) % (cells // COL)) * COL, COL), COL)
        x_place = k * 2 + lane // NY
        y_place = lane % NY
        z_place = slab * 32 + core * 16 + z * 8 + row
        own = kappa[centre, here]
        turned = turn(own, 64, 1)
        x_ahead = jnp.where(left, turned, turn(kappa[centre, after], 64, 1))
        x_behind = jnp.where(left, turn(kappa[centre, before], 64, 1), turned)
        z_ahead = jnp.where(
            last_row, turn(kappa[above, here], 1, 0), turn(own, 1, 0)
        )
        z_behind = jnp.where(
            first_row, turn(kappa[below, here], -1, 0), turn(own, -1, 0)
        )
        diagonal = jnp.zeros((8, COL), jnp.float32)
        for direction, (ahead, behind, place, count, component) in enumerate(
            (
                (z_ahead, z_behind, z_place, slabs * 32, 2),
                (x_ahead, x_behind, x_place, cells // NY, 0),
                (turn(own, 1, 1), turn(own, -1, 1), y_place, NY, 1),
            )
        ):
            has_ahead = place < count - 1
            has_behind = place > 0
            face_ahead = jnp.where(has_ahead, 0.5 * (own + ahead), own)
            face_behind = jnp.where(has_behind, 0.5 * (own + behind), own)
            diagonal = diagonal + face_ahead + face_behind
            drift = 0.5 * speed[component, there, here]
            couple[0, direction, 0, there, here] = jnp.where(has_ahead, face_ahead - drift, 0.0)
            couple[0, direction, 1, there, here] = jnp.where(has_behind, face_behind + drift, 0.0)
            couple[1, direction, 0, there, here] = jnp.where(has_ahead, face_ahead + drift, 0.0)
            couple[1, direction, 1, there, here] = jnp.where(has_behind, face_behind - drift, 0.0)
        large = 1.0 + diagonal
        over = 1.0 / (large * ratio)
        minus = ((large - ratio) * (large - ratio) + HALF * HALF) * over
        plus = minus + 4.0
        root = 2.0 / (minus + 2.0 + jnp.sqrt(minus * plus))
        lead = large - ratio * root
        gain = root * over / (1.0 - root * root)
        solve[0, there, here] = lead
        solve[1, there, here] = root * (1.0 / ratio)
        solve[2, there, here] = root * ratio
        solve[3, there, here] = gain
        solve[4, there, here] = HALF / lead
        solve[5, there, here] = ratio * (1.0 - root * root) / root
        for index, base in ((0, root * (1.0 / ratio)), (1, root * ratio)):
            square = base * base
            fourth = square * square
            power[k // lanes, z * lanes + k % lanes, index] = fourth * fourth

    def inner_coefficients(step, _):
        for k in range(4):
            coefficients(step * 4 + k, 1 - core)
        return 0

    def outer_coefficients(step, _):
        for k in range(8):
            coefficients(step * 8 + k, core)
        return 0

    pl.semaphore_wait(barrier, chips + 1 + core)

    @pl.when(core == 1)
    def _():
        for side in range(2):
            kappa_copy(side).start()

    for group in range(groups):
        for copy in rhs_copies(group):
            copy.start()

    lax.fori_loop(0, cells // COL // 4, inner_coefficients, 0)
    pltpu.make_async_copy(rhs.at[:, own_times], rhs.at[:, own_times], load_sem.at[2]).wait()
    kappa_copy(1).wait_recv()
    for side in range(2):

        @pl.when(core == side)
        def _():
            for piece in range(8):
                part = slice(piece * piece_width, piece * piece_width + piece_width)
                kappa[7 + 17 * side : 8 + 17 * side, part] = rim[2, piece : piece + 1, :]

    lax.fori_loop(0, cells // COL // 8, outer_coefficients, 0)

    def carry_copy(lot, other):
        return pltpu.make_async_remote_copy(
            src_ref=carry_out.at[lot, other],
            dst_ref=carry_in.at[lot, chip],
            send_sem=carry_send,
            recv_sem=carry_recv.at[lot],
            device_id=peer(other),
        )

    def entry_copy(lot, other, kind):
        return pltpu.make_async_remote_copy(
            src_ref=entry_out.at[lot, other],
            dst_ref=entry_in.at[lot, chip],
            send_sem=entry_send,
            recv_sem=entry_recv.at[lot, kind],
            device_id=peer(other),
        )

    def await_entry(lot, kind):
        blocks = entry_in.at[lot, pl.ds(0, chips // classes)]
        pltpu.make_async_copy(blocks, blocks, entry_recv.at[lot, kind]).wait()

    def powers(group):
        for direction in range(2):
            factor = base[group, direction]
            run = factor
            for step in range(1, chips + 1):
                growth[group, step, direction] = run
                run = run * factor

    def exchange(sweep, group):
        lot = sweep * groups + group

        arrived = carry_in.at[lot]
        pltpu.make_async_copy(arrived, arrived, carry_recv.at[lot]).wait()
        for direction, wrap in ((0, ALPHA), (1, 1.0 / ALPHA)):
            factor = growth[group, 1, direction]
            order = range(chips) if direction == 0 else range(chips - 1, -1, -1)
            run = None
            before = []
            for place in order:
                before.append(run)
                carry = carry_in[lot, place, direction]
                run = carry if run is None else carry + factor * run
            start = wrap * (run / (1.0 - wrap * growth[group, chips, direction]))
            for step, place in enumerate(order):
                value = start
                if step:
                    value = before[step] + start * growth[group, step, direction]
                entry_out[lot, place, direction] = value
        for half in range(pairs):
            for odd in range(2):
                for z in range(2):
                    other = z * lanes + lane_of(half, odd)
                    entry_copy(lot, other, half // 2).start()

    def sums(values, forward, backward):
        ahead = values[0]
        behind = values[-1]
        for step in range(1, times):
            ahead = values[step] + forward * ahead
            behind = values[times - 1 - step] + backward * behind
        return ahead, behind

    base_copy = pltpu.make_async_remote_copy(
        src_ref=power.at[:, chip],
        dst_ref=base,
        send_sem=base_sem.at[0],
        recv_sem=base_sem.at[1],
        device_id=pair,
    )
    base_copy.start()
    twin_copies = [
        pltpu.make_async_remote_copy(
            src_ref=solve.at[source],
            dst_ref=twin.at[target],
            send_sem=twin_send,
            recv_sem=twin_recv,
            device_id=pair,
        )
        for target, source in enumerate((1, 4, 3))
    ]

    def first_sums(group):
        def quad_sums(step, _):
            places = [(2 * step + more, odd) for more in range(2) for odd in range(2)]
            for half, odd in places:
                lane = lane_of(half, odd)
                here = pl.ds(pl.multiple_of(group * width + lane * COL, COL), COL)
                for z in range(2):
                    there = slice(z * 8, z * 8 + 8)
                    lead = solve[0, there, here]
                    forward = solve[1, there, here]
                    backward = solve[2, there, here]
                    sides = [
                        sums([rhs[field, j, there, here] for j in range(times)], forward, backward)
                        for field in range(2)
                    ]
                    block = z * lanes + lane
                    carry_out[group, block, 0] = lead * sides[0][0] + HALF * sides[1][0]
                    carry_out[group, block, 1] = lead * sides[1][1] - HALF * sides[0][1]
            for half, odd in places:
                for z in range(2):
                    carry_copy(group, z * lanes + lane_of(half, odd)).start()
            return 0

        lax.fori_loop(0, pairs // 2, quad_sums, 0)

    for group in range(groups):
        arrived = rhs.at[:, own_times, :, slice(0, width)]
        pltpu.make_async_copy(arrived, arrived, rhs_recv.at[group]).wait()
        first_sums(group)
    for copy in twin_copies:
        copy.start()
    base_copy.wait_recv()
    for group in range(groups):
        powers(group)
    def solved(group, lane, z, scaled, ahead, back, emit):
        here = pl.ds(pl.multiple_of(group * width + lane * COL, COL), COL)
        there = slice(z * 8, z * 8 + 8)
        lead = solve[0, there, here]
        forward = solve[1, there, here]
        backward = solve[2, there, here]
        gain = solve[3, there, here]
        cross = solve[4, there, here]
        plain = solve[5, there, here]
        backs = [None] * times
        for j in reversed(range(times)):
            backs[j] = backward * back
            back = (
                lead * rhs[1, j, there, here] - HALF * rhs[0, j, there, here] + backs[j]
            )
        for j in range(times):
            adjoint = rhs[1, j, there, here]
            ahead = lead * rhs[0, j, there, here] + HALF * adjoint + forward * ahead
            state = ahead + cross * backs[j]
            adjoint = backs[j] - cross * ahead + plain * adjoint
            if scaled:
                state, adjoint = gain * state, gain * adjoint
            emit(j, state, adjoint)

    def edge_copies(column, mark):
        part = pl.ds(pl.multiple_of(column * COL, COL), COL)
        return (
            pltpu.make_async_remote_copy(
                src_ref=edge_out.at[core, :, part],
                dst_ref=edge_in.at[1 - core, :, part],
                send_sem=edge_send,
                recv_sem=edge_recv.at[mark],
                device_id=beside,
            ),
            pltpu.make_async_remote_copy(
                src_ref=edge_out.at[1 - core, :, part],
                dst_ref=edge_in.at[core, :, part],
                send_sem=edge_send,
                recv_sem=edge_recv.at[mark],
                device_id=pair,
            ),
        )

    def first_values(group):
        def pair_values(step, _):
            half = pairs - 1 - step
            for odd in (1, 0):
                lane = lane_of(half, odd)
                column = group * lanes + lane
                here = pl.ds(pl.multiple_of(column * COL, COL), COL)
                shifted = pl.ds(pl.multiple_of(column * COL + COL, COL), COL)
                for z in range(2):

                    def emit(j, state, adjoint):
                        first[0, j, z * 8 : z * 8 + 8, here] = state
                        first[1, j, z * 8 : z * 8 + 8, here] = adjoint
                        twist[0, j, z * 8 : z * 8 + 8, shifted] = turn(state, 64, 1)
                        twist[1, j, z * 8 : z * 8 + 8, shifted] = turn(adjoint, 64, 1)
                        edge = slice(7 * z, 7 * z + 1)
                        edge_out[z, j : j + 1, here] = state[edge]
                        edge_out[z, times + j : times + j + 1, here] = adjoint[edge]

                    solved(group, lane, z, True, zero, zero, emit)
                    line = z * 15
                    edge_out[z, 2 * times : 2 * times + 1, here] = solve[1, line : line + 1, here]
                    edge_out[z, 2 * times + 1 : 2 * times + 2, here] = solve[4, line : line + 1, here]
            for odd in (1, 0):
                for copy in edge_copies(group * lanes + lane_of(half, odd), group * classes + half // 2):
                    copy.start()
            return 0

        lax.fori_loop(0, pairs, pair_values, 0)

    for group in range(groups):
        first_values(group)

    for group in range(groups):
        exchange(0, group)

    tiles = (slice(0, 8), slice(8, 16))

    def column_of(column):
        return pl.ds(pl.multiple_of((column % columns) * COL, COL), COL)

    def in_z(own, below, above):
        up = [turn(value, 1, 0) for value in own]
        down = [turn(value, -1, 0) for value in own]
        return (
            [jnp.where(last_row, up[1], up[0]), jnp.where(last_row, above, up[1])],
            [jnp.where(first_row, below, down[0]), jnp.where(first_row, down[0], down[1])],
        )

    def in_plane(own, before, after):
        turned = turn(own, 64, 1)
        return (
            jnp.where(left, turned, turn(after, 64, 1)),
            jnp.where(left, turn(before, 64, 1), turned),
            turn(own, 1, 1),
            turn(own, -1, 1),
        )

    def edge_rows(line, here):
        return [jnp.broadcast_to(edge_in[side, line : line + 1, here], (8, COL)) for side in range(2)]

    def make_responses(column):
        here, before, after = column_of(column), column_of(column + columns - 1), column_of(column + 1)
        sides = []
        for index, line in ((1, 2 * times), (4, 2 * times + 1)):
            own = [solve[index, there, here] for there in tiles]
            z_ahead, z_behind = in_z(own, *edge_rows(line, here))
            sides.append(
                [
                    (z_ahead[z], z_behind[z])
                    + in_plane(own[z], solve[index, tiles[z], before], solve[index, tiles[z], after])
                    for z in range(2)
                ]
            )
        square_ratio = ratio * ratio
        for z in range(2):
            there = tiles[z]
            lead = solve[0, there, here]
            base_own = solve[1, there, here]
            square_own = base_own * base_own
            fourth_own = square_own * square_own
            for place in range(6):
                base_near, cross_near = sides[0][z][place], sides[1][z][place]
                square_near = base_near * base_near
                mixed = (base_own + base_near) * (square_own + square_near)
                mixed = mixed * (fourth_own + square_near * square_near)
                product = square_ratio * (base_own * base_near)
                square = product * product
                series = (1.0 + product) * (1.0 + square) * (1.0 + square * square)
                to_state = couple[0, place // 2, place % 2, there, here]
                to_adjoint = couple[1, place // 2, place % 2, there, here]
                state_lead, state_half = lead * to_state, HALF * to_state
                adjoint_lead, adjoint_half = lead * to_adjoint, HALF * to_adjoint
                response[place, 0, there, here] = mixed * (state_lead - cross_near * adjoint_half)
                response[place, 1, there, here] = series * (cross_near * state_lead + adjoint_half)
                response[place, 2, there, here] = -series * (state_half + cross_near * adjoint_lead)
                response[place, 3, there, here] = (square_ratio**7 * mixed) * (
                    adjoint_lead - cross_near * state_half
                )

    def couplings(group, summed):
        def pair_couplings(step, _):
            half = pairs - 1 - step
            if summed:

                @pl.when(step % 2 == 0)
                def _():
                    arrived = edge_in.at[:, :, pl.ds(0, 2 * pairs // classes * COL)]
                    sem = edge_recv.at[group * classes + half // 2]
                    pltpu.make_async_copy(arrived, arrived, sem).wait()

            for odd in (1, 0):
                lane = lane_of(half, odd)
                column = group * lanes + lane
                lane0 = column * COL
                here = pl.ds(pl.multiple_of(lane0, COL), COL)
                shifted = pl.ds(pl.multiple_of(lane0 + COL, COL), COL)
                after = pl.ds(pl.multiple_of(lane0 + 2 * COL, COL), COL)
                forward = [solve[1, there, here] for there in tiles]
                backward = [solve[2, there, here] for there in tiles]
                sides = []
                for field in range(2):
                    weights = [
                        [couple[field, d, s, there, here] for there in tiles]
                        for d in range(3)
                        for s in range(2)
                    ]
                    ahead_sum = [zero, zero]
                    behind_sum = [zero, zero]
                    scale = [jnp.ones((8, COL), jnp.float32)] * 2
                    for j in range(times):
                        own = [first[field, j, there, here] for there in tiles]
                        z_ahead, z_behind = in_z(own, *edge_rows(field * times + j, here))
                        for z in range(2):
                            there = tiles[z]
                            turned = twist[field, j, there, shifted]
                            x_ahead = jnp.where(left, turned, twist[field, j, there, after])
                            x_behind = jnp.where(left, twist[field, j, there, here], turned)
                            value = (
                                rhs[field, j, there, here]
                                + weights[0][z] * z_ahead[z]
                                + weights[1][z] * z_behind[z]
                                + weights[2][z] * x_ahead
                                + weights[3][z] * x_behind
                                + weights[4][z] * turn(own[z], 1, 1)
                                + weights[5][z] * turn(own[z], -1, 1)
                            )
                            rhs[field, j, there, here] = value
                            if summed:
                                ahead_sum[z] = value + forward[z] * ahead_sum[z]
                                behind_sum[z] = behind_sum[z] + scale[z] * value
                                if j < times - 1:
                                    scale[z] = scale[z] * backward[z]
                    sides.append((ahead_sum, behind_sum))
                if summed:
                    make_responses(column)
                    for z in range(2):
                        lead = solve[0, tiles[z], here]
                        block = z * lanes + lane
                        lot = groups + group
                        carry_out[lot, block, 0] = lead * sides[0][0][z] + HALF * sides[1][0][z]
                        carry_out[lot, block, 1] = lead * sides[1][1][z] - HALF * sides[0][1][z]
            return 0

        lax.fori_loop(0, pairs, pair_couplings, 0)

    for group in range(groups):
        couplings(group, True)

    def entries(group):
        def pair_entries(step, _):
            half = pairs - 1 - step

            for odd in (1, 0):
                lane = lane_of(half, odd)
                here = pl.ds(pl.multiple_of((group * lanes + lane) * COL, COL), COL)
                for z in range(2):
                    gain = solve[3, tiles[z], here]
                    for index in range(2):
                        entered[index, 8 + z * 8 : 16 + z * 8, here] = (
                            gain * solve[1 + index, tiles[z], here] * entry_in[group, z * lanes + lane, index]
                        )
            return 0

        lax.fori_loop(0, pairs, pair_entries, 0)

    for group in range(groups):
        for kind in range(classes):
            await_entry(group, kind)
        for lane in range(lanes):
            column = group * lanes + lane
            here = slice(column * COL, column * COL + COL)
            for side in range(2):
                line, edge, block = slice(15 * side, 15 * side + 1), slice(7 * side, 7 * side + 1), side * lanes + lane
                gain = solve[3, line, here]
                for index in range(2):
                    pack_out[side, index, column : column + 1, :] = (
                        gain * solve[1 + index, line, here] * entry_in[group, block, index, edge]
                    )
    pack_copies = [
        pltpu.make_async_remote_copy(
            src_ref=pack_out.at[1 - core],
            dst_ref=pack_in.at[core],
            send_sem=pack_send,
            recv_sem=pack_recv.at[0],
            device_id=pair,
        ),
        pltpu.make_async_remote_copy(
            src_ref=pack_out.at[core],
            dst_ref=pack_in.at[1 - core],
            send_sem=pack_send,
            recv_sem=pack_recv.at[1],
            device_id=beside,
        ),
    ]
    for copy in pack_copies:
        copy.start()
    for group in range(groups):
        entries(group)

    def unpack(side):
        for index in range(2):
            for column in range(columns):
                part = slice(column * COL, column * COL + COL)
                line = 7 + 17 * side
                entered[index, line : line + 1, part] = pack_in[side, index, column : column + 1, :]

    def second_sums(step, _):
        for k in range(4):
            column = step * 4 + k
            here, before, after = column_of(column), column_of(column + columns - 1), column_of(column + 1)
            lot = groups + column // lanes
            sides = [[], []]
            for index in range(2):
                own = [entered[index, 8 + z * 8 : 16 + z * 8, here] for z in range(2)]
                z_ahead, z_behind = in_z(own, zero, zero)
                for z in range(2):
                    centre = slice(8 + z * 8, 16 + z * 8)
                    sides[z].append(
                        (z_ahead[z], z_behind[z])
                        + in_plane(own[z], entered[index, centre, before], entered[index, centre, after])
                    )
            for z in range(2):
                block = z * lanes + column % lanes
                for direction in range(2):
                    total_sum = carry_out[lot, block, direction]
                    for place in range(6):
                        for index in range(2):
                            factor = response[place, 2 * direction + index, tiles[z], here]
                            total_sum = total_sum + factor * sides[z][index][place]
                    carry_out[lot, block, direction] = total_sum
        return 0

    lax.fori_loop(0, columns // 4, second_sums, 0)

    def add_rows(side):
        z, place, edge = side, 1 - side, (last_row if side else first_row)
        for column in range(columns):
            here = slice(column * COL, column * COL + COL)
            lot, block = groups + column // lanes, z * lanes + column % lanes
            enter = [
                jnp.broadcast_to(pack_in[side, index, column : column + 1, :], (8, COL)) for index in range(2)
            ]
            for direction in range(2):
                more = (
                    response[place, 2 * direction, tiles[z], here] * enter[0]
                    + response[place, 2 * direction + 1, tiles[z], here] * enter[1]
                )
                carry_out[lot, block, direction] = carry_out[lot, block, direction] + jnp.where(edge, more, 0.0)
        for group in range(groups):
            for half in range(pairs):
                for odd in range(2):
                    carry_copy(groups + group, z * lanes + lane_of(half, odd)).start()

    for outer in range(2):
        pack_copies[outer].wait_recv()
        for side in range(2):

            @pl.when(core == (side if outer else 1 - side))
            def _():
                add_rows(side)

    for side in range(2):
        unpack(side)

    def entered_values(step, _):
        for k in range(2):
            column_values(step * 2 + k)
        return 0

    def column_values(column):
        here = pl.ds(pl.multiple_of(column * COL, COL), COL)
        shifted = pl.ds(pl.multiple_of(column * COL + COL, COL), COL)

        def emit_all(ahead, behind, forward, backward, cross, emit):
            behinds = [behind]
            for _ in range(times - 1):
                behinds.append(behinds[-1] * backward)
            for j in range(times):
                emit(j, ahead + cross * behinds[times - 1 - j], behinds[times - 1 - j] - cross * ahead)
                if j < times - 1:
                    ahead = ahead * forward

        for z in range(2):

            def emit(j, state, adjoint):
                first[0, j, tiles[z], here] = state
                first[1, j, tiles[z], here] = adjoint
                twist[0, j, tiles[z], shifted] = turn(state, 64, 1)
                twist[1, j, tiles[z], shifted] = turn(adjoint, 64, 1)

            own = slice(8 + z * 8, 16 + z * 8)
            emit_all(
                entered[0, own, here],
                entered[1, own, here],
                solve[1, tiles[z], here],
                solve[2, tiles[z], here],
                solve[4, tiles[z], here],
                emit,
            )
        for side in range(2):

            def emit(j, state, adjoint):
                edge_in[side, j : j + 1, here] = state
                edge_in[side, times + j : times + j + 1, here] = adjoint

            line = slice(7 + 17 * side, 8 + 17 * side)
            forward = edge_in[side, 2 * times : 2 * times + 1, here]
            cross = edge_in[side, 2 * times + 1 : 2 * times + 2, here]
            emit_all(
                entered[0, line, here],
                entered[1, line, here],
                forward,
                forward * (ratio * ratio),
                cross,
                emit,
            )

    lax.fori_loop(0, columns // 2, entered_values, 0)
    def give_copy(column):
        part = pl.ds(pl.multiple_of(column * COL, COL), COL)
        return pltpu.make_async_remote_copy(
            src_ref=result.at[:, pair_times, :, part],
            dst_ref=given.at[:, :, :, part],
            send_sem=give_send,
            recv_sem=give_recv,
            device_id=pair,
        )

    def second_values(step, _):
        for k in range(2):
            column = step * 2 + k
            here = pl.ds(pl.multiple_of(column * COL, COL), COL)
            for z in range(2):

                def emit(j, state, adjoint):
                    result[0, j, tiles[z], here] = state
                    result[1, j, tiles[z], here] = adjoint

                solved(0, column, z, False, zero, zero, emit)
        for k in range(2):
            give_copy(step * 2 + k).start()
        return 0

    for group in range(groups):
        couplings(group, False)
        lax.fori_loop(group * lanes // 2, (group + 1) * lanes // 2, second_values, 0)
        if group == groups // 2 - 1:
            for other_group in range(groups):
                exchange(1, other_group)

    def twin_entry_copy(group):
        return pltpu.make_async_remote_copy(
            src_ref=entry_in.at[groups + group],
            dst_ref=twin_entry.at[group],
            send_sem=twin_entry_send,
            recv_sem=twin_entry_recv.at[group],
            device_id=pair,
        )

    def finish(group, first_line, entered_at, base_at, cross_at, gain_at, value_at):
        def finish_columns(step, _):
            for k in range(4):
                lane = step * 4 + k
                here = pl.ds(pl.multiple_of((group * lanes + lane) * COL, COL), COL)
                for z in range(2):
                    there = pl.ds(pl.multiple_of(first_line + z * 8, 8), 8)
                    forward = base_at(tiles[z], here)
                    backward = forward * (ratio * ratio)
                    cross = cross_at(tiles[z], here)
                    gain = gain_at(tiles[z], here)
                    forward_half, backward_half = forward, backward
                    for _ in range(half_times.bit_length() - 1):
                        forward_half = forward_half * forward_half
                        backward_half = backward_half * backward_half
                    ahead = entered_at(z * lanes + lane, 0)
                    ahead = jnp.where(core == 1, forward_half * ahead, ahead)
                    behind = entered_at(z * lanes + lane, 1)
                    behind = jnp.where(core == 1, behind, backward_half * behind)
                    behinds = []
                    for _ in range(half_times):
                        behind = backward * behind
                        behinds.append(behind)
                    for j in range(half_times):
                        ahead = forward * ahead
                        behind = behinds[half_times - 1 - j]
                        both_out[0, j, there, here] = gain * (value_at(0, j, tiles[z], here) + (ahead + cross * behind))
                        both_out[1, j, there, here] = gain * (value_at(1, j, tiles[z], here) + (behind - cross * ahead))
            return 0

        lax.fori_loop(0, lanes // 4, finish_columns, 0)

    def drain(ref, semaphore):
        pltpu.make_async_copy(ref, ref, semaphore).wait()

    for group in range(groups):
        for kind in range(classes):
            await_entry(groups + group, kind)
        twin_entry_copy(group).start()
        finish(
            group,
            core * 16,
            lambda block, index: entry_in[groups + group, block, index],
            lambda there, here: solve[1, there, here],
            lambda there, here: solve[4, there, here],
            lambda there, here: solve[3, there, here],
            lambda field, j, there, here: result[field, core * half_times + j, there, here],
        )
    drain(twin, twin_recv)
    drain(given, give_recv)
    for group in range(groups):
        drain(twin_entry.at[group], twin_entry_recv.at[group])
        finish(
            group,
            16 - core * 16,
            lambda block, index: twin_entry[group, block, index],
            lambda there, here: twin[0, there, here],
            lambda there, here: twin[1, there, here],
            lambda there, here: twin[2, there, here],
            lambda field, j, there, here: given[field, j, there, here],
        )

    base_copy.wait_send()

    @pl.when(core == 1)
    def _():
        drain(rim.at[pl.ds(0, 2)], kappa_send)

    drain(rhs.at[:, own_times], rhs_send)
    drain(carry_out, carry_send)
    drain(entry_out, entry_send)
    drain(edge_out, edge_send)
    drain(pack_out, pack_send)
    drain(result.at[:, own_times], give_send)
    drain(twin, twin_send)
    drain(twin_entry, twin_entry_send)


def write_kernel(both, state_out, adjoint_out, semaphore):
    copies = [
        pltpu.make_async_copy(both.at[field], target, semaphore.at[field])
        for field, target in enumerate((state_out, adjoint_out))
    ]
    for copy in copies:
        copy.start()
    for copy in copies:
        copy.wait()


def solution(mesh):
    ranks = mesh.shape["tm"]
    slabs = mesh.shape["gz"]
    chips = ranks // 2

    def body(state_rhs, adjoint_rhs, diffusivity, velocity):
        steps, depth, cells = state_rhs.shape
        times = 2 * steps
        columns = cells // COL
        groups = 2 * columns // chips
        f32 = jnp.float32
        dma = pltpu.SemaphoreType.DMA
        anywhere = pl.BlockSpec(memory_space=pl.ANY)
        exchanged = pltpu.VMEM((2 * groups, chips, 2, 8, COL), f32)
        call = pl.pallas_call(
            functools.partial(kernel, chips, slabs, cells, times),
            out_shape=pltpu.VMEM((2, steps, depth, cells), f32),
            in_specs=[anywhere] * 4,
            out_specs=pl.BlockSpec(memory_space=pltpu.VMEM),
            scratch_shapes=[
                pltpu.VMEM((2, times, 16, cells), f32),
                pltpu.VMEM((2, times, 16, cells), f32),
                pltpu.VMEM((2, times, 16, cells + 2 * COL), f32),
                pltpu.VMEM((2, times, 16, cells), f32),
                pltpu.VMEM((32, cells), f32),
                pltpu.VMEM((8, cells), f32),
                pltpu.VMEM((3, 8, cells // 8), f32),
                pltpu.VMEM((3, 16, cells), f32),
                pltpu.VMEM((2, 3, 2, 16, cells), f32),
                pltpu.VMEM((6, 16, cells), f32),
                pltpu.VMEM((groups, chips, 2, 8, COL), f32),
                pltpu.VMEM((groups, 2, 8, COL), f32),
                pltpu.VMEM((groups, chips + 1, 2, 8, COL), f32),
                exchanged,
                exchanged,
                exchanged,
                exchanged,
                pltpu.VMEM((2, 3 * times, cells), f32),
                pltpu.VMEM((2, 3 * times, cells), f32),
                pltpu.VMEM((6, 4, 16, cells), f32),
                pltpu.VMEM((2, 32, cells), f32),
                pltpu.VMEM((2, 2, columns, COL), f32),
                pltpu.VMEM((2, 2, columns, COL), f32),
                pltpu.VMEM((3, 16, cells), f32),
                pltpu.VMEM((2, steps, 16, cells), f32),
                pltpu.VMEM((groups, chips, 2, 8, COL), f32),
                dma((3,)),
                dma,
                dma((groups,)),
                dma,
                dma,
                dma((2,)),
                dma,
                dma((2 * groups,)),
                dma,
                dma((2 * groups, 2)),
                dma,
                dma((2 * groups,)),
                dma,
                dma((2,)),
                dma,
                dma,
                dma,
                dma((groups,)),
                dma,
                dma,
            ],
            compiler_params=pltpu.CompilerParams(
                collective_id=0, has_side_effects=True, vmem_limit_bytes=48 * 1024 * 1024
            ),
            cost_estimate=pl.CostEstimate(
                flops=60 * state_rhs.size, bytes_accessed=20 * state_rhs.size, transcendentals=0
            ),
        )
        held = [
            pltpu.with_memory_space_constraint(array, pltpu.HBM)
            for array in (state_rhs, adjoint_rhs, diffusivity, velocity)
        ]
        both = call(*held)
        write = pl.pallas_call(
            write_kernel,
            out_shape=[jax.ShapeDtypeStruct(state_rhs.shape, f32)] * 2,
            in_specs=[pl.BlockSpec(memory_space=pltpu.VMEM)],
            out_specs=[anywhere] * 2,
            scratch_shapes=[dma((2,))],
            compiler_params=pltpu.CompilerParams(vmem_limit_bytes=48 * 1024 * 1024),
        )
        return tuple(write(pltpu.with_memory_space_constraint(both, pltpu.VMEM)))

    placed = (P("tm", "gz", None), P("tm", "gz", None), P("gz", None), P(None, "gz", None))
    return jax.shard_map(
        body,
        mesh=mesh,
        in_specs=placed,
        out_specs=(P("tm", "gz", None), P("tm", "gz", None)),
        check_vma=False,
    )
```

```python
import functools
import math

import jax
import jax.numpy as jnp
from jax import lax
from jax.experimental import pallas as pl
from jax.experimental.pallas import tpu as pltpu
from jax.sharding import PartitionSpec as P

NY = 64
COL = 128
ALPHA = 0.1
HALF = 0.5


def turn(value, shift, axis):
    return pltpu.roll(value, (-shift) % value.shape[axis], axis)


def kernel(
    chips, slabs, cells, times,
    state_hbm, adjoint_hbm, kappa_hbm, speed_hbm,
    both_out,
    rhs, first, twist, result, kappa, edge_row, rim, speed, couple, solve, power, base, growth,
    carry_out, carry_in, entry_out, entry_in, edge_out, edge_in,
    response, entered, pack_out, pack_in, twin, given, twin_entry,
    load_sem, rhs_send, rhs_recv, kappa_send, kappa_recv, base_sem,
    carry_send, carry_recv, entry_send, entry_recv,
    edge_send, edge_recv, pack_send, pack_recv, twin_send, twin_recv, twin_entry_send, twin_entry_recv, give_send, give_recv,
):
    half_times = times // 2
    lanes = chips // 2
    columns = cells // COL
    groups = columns // lanes
    width = lanes * COL
    total = chips * times
    ratio = ALPHA ** (1.0 / total)

    me = lax.axis_index("tm")
    slab = lax.axis_index("gz")
    chip = me // 2
    core = me % 2
    pair = {"tm": chip * 2 + 1 - core, "gz": slab}
    beside = {"tm": chip * 2 + 1 - core, "gz": (slab + slabs + 2 * core - 1) % slabs}

    behind_same = {"tm": me, "gz": (slab + slabs - 1) % slabs}

    def peer(other):
        return {"tm": other * 2 + 1 - core, "gz": slab}

    rows = pl.ds(pl.multiple_of(core * 16, 16), 16)
    rows_pair = pl.ds(pl.multiple_of(16 - core * 16, 16), 16)
    own_times = pl.ds(core * half_times, half_times)
    pair_times = pl.ds((1 - core) * half_times, half_times)

    def lane_of(half, odd):
        if lanes != 8:
            return (chip + 2 * half + odd) % lanes
        outer = half % 3 == 0
        if isinstance(half, int):
            move_x = 2 - 2 * (half // 3) if outer else 1 + 2 * odd
            move_y = odd if outer else half - 1
        else:
            move_x = jnp.where(outer, 2 - 2 * (half // 3), 1 + 2 * odd)
            move_y = jnp.where(outer, odd, half - 1)
        return ((chip // 4 + move_y) % 2) * 4 + (chip % 4 + move_x) % 4

    pairs = lanes // 2
    classes = (pairs + 1) // 2

    def tile8(start):
        return pl.ds(pl.multiple_of(start, 8), 8)

    barrier = pltpu.get_barrier_semaphore()
    for half in range(lanes // 2):
        for odd in range(2):
            for z in range(2):
                target = peer(z * lanes + lane_of(half, odd))
                pl.semaphore_signal(barrier, inc=1, device_id=target)
    pl.semaphore_signal(barrier, inc=1, device_id=beside)

    @pl.when(core == 1)
    def _():
        pl.semaphore_signal(barrier, inc=1, device_id={"tm": me, "gz": (slab + 1) % slabs})

    loads = [
        pltpu.make_async_copy(kappa_hbm.at[rows], kappa.at[pl.ds(8, 16)], load_sem.at[0]),
        pltpu.make_async_copy(
            kappa_hbm.at[tile8(16 - 8 * core)], kappa.at[tile8(24 - 24 * core)], load_sem.at[0]
        ),
        pltpu.make_async_copy(kappa_hbm.at[pl.ds(0, 8)], edge_row, load_sem.at[0]),
        pltpu.make_async_copy(speed_hbm.at[:, rows], speed, load_sem.at[1]),
        pltpu.make_async_copy(state_hbm.at[:, rows], rhs.at[0, own_times], load_sem.at[2]),
        pltpu.make_async_copy(adjoint_hbm.at[:, rows], rhs.at[1, own_times], load_sem.at[2]),
    ]
    for load in loads:
        load.start()

    def kappa_copy(side):
        return pltpu.make_async_remote_copy(
            src_ref=rim.at[side],
            dst_ref=rim.at[2],
            send_sem=kappa_send,
            recv_sem=kappa_recv,
            device_id=beside if side else behind_same,
        )

    def rhs_copies(group):
        part = slice(group * width, group * width + width)
        return [
            pltpu.make_async_remote_copy(
                src_ref=source.at[:, rows_pair, part],
                dst_ref=rhs.at[field, own_times, :, part],
                send_sem=rhs_send,
                recv_sem=rhs_recv.at[group],
                device_id=pair,
            )
            for field, source in enumerate((state_hbm, adjoint_hbm))
        ]

    lane = lax.broadcasted_iota(jnp.int32, (8, COL), 1)
    row = lax.broadcasted_iota(jnp.int32, (8, COL), 0)
    left = lane < 64
    first_row = row == 0
    last_row = row == 7

    zero = jnp.zeros((8, COL), jnp.float32)
    for field in range(2):
        for step in range(times):
            for z in range(2):
                twist[field, step, z * 8 : z * 8 + 8, :COL] = zero
                twist[field, step, z * 8 : z * 8 + 8, cells + COL :] = zero

    pltpu.make_async_copy(kappa.at[pl.ds(0, 32)], kappa.at[pl.ds(0, 32)], load_sem.at[0]).wait()
    piece_width = cells // 8

    @pl.when(core == 1)
    def _():
        for side, source, line in ((0, edge_row, 0), (1, kappa, 23)):
            for piece in range(8):
                part = slice(piece * piece_width, piece * piece_width + piece_width)
                rim[side, piece : piece + 1, :] = source[line : line + 1, part]

    loads[3].wait()

    def coefficients(k, z):
        there = pl.ds(pl.multiple_of(z * 8, 8), 8)
        centre = pl.ds(pl.multiple_of(8 + z * 8, 8), 8)
        below = pl.ds(pl.multiple_of(z * 8, 8), 8)
        above = pl.ds(pl.multiple_of(16 + z * 8, 8), 8)
        lane0 = pl.multiple_of(k * COL, COL)
        here = pl.ds(lane0, COL)
        before = pl.ds(pl.multiple_of(((k + cells // COL - 1) % (cells // COL)) * COL, COL), COL)
        after = pl.ds(pl.multiple_of(((k + 1) % (cells // COL)) * COL, COL), COL)
        x_place = k * 2 + lane // NY
        y_place = lane % NY
        z_place = slab * 32 + core * 16 + z * 8 + row
        own = kappa[centre, here]
        turned = turn(own, 64, 1)
        x_ahead = jnp.where(left, turned, turn(kappa[centre, after], 64, 1))
        x_behind = jnp.where(left, turn(kappa[centre, before], 64, 1), turned)
        z_ahead = jnp.where(
            last_row, turn(kappa[above, here], 1, 0), turn(own, 1, 0)
        )
        z_behind = jnp.where(
            first_row, turn(kappa[below, here], -1, 0), turn(own, -1, 0)
        )
        diagonal = jnp.zeros((8, COL), jnp.float32)
        for direction, (ahead, behind, place, count, component) in enumerate(
            (
                (z_ahead, z_behind, z_place, slabs * 32, 2),
                (x_ahead, x_behind, x_place, cells // NY, 0),
                (turn(own, 1, 1), turn(own, -1, 1), y_place, NY, 1),
            )
        ):
            has_ahead = place < count - 1
            has_behind = place > 0
            face_ahead = jnp.where(has_ahead, 0.5 * (own + ahead), own)
            face_behind = jnp.where(has_behind, 0.5 * (own + behind), own)
            diagonal = diagonal + face_ahead + face_behind
            drift = 0.5 * speed[component, there, here]
            couple[0, direction, 0, there, here] = jnp.where(has_ahead, face_ahead - drift, 0.0)
            couple[0, direction, 1, there, here] = jnp.where(has_behind, face_behind + drift, 0.0)
            couple[1, direction, 0, there, here] = jnp.where(has_ahead, face_ahead + drift, 0.0)
            couple[1, direction, 1, there, here] = jnp.where(has_behind, face_behind - drift, 0.0)
        large = 1.0 + diagonal
        over = 1.0 / (large * ratio)
        minus = ((large - ratio) * (large - ratio) + HALF * HALF) * over
        plus = minus + 4.0
        root = 2.0 / (minus + 2.0 + jnp.sqrt(minus * plus))
        lead = large - ratio * root
        gain = root * over / (1.0 - root * root)
        solve[0, there, here] = lead
        solve[1, there, here] = root * (1.0 / ratio)
        solve[2, there, here] = root * ratio
        solve[3, there, here] = gain
        solve[4, there, here] = HALF / lead
        solve[5, there, here] = ratio * (1.0 - root * root) / root
        for index, base in ((0, root * (1.0 / ratio)), (1, root * ratio)):
            square = base * base
            fourth = square * square
            power[k // lanes, z * lanes + k % lanes, index] = fourth * fourth

    def inner_coefficients(step, _):
        for k in range(4):
            coefficients(step * 4 + k, 1 - core)
        return 0

    def outer_coefficients(step, _):
        for k in range(8):
            coefficients(step * 8 + k, core)
        return 0

    pl.semaphore_wait(barrier, chips + 1 + core)

    @pl.when(core == 1)
    def _():
        for side in range(2):
            kappa_copy(side).start()

    for group in range(groups):
        for copy in rhs_copies(group):
            copy.start()

    lax.fori_loop(0, cells // COL // 4, inner_coefficients, 0)
    pltpu.make_async_copy(rhs.at[:, own_times], rhs.at[:, own_times], load_sem.at[2]).wait()
    kappa_copy(1).wait_recv()
    for side in range(2):

        @pl.when(core == side)
        def _():
            for piece in range(8):
                part = slice(piece * piece_width, piece * piece_width + piece_width)
                kappa[7 + 17 * side : 8 + 17 * side, part] = rim[2, piece : piece + 1, :]

    lax.fori_loop(0, cells // COL // 8, outer_coefficients, 0)

    def carry_copy(lot, other):
        return pltpu.make_async_remote_copy(
            src_ref=carry_out.at[lot, other],
            dst_ref=carry_in.at[lot, chip],
            send_sem=carry_send,
            recv_sem=carry_recv.at[lot],
            device_id=peer(other),
        )

    def entry_copy(lot, other, kind):
        return pltpu.make_async_remote_copy(
            src_ref=entry_out.at[lot, other],
            dst_ref=entry_in.at[lot, chip],
            send_sem=entry_send,
            recv_sem=entry_recv.at[lot, kind],
            device_id=peer(other),
        )

    def await_entry(lot, kind):
        blocks = entry_in.at[lot, pl.ds(0, chips // classes)]
        pltpu.make_async_copy(blocks, blocks, entry_recv.at[lot, kind]).wait()

    def powers(group):
        for direction in range(2):
            factor = base[group, direction]
            run = factor
            for step in range(1, chips + 1):
                growth[group, step, direction] = run
                run = run * factor

    def exchange(sweep, group):
        lot = sweep * groups + group

        arrived = carry_in.at[lot]
        pltpu.make_async_copy(arrived, arrived, carry_recv.at[lot]).wait()
        for direction, wrap in ((0, ALPHA), (1, 1.0 / ALPHA)):
            factor = growth[group, 1, direction]
            order = range(chips) if direction == 0 else range(chips - 1, -1, -1)
            run = None
            before = []
            for place in order:
                before.append(run)
                carry = carry_in[lot, place, direction]
                run = carry if run is None else carry + factor * run
            start = wrap * (run / (1.0 - wrap * growth[group, chips, direction]))
            for step, place in enumerate(order):
                value = start
                if step:
                    value = before[step] + start * growth[group, step, direction]
                entry_out[lot, place, direction] = value
        for half in range(pairs):
            for odd in range(2):
                for z in range(2):
                    other = z * lanes + lane_of(half, odd)
                    entry_copy(lot, other, half // 2).start()

    def sums(values, forward, backward):
        ahead = values[0]
        behind = values[-1]
        for step in range(1, times):
            ahead = values[step] + forward * ahead
            behind = values[times - 1 - step] + backward * behind
        return ahead, behind

    base_copy = pltpu.make_async_remote_copy(
        src_ref=power.at[:, chip],
        dst_ref=base,
        send_sem=base_sem.at[0],
        recv_sem=base_sem.at[1],
        device_id=pair,
    )
    base_copy.start()
    twin_copies = [
        pltpu.make_async_remote_copy(
            src_ref=solve.at[source],
            dst_ref=twin.at[target],
            send_sem=twin_send,
            recv_sem=twin_recv,
            device_id=pair,
        )
        for target, source in enumerate((1, 4, 3))
    ]

    def first_sums(group):
        def quad_sums(step, _):
            places = [(2 * step + more, odd) for more in range(2) for odd in range(2)]
            for half, odd in places:
                lane = lane_of(half, odd)
                here = pl.ds(pl.multiple_of(group * width + lane * COL, COL), COL)
                for z in range(2):
                    there = slice(z * 8, z * 8 + 8)
                    lead = solve[0, there, here]
                    forward = solve[1, there, here]
                    backward = solve[2, there, here]
                    sides = [
                        sums([rhs[field, j, there, here] for j in range(times)], forward, backward)
                        for field in range(2)
                    ]
                    block = z * lanes + lane
                    carry_out[group, block, 0] = lead * sides[0][0] + HALF * sides[1][0]
                    carry_out[group, block, 1] = lead * sides[1][1] - HALF * sides[0][1]
            for half, odd in places:
                for z in range(2):
                    carry_copy(group, z * lanes + lane_of(half, odd)).start()
            return 0

        lax.fori_loop(0, pairs // 2, quad_sums, 0)

    for group in range(groups):
        arrived = rhs.at[:, own_times, :, slice(0, width)]
        pltpu.make_async_copy(arrived, arrived, rhs_recv.at[group]).wait()
        first_sums(group)
    for copy in twin_copies:
        copy.start()
    base_copy.wait_recv()
    for group in range(groups):
        powers(group)
    def solved(group, lane, z, scaled, ahead, back, emit):
        here = pl.ds(pl.multiple_of(group * width + lane * COL, COL), COL)
        there = slice(z * 8, z * 8 + 8)
        lead = solve[0, there, here]
        forward = solve[1, there, here]
        backward = solve[2, there, here]
        gain = solve[3, there, here]
        cross = solve[4, there, here]
        plain = solve[5, there, here]
        backs = [None] * times
        for j in reversed(range(times)):
            backs[j] = backward * back
            back = (
                lead * rhs[1, j, there, here] - HALF * rhs[0, j, there, here] + backs[j]
            )
        for j in range(times):
            adjoint = rhs[1, j, there, here]
            ahead = lead * rhs[0, j, there, here] + HALF * adjoint + forward * ahead
            state = ahead + cross * backs[j]
            adjoint = backs[j] - cross * ahead + plain * adjoint
            if scaled:
                state, adjoint = gain * state, gain * adjoint
            emit(j, state, adjoint)

    def edge_copies(column, mark):
        part = pl.ds(pl.multiple_of(column * COL, COL), COL)
        return (
            pltpu.make_async_remote_copy(
                src_ref=edge_out.at[core, :, part],
                dst_ref=edge_in.at[1 - core, :, part],
                send_sem=edge_send,
                recv_sem=edge_recv.at[mark],
                device_id=beside,
            ),
            pltpu.make_async_remote_copy(
                src_ref=edge_out.at[1 - core, :, part],
                dst_ref=edge_in.at[core, :, part],
                send_sem=edge_send,
                recv_sem=edge_recv.at[mark],
                device_id=pair,
            ),
        )

    def first_values(group):
        def pair_values(step, _):
            half = pairs - 1 - step
            for odd in (1, 0):
                lane = lane_of(half, odd)
                column = group * lanes + lane
                here = pl.ds(pl.multiple_of(column * COL, COL), COL)
                shifted = pl.ds(pl.multiple_of(column * COL + COL, COL), COL)
                for z in range(2):

                    def emit(j, state, adjoint):
                        first[0, j, z * 8 : z * 8 + 8, here] = state
                        first[1, j, z * 8 : z * 8 + 8, here] = adjoint
                        twist[0, j, z * 8 : z * 8 + 8, shifted] = turn(state, 64, 1)
                        twist[1, j, z * 8 : z * 8 + 8, shifted] = turn(adjoint, 64, 1)
                        edge = slice(7 * z, 7 * z + 1)
                        edge_out[z, j : j + 1, here] = state[edge]
                        edge_out[z, times + j : times + j + 1, here] = adjoint[edge]

                    solved(group, lane, z, True, zero, zero, emit)
                    line = z * 15
                    edge_out[z, 2 * times : 2 * times + 1, here] = solve[1, line : line + 1, here]
                    edge_out[z, 2 * times + 1 : 2 * times + 2, here] = solve[4, line : line + 1, here]
            for odd in (1, 0):
                for copy in edge_copies(group * lanes + lane_of(half, odd), group * classes + half // 2):
                    copy.start()
            return 0

        lax.fori_loop(0, pairs, pair_values, 0)

    for group in range(groups):
        first_values(group)

    for group in range(groups):
        exchange(0, group)

    tiles = (slice(0, 8), slice(8, 16))

    def column_of(column):
        return pl.ds(pl.multiple_of((column % columns) * COL, COL), COL)

    def in_z(own, below, above):
        up = [turn(value, 1, 0) for value in own]
        down = [turn(value, -1, 0) for value in own]
        return (
            [jnp.where(last_row, up[1], up[0]), jnp.where(last_row, above, up[1])],
            [jnp.where(first_row, below, down[0]), jnp.where(first_row, down[0], down[1])],
        )

    def in_plane(own, before, after):
        turned = turn(own, 64, 1)
        return (
            jnp.where(left, turned, turn(after, 64, 1)),
            jnp.where(left, turn(before, 64, 1), turned),
            turn(own, 1, 1),
            turn(own, -1, 1),
        )

    def edge_rows(line, here):
        return [jnp.broadcast_to(edge_in[side, line : line + 1, here], (8, COL)) for side in range(2)]

    def make_responses(column):
        here, before, after = column_of(column), column_of(column + columns - 1), column_of(column + 1)
        sides = []
        for index, line in ((1, 2 * times), (4, 2 * times + 1)):
            own = [solve[index, there, here] for there in tiles]
            z_ahead, z_behind = in_z(own, *edge_rows(line, here))
            sides.append(
                [
                    (z_ahead[z], z_behind[z])
                    + in_plane(own[z], solve[index, tiles[z], before], solve[index, tiles[z], after])
                    for z in range(2)
                ]
            )
        square_ratio = ratio * ratio
        for z in range(2):
            there = tiles[z]
            lead = solve[0, there, here]
            base_own = solve[1, there, here]
            square_own = base_own * base_own
            fourth_own = square_own * square_own
            for place in range(6):
                base_near, cross_near = sides[0][z][place], sides[1][z][place]
                square_near = base_near * base_near
                mixed = (base_own + base_near) * (square_own + square_near)
                mixed = mixed * (fourth_own + square_near * square_near)
                product = square_ratio * (base_own * base_near)
                square = product * product
                series = (1.0 + product) * (1.0 + square) * (1.0 + square * square)
                to_state = couple[0, place // 2, place % 2, there, here]
                to_adjoint = couple[1, place // 2, place % 2, there, here]
                state_lead, state_half = lead * to_state, HALF * to_state
                adjoint_lead, adjoint_half = lead * to_adjoint, HALF * to_adjoint
                response[place, 0, there, here] = mixed * (state_lead - cross_near * adjoint_half)
                response[place, 1, there, here] = series * (cross_near * state_lead + adjoint_half)
                response[place, 2, there, here] = -series * (state_half + cross_near * adjoint_lead)
                response[place, 3, there, here] = (square_ratio**7 * mixed) * (
                    adjoint_lead - cross_near * state_half
                )

    def couplings(group, summed):
        def pair_couplings(step, _):
            half = pairs - 1 - step
            if summed:

                @pl.when(step % 2 == 0)
                def _():
                    arrived = edge_in.at[:, :, pl.ds(0, 2 * pairs // classes * COL)]
                    sem = edge_recv.at[group * classes + half // 2]
                    pltpu.make_async_copy(arrived, arrived, sem).wait()

            for odd in (1, 0):
                lane = lane_of(half, odd)
                column = group * lanes + lane
                lane0 = column * COL
                here = pl.ds(pl.multiple_of(lane0, COL), COL)
                shifted = pl.ds(pl.multiple_of(lane0 + COL, COL), COL)
                after = pl.ds(pl.multiple_of(lane0 + 2 * COL, COL), COL)
                forward = [solve[1, there, here] for there in tiles]
                backward = [solve[2, there, here] for there in tiles]
                sides = []
                for field in range(2):
                    weights = [
                        [couple[field, d, s, there, here] for there in tiles]
                        for d in range(3)
                        for s in range(2)
                    ]
                    ahead_sum = [zero, zero]
                    behind_sum = [zero, zero]
                    scale = [jnp.ones((8, COL), jnp.float32)] * 2
                    for j in range(times):
                        own = [first[field, j, there, here] for there in tiles]
                        z_ahead, z_behind = in_z(own, *edge_rows(field * times + j, here))
                        for z in range(2):
                            there = tiles[z]
                            turned = twist[field, j, there, shifted]
                            x_ahead = jnp.where(left, turned, twist[field, j, there, after])
                            x_behind = jnp.where(left, twist[field, j, there, here], turned)
                            value = (
                                rhs[field, j, there, here]
                                + weights[0][z] * z_ahead[z]
                                + weights[1][z] * z_behind[z]
                                + weights[2][z] * x_ahead
                                + weights[3][z] * x_behind
                                + weights[4][z] * turn(own[z], 1, 1)
                                + weights[5][z] * turn(own[z], -1, 1)
                            )
                            rhs[field, j, there, here] = value
                            if summed:
                                ahead_sum[z] = value + forward[z] * ahead_sum[z]
                                behind_sum[z] = behind_sum[z] + scale[z] * value
                                if j < times - 1:
                                    scale[z] = scale[z] * backward[z]
                    sides.append((ahead_sum, behind_sum))
                if summed:
                    make_responses(column)
                    for z in range(2):
                        lead = solve[0, tiles[z], here]
                        block = z * lanes + lane
                        lot = groups + group
                        carry_out[lot, block, 0] = lead * sides[0][0][z] + HALF * sides[1][0][z]
                        carry_out[lot, block, 1] = lead * sides[1][1][z] - HALF * sides[0][1][z]
            return 0

        lax.fori_loop(0, pairs, pair_couplings, 0)

    for group in range(groups):
        couplings(group, True)

    def entries(group):
        def pair_entries(step, _):
            half = pairs - 1 - step

            for odd in (1, 0):
                lane = lane_of(half, odd)
                here = pl.ds(pl.multiple_of((group * lanes + lane) * COL, COL), COL)
                for z in range(2):
                    gain = solve[3, tiles[z], here]
                    for index in range(2):
                        entered[index, 8 + z * 8 : 16 + z * 8, here] = (
                            gain * solve[1 + index, tiles[z], here] * entry_in[group, z * lanes + lane, index]
                        )
            return 0

        lax.fori_loop(0, pairs, pair_entries, 0)

    for group in range(groups):
        for kind in range(classes):
            await_entry(group, kind)
        for lane in range(lanes):
            column = group * lanes + lane
            here = slice(column * COL, column * COL + COL)
            for side in range(2):
                line, edge, block = slice(15 * side, 15 * side + 1), slice(7 * side, 7 * side + 1), side * lanes + lane
                gain = solve[3, line, here]
                for index in range(2):
                    pack_out[side, index, column : column + 1, :] = (
                        gain * solve[1 + index, line, here] * entry_in[group, block, index, edge]
                    )
    pack_copies = [
        pltpu.make_async_remote_copy(
            src_ref=pack_out.at[1 - core],
            dst_ref=pack_in.at[core],
            send_sem=pack_send,
            recv_sem=pack_recv.at[0],
            device_id=pair,
        ),
        pltpu.make_async_remote_copy(
            src_ref=pack_out.at[core],
            dst_ref=pack_in.at[1 - core],
            send_sem=pack_send,
            recv_sem=pack_recv.at[1],
            device_id=beside,
        ),
    ]
    for copy in reversed(pack_copies):
        copy.start()
    for group in range(groups):
        entries(group)

    def unpack(side):
        for index in range(2):
            for column in range(columns):
                part = slice(column * COL, column * COL + COL)
                line = 7 + 17 * side
                entered[index, line : line + 1, part] = pack_in[side, index, column : column + 1, :]

    def second_sums(step, _):
        for k in range(4):
            column = step * 4 + k
            here, before, after = column_of(column), column_of(column + columns - 1), column_of(column + 1)
            lot = groups + column // lanes
            sides = [[], []]
            for index in range(2):
                own = [entered[index, 8 + z * 8 : 16 + z * 8, here] for z in range(2)]
                z_ahead, z_behind = in_z(own, zero, zero)
                for z in range(2):
                    centre = slice(8 + z * 8, 16 + z * 8)
                    sides[z].append(
                        (z_ahead[z], z_behind[z])
                        + in_plane(own[z], entered[index, centre, before], entered[index, centre, after])
                    )
            for z in range(2):
                block = z * lanes + column % lanes
                for direction in range(2):
                    total_sum = carry_out[lot, block, direction]
                    for place in range(6):
                        for index in range(2):
                            factor = response[place, 2 * direction + index, tiles[z], here]
                            total_sum = total_sum + factor * sides[z][index][place]
                    carry_out[lot, block, direction] = total_sum
        return 0

    lax.fori_loop(0, columns // 4, second_sums, 0)

    def add_rows(side):
        z, place, edge = side, 1 - side, (last_row if side else first_row)
        for column in range(columns):
            here = slice(column * COL, column * COL + COL)
            lot, block = groups + column // lanes, z * lanes + column % lanes
            enter = [
                jnp.broadcast_to(pack_in[side, index, column : column + 1, :], (8, COL)) for index in range(2)
            ]
            for direction in range(2):
                more = (
                    response[place, 2 * direction, tiles[z], here] * enter[0]
                    + response[place, 2 * direction + 1, tiles[z], here] * enter[1]
                )
                carry_out[lot, block, direction] = carry_out[lot, block, direction] + jnp.where(edge, more, 0.0)
        for group in range(groups):
            for half in range(pairs):
                for odd in range(2):
                    carry_copy(groups + group, z * lanes + lane_of(half, odd)).start()

    for outer in range(2):
        pack_copies[outer].wait_recv()
        for side in range(2):

            @pl.when(core == (side if outer else 1 - side))
            def _():
                add_rows(side)

    for side in range(2):
        unpack(side)

    def entered_values(step, _):
        for k in range(2):
            column_values(step * 2 + k)
        return 0

    def column_values(column):
        here = pl.ds(pl.multiple_of(column * COL, COL), COL)
        shifted = pl.ds(pl.multiple_of(column * COL + COL, COL), COL)

        def emit_all(ahead, behind, forward, backward, cross, emit):
            behinds = [behind]
            for _ in range(times - 1):
                behinds.append(behinds[-1] * backward)
            for j in range(times):
                emit(j, ahead + cross * behinds[times - 1 - j], behinds[times - 1 - j] - cross * ahead)
                if j < times - 1:
                    ahead = ahead * forward

        for z in range(2):

            def emit(j, state, adjoint):
                first[0, j, tiles[z], here] = state
                first[1, j, tiles[z], here] = adjoint
                twist[0, j, tiles[z], shifted] = turn(state, 64, 1)
                twist[1, j, tiles[z], shifted] = turn(adjoint, 64, 1)

            own = slice(8 + z * 8, 16 + z * 8)
            emit_all(
                entered[0, own, here],
                entered[1, own, here],
                solve[1, tiles[z], here],
                solve[2, tiles[z], here],
                solve[4, tiles[z], here],
                emit,
            )
        for side in range(2):

            def emit(j, state, adjoint):
                edge_in[side, j : j + 1, here] = state
                edge_in[side, times + j : times + j + 1, here] = adjoint

            line = slice(7 + 17 * side, 8 + 17 * side)
            forward = edge_in[side, 2 * times : 2 * times + 1, here]
            cross = edge_in[side, 2 * times + 1 : 2 * times + 2, here]
            emit_all(
                entered[0, line, here],
                entered[1, line, here],
                forward,
                forward * (ratio * ratio),
                cross,
                emit,
            )

    lax.fori_loop(0, columns // 2, entered_values, 0)
    def give_copy(column):
        part = pl.ds(pl.multiple_of(column * COL, COL), COL)
        return pltpu.make_async_remote_copy(
            src_ref=result.at[:, pair_times, :, part],
            dst_ref=given.at[:, :, :, part],
            send_sem=give_send,
            recv_sem=give_recv,
            device_id=pair,
        )

    def second_values(step, _):
        for k in range(2):
            column = step * 2 + k
            here = pl.ds(pl.multiple_of(column * COL, COL), COL)
            for z in range(2):

                def emit(j, state, adjoint):
                    result[0, j, tiles[z], here] = state
                    result[1, j, tiles[z], here] = adjoint

                solved(0, column, z, False, zero, zero, emit)
        for k in range(2):
            give_copy(step * 2 + k).start()
        return 0

    for group in range(groups):
        couplings(group, False)
        lax.fori_loop(group * lanes // 2, (group + 1) * lanes // 2, second_values, 0)
        if group == groups // 2 - 1:
            for other_group in range(groups):
                exchange(1, other_group)

    def twin_entry_copy(group):
        return pltpu.make_async_remote_copy(
            src_ref=entry_in.at[groups + group],
            dst_ref=twin_entry.at[group],
            send_sem=twin_entry_send,
            recv_sem=twin_entry_recv.at[group],
            device_id=pair,
        )

    def finish(group, first_line, entered_at, base_at, cross_at, gain_at, value_at):
        def finish_columns(step, _):
            for k in range(4):
                lane = step * 4 + k
                here = pl.ds(pl.multiple_of((group * lanes + lane) * COL, COL), COL)
                for z in range(2):
                    there = pl.ds(pl.multiple_of(first_line + z * 8, 8), 8)
                    forward = base_at(tiles[z], here)
                    backward = forward * (ratio * ratio)
                    cross = cross_at(tiles[z], here)
                    gain = gain_at(tiles[z], here)
                    forward_half, backward_half = forward, backward
                    for _ in range(half_times.bit_length() - 1):
                        forward_half = forward_half * forward_half
                        backward_half = backward_half * backward_half
                    ahead = entered_at(z * lanes + lane, 0)
                    ahead = jnp.where(core == 1, forward_half * ahead, ahead)
                    behind = entered_at(z * lanes + lane, 1)
                    behind = jnp.where(core == 1, behind, backward_half * behind)
                    behinds = []
                    for _ in range(half_times):
                        behind = backward * behind
                        behinds.append(behind)
                    for j in range(half_times):
                        ahead = forward * ahead
                        behind = behinds[half_times - 1 - j]
                        both_out[0, j, there, here] = gain * (value_at(0, j, tiles[z], here) + (ahead + cross * behind))
                        both_out[1, j, there, here] = gain * (value_at(1, j, tiles[z], here) + (behind - cross * ahead))
            return 0

        lax.fori_loop(0, lanes // 4, finish_columns, 0)

    def drain(ref, semaphore):
        pltpu.make_async_copy(ref, ref, semaphore).wait()

    for group in range(groups):
        for kind in range(classes):
            await_entry(groups + group, kind)
        twin_entry_copy(group).start()
        finish(
            group,
            core * 16,
            lambda block, index: entry_in[groups + group, block, index],
            lambda there, here: solve[1, there, here],
            lambda there, here: solve[4, there, here],
            lambda there, here: solve[3, there, here],
            lambda field, j, there, here: result[field, core * half_times + j, there, here],
        )
    drain(twin, twin_recv)
    drain(given, give_recv)
    for group in range(groups):
        drain(twin_entry.at[group], twin_entry_recv.at[group])
        finish(
            group,
            16 - core * 16,
            lambda block, index: twin_entry[group, block, index],
            lambda there, here: twin[0, there, here],
            lambda there, here: twin[1, there, here],
            lambda there, here: twin[2, there, here],
            lambda field, j, there, here: given[field, j, there, here],
        )

    base_copy.wait_send()

    @pl.when(core == 1)
    def _():
        drain(rim.at[pl.ds(0, 2)], kappa_send)

    drain(rhs.at[:, own_times], rhs_send)
    drain(carry_out, carry_send)
    drain(entry_out, entry_send)
    drain(edge_out, edge_send)
    drain(pack_out, pack_send)
    drain(result.at[:, own_times], give_send)
    drain(twin, twin_send)
    drain(twin_entry, twin_entry_send)


def write_kernel(both, state_out, adjoint_out, semaphore):
    copies = [
        pltpu.make_async_copy(both.at[field], target, semaphore.at[field])
        for field, target in enumerate((state_out, adjoint_out))
    ]
    for copy in copies:
        copy.start()
    for copy in copies:
        copy.wait()


def solution(mesh):
    ranks = mesh.shape["tm"]
    slabs = mesh.shape["gz"]
    chips = ranks // 2

    def body(state_rhs, adjoint_rhs, diffusivity, velocity):
        steps, depth, cells = state_rhs.shape
        times = 2 * steps
        columns = cells // COL
        groups = 2 * columns // chips
        f32 = jnp.float32
        dma = pltpu.SemaphoreType.DMA
        anywhere = pl.BlockSpec(memory_space=pl.ANY)
        exchanged = pltpu.VMEM((2 * groups, chips, 2, 8, COL), f32)
        call = pl.pallas_call(
            functools.partial(kernel, chips, slabs, cells, times),
            out_shape=pltpu.VMEM((2, steps, depth, cells), f32),
            in_specs=[anywhere] * 4,
            out_specs=pl.BlockSpec(memory_space=pltpu.VMEM),
            scratch_shapes=[
                pltpu.VMEM((2, times, 16, cells), f32),
                pltpu.VMEM((2, times, 16, cells), f32),
                pltpu.VMEM((2, times, 16, cells + 2 * COL), f32),
                pltpu.VMEM((2, times, 16, cells), f32),
                pltpu.VMEM((32, cells), f32),
                pltpu.VMEM((8, cells), f32),
                pltpu.VMEM((3, 8, cells // 8), f32),
                pltpu.VMEM((3, 16, cells), f32),
                pltpu.VMEM((2, 3, 2, 16, cells), f32),
                pltpu.VMEM((6, 16, cells), f32),
                pltpu.VMEM((groups, chips, 2, 8, COL), f32),
                pltpu.VMEM((groups, 2, 8, COL), f32),
                pltpu.VMEM((groups, chips + 1, 2, 8, COL), f32),
                exchanged,
                exchanged,
                exchanged,
                exchanged,
                pltpu.VMEM((2, 3 * times, cells), f32),
                pltpu.VMEM((2, 3 * times, cells), f32),
                pltpu.VMEM((6, 4, 16, cells), f32),
                pltpu.VMEM((2, 32, cells), f32),
                pltpu.VMEM((2, 2, columns, COL), f32),
                pltpu.VMEM((2, 2, columns, COL), f32),
                pltpu.VMEM((3, 16, cells), f32),
                pltpu.VMEM((2, steps, 16, cells), f32),
                pltpu.VMEM((groups, chips, 2, 8, COL), f32),
                dma((3,)),
                dma,
                dma((groups,)),
                dma,
                dma,
                dma((2,)),
                dma,
                dma((2 * groups,)),
                dma,
                dma((2 * groups, 2)),
                dma,
                dma((2 * groups,)),
                dma,
                dma((2,)),
                dma,
                dma,
                dma,
                dma((groups,)),
                dma,
                dma,
            ],
            compiler_params=pltpu.CompilerParams(
                collective_id=0, has_side_effects=True, vmem_limit_bytes=48 * 1024 * 1024
            ),
            cost_estimate=pl.CostEstimate(
                flops=60 * state_rhs.size, bytes_accessed=20 * state_rhs.size, transcendentals=0
            ),
        )
        held = [
            pltpu.with_memory_space_constraint(array, pltpu.HBM)
            for array in (state_rhs, adjoint_rhs, diffusivity, velocity)
        ]
        both = call(*held)
        write = pl.pallas_call(
            write_kernel,
            out_shape=[jax.ShapeDtypeStruct(state_rhs.shape, f32)] * 2,
            in_specs=[pl.BlockSpec(memory_space=pltpu.VMEM)],
            out_specs=[anywhere] * 2,
            scratch_shapes=[dma((2,))],
            compiler_params=pltpu.CompilerParams(vmem_limit_bytes=48 * 1024 * 1024),
        )
        return tuple(write(pltpu.with_memory_space_constraint(both, pltpu.VMEM)))

    placed = (P("tm", "gz", None), P("tm", "gz", None), P("gz", None), P(None, "gz", None))
    return jax.shard_map(
        body,
        mesh=mesh,
        in_specs=placed,
        out_specs=(P("tm", "gz", None), P("tm", "gz", None)),
        check_vma=False,
    )
```
